512 devices in a mesh: leaf: 16 (over y, core), front: 32 (over z, x).
Axes of the slice: x: 4, y: 8, z: 8, core: 2. Of those that a mesh axis runs over, the one named last changes fastest.
Arguments:
- right_side: float32 [64, 65536], P(None, ('leaf', 'front')), may hold values from -3 to 3
- inverse_blocks: float32 [65536, 4096], P(('leaf', 'front')), as said below
- panels: float32 [4096, 4096], P('leaf', 'front'), may hold values from -0.3125 to 0.3125
- receive_rows: int32 [16, 256], P('leaf'), may hold values from 0 to 4095, as said below
- below_update: float32 [64, 256], replicated, may hold values from -6 to 6
- above_solution: float32 [64, 256], replicated, may hold values from -6 to 6
Outputs:
- solution: float32 [64, 65536], P(None, ('leaf', 'front'))
- sent_updates: float32 [64, 4096], P(None, ('leaf', 'front'))
The draws below stay inside these ranges and needn't reach their ends.
Inputs may be any that keep to these rules, and one draw needn't show every extreme that they name: `receive_rows`: each row holds 256 distinct columns in increasing order, the first 0 and the last 4095. `inverse_blocks`: each 4096 x 4096 block is lower triangular with a positive diagonal.
All inputs are finite; a program needn't handle non-finite values.
Results may differ from the reference program's by a relative error of at most 0.00019.
Values sent between devices are 32-bit elements; how exact they have to be, the bound alone decides.
No kernel may reach another device: no remote copies, remote signals or barrier semaphores. Data moves between devices by JAX's collectives and lax.ppermute only.
A program may use at most 64 MiB of HBM per device.

```python
import math
import jax
import jax.numpy as jnp
from jax import lax

W = 4096
K = 256
R = 64
COLUMNS = 65536
PANEL_TOTAL = 4096
N_LEAF = 16


def draw_inverse_blocks(key, part):
    key = jax.random.fold_in(key, 11)
    noise_key, diag_key = jax.random.split(key)
    shape_full = (N_LEAF * W, W)
    row_pos = lax.broadcasted_iota(jnp.int32, shape_full, 0) % W
    col_pos = lax.broadcasted_iota(jnp.int32, shape_full, 1)
    noise_part = jnp.clip(jax.random.normal(noise_key, shape_full, jnp.float32), -3.0, 3.0)
    diag_part = jax.random.uniform(diag_key, shape_full, jnp.float32, 0.6, 1.4)
    lower_part = jnp.where(col_pos < row_pos, noise_part * (0.8 / math.sqrt(W)), 0.0)
    return (lower_part + jnp.where(col_pos == row_pos, diag_part, 0.0)).astype(jnp.float32)


def draw_receive_rows(key, part):
    key = jax.random.fold_in(key, 23)
    section_keys = jax.random.split(key, N_LEAF)

    def draw_row(row_key):
        inner_rows = jax.random.permutation(row_key, W - 2)[:K - 2] + 1
        edges = jnp.array([0, W - 1], dtype=jnp.int32)
        return jnp.sort(jnp.concatenate([edges, inner_rows.astype(jnp.int32)]))
    return jax.vmap(draw_row)(section_keys).astype(jnp.int32)


def level_of(rng, extent, pieces, smallest, largest):
    loudness = 1.0
    for position, shards_of in pieces:
        heights = jax.random.uniform(jax.random.fold_in(jax.random.fold_in(rng, 6), position), (shards_of,), jnp.float32, smallest / len(pieces), largest / len(pieces))
        loudness = loudness * jnp.repeat(jnp.exp(heights), extent[position] // shards_of).reshape((-1,) + (1,) * (len(extent) - 1 - position))
    return loudness


def normal_values(rng, dims, spread, limit, pieces=(), kind=jnp.bfloat16):
    drawn = spread * jax.random.normal(rng, dims, jnp.float32)
    if pieces:
        drawn = drawn * level_of(rng, dims, pieces, -0.22, 0.18)
    return jnp.clip(drawn, -limit, limit).astype(kind)


def setup_inputs(seed: int = 0) -> dict:
    key_of = jax.random.split(jax.random.key(seed), 7)
    return {
        "right_side": normal_values(key_of[0], (R, COLUMNS), 0.5, 3.0, ((1, 512),), jnp.float32),
        "inverse_blocks": draw_inverse_blocks(jax.random.fold_in(key_of[6], 71), 0),
        "panels": normal_values(key_of[2], (PANEL_TOTAL, W), (K * 5 // 3) ** -0.5, 0.3125, ((0, 16), (1, 32)), jnp.float32),
        "receive_rows": draw_receive_rows(jax.random.fold_in(key_of[6], 71), 0),
        "below_update": normal_values(key_of[4], (R, K), 1.0, 6.0, (), jnp.float32),
        "above_solution": normal_values(key_of[5], (R, K), 1.0, 6.0, (), jnp.float32),
    }


def reference(right_side, inverse_blocks, panels, receive_rows, below_update, above_solution):
    highest = lax.Precision.HIGHEST
    incoming = below_update
    forward_list = []
    update_list = []
    for section in range(N_LEAF):
        rhs_block = right_side[:, section * W:(section + 1) * W]
        targets = receive_rows[section].astype(jnp.int32)
        residual = rhs_block.at[:, targets].add(-incoming)
        inverse = inverse_blocks[section * W:(section + 1) * W]
        forward = jnp.dot(residual, inverse.T, precision=highest, preferred_element_type=jnp.float32)
        panel_rows = panels[section * K:(section + 1) * K]
        incoming = jnp.dot(forward, panel_rows.T, precision=highest, preferred_element_type=jnp.float32)
        forward_list.append(forward)
        update_list.append(incoming)
    from_above = above_solution
    solution_list = [None] * N_LEAF
    for section in range(N_LEAF - 1, -1, -1):
        inverse = inverse_blocks[section * W:(section + 1) * W]
        panel_rows = panels[section * K:(section + 1) * K]
        reduced = forward_list[section] - jnp.dot(from_above, panel_rows, precision=highest, preferred_element_type=jnp.float32)
        solved = jnp.dot(reduced, inverse, precision=highest, preferred_element_type=jnp.float32)
        solution_list[section] = solved
        from_above = solved[:, receive_rows[section].astype(jnp.int32)]
    return jnp.concatenate(solution_list, axis=1), jnp.concatenate(update_list, axis=1)
```

```python
import jax
import jax.numpy as jnp
from jax import lax
from jax.sharding import PartitionSpec as P

exact = lax.Precision.HIGHEST


def product(left, right):
    return jnp.dot(left, right, precision=exact, preferred_element_type=jnp.float32)


def product_nt(left, right):
    return lax.dot_general(
        left, right, (((1,), (1,)), ((), ())), precision=exact, preferred_element_type=jnp.float32
    )


def exchange(blocks):
    return lax.all_to_all(blocks, "front", 0, 0, tiled=True)


def gather_front(block):
    count = lax.axis_size("front")
    return exchange(jnp.broadcast_to(block[None], (count, *block.shape)))


def scatter_front(total):
    count = lax.axis_size("front")
    pieces = total.reshape(count, total.shape[0] // count, *total.shape[1:])
    return jnp.sum(exchange(pieces), axis=0)


def on_device(right_side, inverse_blocks, panels, receive_rows, below_update, above_solution):
    rhs = right_side.shape[0]
    block = inverse_blocks.shape[0]
    rows = panels.shape[0]
    leaf_count = lax.axis_size("leaf")
    front_count = lax.axis_size("front")
    front_pos = lax.axis_index("front")
    leaf_pos = lax.axis_index("leaf")
    share = rhs // front_count
    targets = receive_rows[0]
    is_upper = leaf_pos % 2 == 1

    section_side = gather_front(right_side)
    picked = jnp.take(inverse_blocks, targets, axis=1)
    stacked = jnp.concatenate([panels, picked.T], axis=0)
    coupling = scatter_front(product(stacked, picked))
    coupling = gather_front(coupling).reshape(2 * rows, rows)

    section_side = section_side.transpose(1, 0, 2).reshape(rhs, front_count * block)
    local_forward = product_nt(section_side, inverse_blocks)
    vectors = scatter_front(product_nt(local_forward, stacked))

    swap = [(s, s ^ 1) for s in range(leaf_count)]
    up = [(s, (s + 2) % leaf_count) for s in range(leaf_count)]
    down = [(target, source) for source, target in up]
    mate_coupling = lax.ppermute(coupling, "leaf", swap)
    mate_vectors = lax.ppermute(vectors, "leaf", swap)
    low = jnp.where(is_upper, mate_coupling, coupling)
    high = jnp.where(is_upper, coupling, mate_coupling)
    low_vec = jnp.where(is_upper, mate_vectors, vectors)
    high_vec = jnp.where(is_upper, vectors, mate_vectors)
    d_low, g_low = (-low[:rows], low[rows:])
    d_high, g_high = (-high[:rows], high[rows:])
    u_low, w_low = (low_vec[:, :rows], low_vec[:, rows:])
    u_high, w_high = (high_vec[:, :rows], high_vec[:, rows:])
    d_pair = product(d_high, d_low)
    g_pair = g_low + product(d_low.T, product(g_high, d_low))
    u_pair = u_high + product_nt(u_low, d_high)
    w_pair = w_low + product(w_high - product(u_low, g_high), d_low)

    below_rows = lax.dynamic_slice_in_dim(below_update, front_pos * share, share, 0)
    above_rows = lax.dynamic_slice_in_dim(above_solution, front_pos * share, share, 0)
    incoming = below_rows
    for _ in range(leaf_count // 2 - 1):
        sent = lax.ppermute(u_pair + product_nt(incoming, d_pair), "leaf", up)
        incoming = jnp.where(leaf_pos < 2, below_rows, sent)
    w_full = w_pair - product(incoming, g_pair)
    from_above = above_rows
    for _ in range(leaf_count // 2 - 1):
        sent = lax.ppermute(w_full + product(from_above, d_pair), "leaf", down)
        from_above = jnp.where(leaf_pos >= leaf_count - 2, above_rows, sent)

    middle = u_low + product_nt(incoming, d_low)
    own_incoming = jnp.where(is_upper, middle, incoming)
    upper_update = u_high + product_nt(middle, d_high)
    own_update = jnp.where(is_upper, upper_update, middle)
    middle_above = w_high - product(middle, g_high) + product(from_above, d_high)
    own_above = jnp.where(is_upper, from_above, middle_above)

    result = gather_front(jnp.concatenate([own_above, own_incoming, own_update], axis=1))
    result = result.reshape(rhs, 3 * rows)
    update_share = rows // front_count
    sent_updates = lax.dynamic_slice_in_dim(
        result, 2 * rows + front_pos * update_share, update_share, 1
    )
    reduced = local_forward - product(result[:, : 2 * rows], stacked)
    spread = product(reduced, inverse_blocks)
    spread = spread.reshape(rhs, front_count, block).transpose(1, 0, 2)
    solution = jnp.sum(exchange(spread), axis=0)
    return (solution, sent_updates)


def solution(mesh):
    in_specs = (
        P(None, ("leaf", "front")),
        P(("leaf", "front"), None),
        P("leaf", "front"),
        P("leaf", None),
        P(),
        P(),
    )
    out_specs = (P(None, ("leaf", "front")), P(None, ("leaf", "front")))
    return jax.shard_map(
        on_device, mesh=mesh, in_specs=in_specs, out_specs=out_specs, check_vma=False
    )
```

```python
import jax
import jax.numpy as jnp
from jax import lax
from jax.sharding import PartitionSpec as P

exact = lax.Precision.HIGHEST


def product(left, right):
    return jnp.dot(left, right, precision=exact, preferred_element_type=jnp.float32)


def product_nt(left, right):
    return lax.dot_general(
        left, right, (((1,), (1,)), ((), ())), precision=exact, preferred_element_type=jnp.float32
    )


def exchange(blocks):
    return lax.all_to_all(blocks, "front", 0, 0, tiled=True)


def gather_front(block):
    count = lax.axis_size("front")
    return exchange(jnp.broadcast_to(block[None], (count, *block.shape)))


def gather_line(block):
    count = lax.axis_size("leaf")
    lines = [list(range(core, count, 2)) for core in range(2)]
    copies = jnp.broadcast_to(block[None], (count // 2, *block.shape))
    return lax.all_to_all(copies, "leaf", 0, 0, tiled=True, axis_index_groups=lines)


def scatter_front(total):
    count = lax.axis_size("front")
    pieces = total.reshape(count, total.shape[0] // count, *total.shape[1:])
    return jnp.sum(exchange(pieces), axis=0)


def on_device(right_side, inverse_blocks, panels, receive_rows, below_update, above_solution):
    rhs = right_side.shape[0]
    block = inverse_blocks.shape[0]
    rows = panels.shape[0]
    leaf_count = lax.axis_size("leaf")
    front_count = lax.axis_size("front")
    front_pos = lax.axis_index("front")
    leaf_pos = lax.axis_index("leaf")
    share = rhs // front_count
    targets = receive_rows[0]
    is_upper = leaf_pos % 2 == 1

    section_side = gather_front(right_side)
    picked = jnp.take(inverse_blocks, targets, axis=1)
    stacked = jnp.concatenate([panels, picked.T], axis=0)
    coupling = scatter_front(product(stacked, picked))
    coupling = gather_front(coupling).reshape(2 * rows, rows)

    section_side = section_side.transpose(1, 0, 2).reshape(rhs, front_count * block)
    local_forward = product_nt(section_side, inverse_blocks)
    vectors = scatter_front(product_nt(local_forward, stacked))

    swap = [(s, s ^ 1) for s in range(leaf_count)]
    mate_coupling = lax.ppermute(coupling, "leaf", swap)
    mate_vectors = lax.ppermute(vectors, "leaf", swap)
    low = jnp.where(is_upper, mate_coupling, coupling)
    high = jnp.where(is_upper, coupling, mate_coupling)
    low_vec = jnp.where(is_upper, mate_vectors, vectors)
    high_vec = jnp.where(is_upper, vectors, mate_vectors)
    d_low, g_low = (-low[:rows], low[rows:])
    d_high, g_high = (-high[:rows], high[rows:])
    u_low, w_low = (low_vec[:, :rows], low_vec[:, rows:])
    u_high, w_high = (high_vec[:, :rows], high_vec[:, rows:])
    d_pair = product(d_high, d_low)
    g_pair = g_low + product(d_low.T, product(g_high, d_low))
    u_pair = u_high + product_nt(u_low, d_high)
    w_pair = w_low + product(w_high - product(u_low, g_high), d_low)

    below_rows = lax.dynamic_slice_in_dim(below_update, front_pos * share, share, 0)
    above_rows = lax.dynamic_slice_in_dim(above_solution, front_pos * share, share, 0)
    pairs = leaf_count // 2
    chip = leaf_pos // 2
    own_half = gather_line(jnp.where(is_upper, g_pair, d_pair))
    mate_half = lax.ppermute(own_half, "leaf", swap)
    d_all = jnp.where(is_upper, mate_half, own_half)
    g_all = jnp.where(is_upper, own_half, mate_half)
    vec_all = gather_line(jnp.concatenate([u_pair, w_pair], axis=1))
    into = [below_rows]
    for y in range(pairs - 1):
        into.append(vec_all[y, :, :rows] + product_nt(into[-1], d_all[y]))
    above = [above_rows]
    for y in range(pairs - 1, 0, -1):
        w_row = vec_all[y, :, rows:] - product(into[y], g_all[y])
        above.append(w_row + product(above[-1], d_all[y]))
    incoming = jnp.take(jnp.stack(into), chip, axis=0)
    from_above = jnp.take(jnp.stack(above[::-1]), chip, axis=0)

    middle = u_low + product_nt(incoming, d_low)
    own_incoming = jnp.where(is_upper, middle, incoming)
    upper_update = u_high + product_nt(middle, d_high)
    own_update = jnp.where(is_upper, upper_update, middle)
    middle_above = w_high - product(middle, g_high) + product(from_above, d_high)
    own_above = jnp.where(is_upper, from_above, middle_above)

    result = gather_front(jnp.concatenate([own_above, own_incoming, own_update], axis=1))
    result = result.reshape(rhs, 3 * rows)
    update_share = rows // front_count
    sent_updates = lax.dynamic_slice_in_dim(
        result, 2 * rows + front_pos * update_share, update_share, 1
    )
    reduced = local_forward - product(result[:, : 2 * rows], stacked)
    spread = product(reduced, inverse_blocks)
    spread = spread.reshape(rhs, front_count, block).transpose(1, 0, 2)
    solution = jnp.sum(exchange(spread), axis=0)
    return (solution, sent_updates)


def solution(mesh):
    in_specs = (
        P(None, ("leaf", "front")),
        P(("leaf", "front"), None),
        P("leaf", "front"),
        P("leaf", None),
        P(),
        P(),
    )
    out_specs = (P(None, ("leaf", "front")), P(None, ("leaf", "front")))
    return jax.shard_map(
        on_device, mesh=mesh, in_specs=in_specs, out_specs=out_specs, check_vma=False
    )
```

```python
import jax
import jax.numpy as jnp
from jax import lax
from jax.experimental import pallas as pl
from jax.experimental.pallas import tpu as pltpu
from jax.sharding import PartitionSpec as P

exact = lax.Precision.HIGHEST
x_chips = 4
padded = 8


def product(left, right):
    return jnp.dot(left, right, precision=exact, preferred_element_type=jnp.float32)


def product_nt(left, right):
    return lax.dot_general(
        left, right, (((1,), (1,)), ((), ())), precision=exact, preferred_element_type=jnp.float32
    )


def exchange(blocks, axis="front", groups=None):
    return lax.all_to_all(blocks, axis, 0, 0, tiled=True, axis_index_groups=groups)


def copies(block, count):
    return jnp.broadcast_to(block[None], (count, *block.shape))


def gather_front(block):
    return exchange(copies(block, lax.axis_size("front")))


def scatter_front(total):
    count = lax.axis_size("front")
    pieces = total.reshape(count, total.shape[0] // count, *total.shape[1:])
    return jnp.sum(exchange(pieces), axis=0)


def gather_leaf(block):
    return lax.all_gather(block, "leaf", axis=0)


def gather_leaf_small(block):
    return exchange(copies(block, lax.axis_size("leaf")), "leaf")


def gather_along_z(block):
    count = lax.axis_size("front")
    groups = [list(range(x, count, x_chips)) for x in range(x_chips)]
    wide = jnp.concatenate([block, jnp.zeros((3 * block.shape[0], block.shape[1]), block.dtype)])
    wide = lax.all_gather(wide, "front", axis=0, axis_index_groups=groups)
    return wide[:, : block.shape[0]]


def gather_along_x(planes):
    count = lax.axis_size("front")
    groups = [list(range(first, first + x_chips)) for first in range(0, count, x_chips)]
    whole = exchange(copies(planes, x_chips), "front", groups)
    return whole.transpose(1, 0, 2, 3).reshape(count, *planes.shape[1:])


def split(value):
    head = value.astype(jnp.bfloat16)
    return head, (value - head.astype(jnp.float32)).astype(jnp.bfloat16)


def two_parts(value):
    head, tail = split(value)
    return jnp.concatenate([head.astype(jnp.float32), tail.astype(jnp.float32)]).astype(
        jnp.bfloat16
    )


def dot_parts(parts, head, tail, contract):
    dims = (((1,), (contract,)), ((), ()))
    both = lax.dot_general(parts, head, dims, preferred_element_type=jnp.float32)
    both += lax.dot_general(parts, tail, dims, preferred_element_type=jnp.float32)
    return both[:padded] + both[padded:]


def chain_kernel(
    pos_ref, coupling_ref, vector_ref, below_ref, above_ref, out_ref,
    held, head, tail, vectors, into, above, sems,
):
    sections, share, _ = vector_ref.shape
    rows = below_ref.shape[1]

    def fetch(s):
        return pltpu.make_async_copy(coupling_ref.at[s], held.at[s], sems.at[s])

    for s in range(sections):
        fetch(s).start()
    vectors[...] = jnp.zeros_like(vectors)
    into[0] = jnp.zeros_like(into[0])
    above[sections - 1] = jnp.zeros_like(into[0])
    for s in range(sections):
        vectors[s, :share, :] = vector_ref[s]
    into[0, :share, :] = below_ref[...]
    above[sections - 1, :share, :] = above_ref[...]

    incoming = into[0]
    for s in range(sections):
        fetch(s).wait()
        block_head, block_tail = split(held[s])
        head[s] = block_head[:rows]
        tail[s] = block_tail[:rows]
        result = vectors[s] - dot_parts(two_parts(incoming), block_head, block_tail, 1)
        incoming = result[:, :rows]
        into[s + 1] = incoming
        vectors[s] = result
    from_above = above[sections - 1]
    for s in range(sections - 1, 0, -1):
        taken = dot_parts(two_parts(from_above), head[s], tail[s], 0)
        from_above = vectors[s, :, rows:] - taken
        above[s - 1] = from_above

    own = pos_ref[0]
    kept = jnp.concatenate([above[own], into[own], into[own + 1]], axis=1)[:share]
    for piece in range(out_ref.shape[0]):
        out_ref[piece] = kept


def run_chain(position, coupling_all, vector_all, below_rows, above_rows, targets):
    sections, share, _ = vector_all.shape
    rows = below_rows.shape[1]
    vmem = pl.BlockSpec(memory_space=pltpu.VMEM)
    return pl.pallas_call(
        chain_kernel,
        out_shape=jax.ShapeDtypeStruct((targets, share, 3 * rows), jnp.float32),
        in_specs=[
            pl.BlockSpec(memory_space=pltpu.SMEM),
            pl.BlockSpec(memory_space=pl.ANY),
            vmem,
            vmem,
            vmem,
        ],
        out_specs=vmem,
        scratch_shapes=[
            pltpu.VMEM((sections, 2 * rows, rows), jnp.float32),
            pltpu.VMEM((sections, rows, rows), jnp.bfloat16),
            pltpu.VMEM((sections, rows, rows), jnp.bfloat16),
            pltpu.VMEM((sections, padded, 2 * rows), jnp.float32),
            pltpu.VMEM((sections + 1, padded, rows), jnp.float32),
            pltpu.VMEM((sections, padded, rows), jnp.float32),
            pltpu.SemaphoreType.DMA((sections,)),
        ],
        compiler_params=pltpu.CompilerParams(vmem_limit_bytes=32 * 1024 * 1024),
        cost_estimate=pl.CostEstimate(
            flops=12 * sections * 16 * rows * rows,
            bytes_accessed=8 * sections * rows * rows,
            transcendentals=0,
        ),
        name="chain",
    )(position.reshape(1), coupling_all, vector_all, below_rows, above_rows)


def on_device(right_side, inverse_blocks, panels, receive_rows, below_update, above_solution):
    rhs = right_side.shape[0]
    block = inverse_blocks.shape[0]
    rows = panels.shape[0]
    front_count = lax.axis_size("front")
    front_pos = lax.axis_index("front")
    leaf_pos = lax.axis_index("leaf")
    share = rhs // front_count
    targets = receive_rows[0]

    planes = gather_along_z(right_side)
    picked = jnp.take(inverse_blocks, targets, axis=1)
    stacked = jnp.concatenate([panels, picked.T], axis=0)
    coupling = scatter_front(product(stacked, picked))
    coupling = gather_front(coupling).reshape(2 * rows, rows)
    coupling, planes = lax.optimization_barrier((coupling, planes))
    coupling_all = gather_leaf(coupling)

    section_side = gather_along_x(planes).transpose(1, 0, 2).reshape(rhs, front_count * block)
    local_forward = product_nt(section_side, inverse_blocks)
    vectors = scatter_front(product_nt(local_forward, stacked))
    vector_all = gather_leaf_small(vectors)

    below_rows = lax.dynamic_slice_in_dim(below_update, front_pos * share, share, 0)
    above_rows = lax.dynamic_slice_in_dim(above_solution, front_pos * share, share, 0)
    result = exchange(
        run_chain(leaf_pos, coupling_all, vector_all, below_rows, above_rows, front_count)
    )
    result = result.reshape(rhs, 3 * rows)
    update_share = rows // front_count
    sent_updates = lax.dynamic_slice_in_dim(
        result, 2 * rows + front_pos * update_share, update_share, 1
    )
    reduced = local_forward - product(result[:, : 2 * rows], stacked)
    spread = product(reduced, inverse_blocks)
    spread = spread.reshape(rhs, front_count, block).transpose(1, 0, 2)
    solution = jnp.sum(exchange(spread), axis=0)
    return (solution, sent_updates)


def solution(mesh):
    in_specs = (
        P(None, ("leaf", "front")),
        P(("leaf", "front"), None),
        P("leaf", "front"),
        P("leaf", None),
        P(),
        P(),
    )
    out_specs = (P(None, ("leaf", "front")), P(None, ("leaf", "front")))
    return jax.shard_map(
        on_device, mesh=mesh, in_specs=in_specs, out_specs=out_specs, check_vma=False
    )
```

```python
import jax
import jax.numpy as jnp
from jax import lax
from jax.experimental import pallas as pl
from jax.experimental.pallas import tpu as pltpu
from jax.sharding import PartitionSpec as P

exact = lax.Precision.HIGHEST
x_chips = 4
padded = 8


def product(left, right):
    return jnp.dot(left, right, precision=exact, preferred_element_type=jnp.float32)


def product_nt(left, right):
    return lax.dot_general(
        left, right, (((1,), (1,)), ((), ())), precision=exact, preferred_element_type=jnp.float32
    )


def exchange(blocks, axis="front", groups=None):
    return lax.all_to_all(blocks, axis, 0, 0, tiled=True, axis_index_groups=groups)


def copies(block, count):
    return jnp.broadcast_to(block[None], (count, *block.shape))


def gather_front(block):
    return exchange(copies(block, lax.axis_size("front")))


def scatter_front(total):
    count = lax.axis_size("front")
    pieces = total.reshape(count, total.shape[0] // count, *total.shape[1:])
    return jnp.sum(exchange(pieces), axis=0)


def gather_leaf(block):
    return lax.all_gather(block, "leaf", axis=0)


def gather_leaf_small(block):
    return exchange(copies(block, lax.axis_size("leaf")), "leaf")


def pad_side(block):
    return jnp.concatenate([block, jnp.zeros((3 * block.shape[0], block.shape[1]), block.dtype)])


def gather_along_z(wide, rhs):
    count = lax.axis_size("front")
    groups = [list(range(x, count, x_chips)) for x in range(x_chips)]
    return lax.all_gather(wide, "front", axis=0, axis_index_groups=groups)[:, :rhs]


def gather_along_x(planes):
    count = lax.axis_size("front")
    groups = [list(range(first, first + x_chips)) for first in range(0, count, x_chips)]
    whole = exchange(copies(planes, x_chips), "front", groups)
    return whole.transpose(1, 0, 2, 3).reshape(count, *planes.shape[1:])


def split(value):
    head = value.astype(jnp.bfloat16)
    return head, (value - head.astype(jnp.float32)).astype(jnp.bfloat16)


def two_parts(value):
    head, tail = split(value)
    return jnp.concatenate([head.astype(jnp.float32), tail.astype(jnp.float32)]).astype(
        jnp.bfloat16
    )


def dot_parts(parts, head, tail, contract):
    dims = (((1,), (contract,)), ((), ()))
    both = lax.dot_general(parts, head, dims, preferred_element_type=jnp.float32)
    both += lax.dot_general(parts, tail, dims, preferred_element_type=jnp.float32)
    return both[:padded] + both[padded:]


def chain_kernel(
    pos_ref, coupling_ref, share_ref, low_ref, high_ref, low_vec_ref, high_vec_ref,
    below_ref, above_ref, out_ref, held, head, tail, vectors, into, above, sems,
):
    pairs = held.shape[0]
    share, rows = below_ref.shape

    def fetch(y):
        return pltpu.make_async_copy(coupling_ref.at[y], held.at[y], sems.at[y])

    for y in range(pairs):
        fetch(y).start()
    vectors[...] = jnp.zeros_like(vectors)
    into[0] = jnp.zeros_like(into[0])
    above[pairs - 1] = jnp.zeros_like(into[0])
    for y in range(pairs):
        vectors[y, :share, :] = share_ref[2 * y] + share_ref[2 * y + 1]
    vectors[pairs, :share, :] = low_vec_ref[...]
    vectors[pairs + 1, :share, :] = high_vec_ref[...]
    into[0, :share, :] = below_ref[...]
    above[pairs - 1, :share, :] = above_ref[...]

    low_head, low_tail = split(low_ref[:rows])
    high_head, high_tail = split(high_ref[...])
    incoming = into[0]
    for y in range(pairs):
        fetch(y).wait()
        block_head, block_tail = split(held[y])
        head[y] = block_head[:rows]
        tail[y] = block_tail[:rows]
        result = vectors[y] - dot_parts(two_parts(incoming), block_head, block_tail, 1)
        incoming = result[:, :rows]
        if y + 1 < pairs:
            into[y + 1] = incoming
        vectors[y] = result
    from_above = above[pairs - 1]
    for y in range(pairs - 1, 0, -1):
        taken = dot_parts(two_parts(from_above), head[y], tail[y], 0)
        from_above = vectors[y, :, rows:] - taken
        above[y - 1] = from_above

    chip = pos_ref[0]
    incoming = into[chip]
    from_above = above[chip]
    middle = vectors[pairs, :, :rows] - dot_parts(two_parts(incoming), low_head, low_tail, 1)
    upper = vectors[pairs + 1] - dot_parts(two_parts(middle), high_head, high_tail, 1)
    taken = dot_parts(two_parts(from_above), high_head[:rows], high_tail[:rows], 0)
    middle_above = upper[:, rows:] - taken
    is_upper = pos_ref[1] == 1
    kept = jnp.concatenate(
        [
            jnp.where(is_upper, from_above, middle_above),
            jnp.where(is_upper, middle, incoming),
            jnp.where(is_upper, upper[:, :rows], middle),
        ],
        axis=1,
    )[:share]
    for piece in range(out_ref.shape[0]):
        out_ref[piece] = kept


def run_chain(position, coupling_all, shares, low, high, low_vec, high_vec, below, above, targets):
    share, rows = below.shape
    pairs = coupling_all.shape[0]
    vmem = pl.BlockSpec(memory_space=pltpu.VMEM)
    return pl.pallas_call(
        chain_kernel,
        out_shape=jax.ShapeDtypeStruct((targets, share, 3 * rows), jnp.float32),
        in_specs=[pl.BlockSpec(memory_space=pltpu.SMEM), pl.BlockSpec(memory_space=pl.ANY)]
        + [vmem] * 7,
        out_specs=vmem,
        scratch_shapes=[
            pltpu.VMEM((pairs, 2 * rows, rows), jnp.float32),
            pltpu.VMEM((pairs, rows, rows), jnp.bfloat16),
            pltpu.VMEM((pairs, rows, rows), jnp.bfloat16),
            pltpu.VMEM((pairs + 2, padded, 2 * rows), jnp.float32),
            pltpu.VMEM((pairs, padded, rows), jnp.float32),
            pltpu.VMEM((pairs, padded, rows), jnp.float32),
            pltpu.SemaphoreType.DMA((pairs,)),
        ],
        compiler_params=pltpu.CompilerParams(vmem_limit_bytes=32 * 1024 * 1024),
        cost_estimate=pl.CostEstimate(
            flops=12 * pairs * 16 * rows * rows,
            bytes_accessed=8 * pairs * rows * rows,
            transcendentals=0,
        ),
        name="chain",
    )(position, coupling_all, shares, low, high, low_vec, high_vec, below, above)


def on_device(right_side, inverse_blocks, panels, receive_rows, below_update, above_solution):
    rhs = right_side.shape[0]
    block = inverse_blocks.shape[0]
    rows = panels.shape[0]
    front_count = lax.axis_size("front")
    front_pos = lax.axis_index("front")
    leaf_pos = lax.axis_index("leaf")
    leaf_count = lax.axis_size("leaf")
    is_upper = leaf_pos % 2 == 1
    share = rhs // front_count
    targets = receive_rows[0]

    wide = pad_side(right_side)
    wide, targets = lax.optimization_barrier((wide, targets))
    planes = gather_along_z(wide, rhs)
    picked = jnp.take(inverse_blocks, targets, axis=1)
    stacked = jnp.concatenate([panels, picked.T], axis=0)
    coupling = scatter_front(product(stacked, picked))
    coupling = gather_front(coupling).reshape(2 * rows, rows)

    swap = [(s, s ^ 1) for s in range(leaf_count)]
    mate = lax.ppermute(coupling, "leaf", swap)
    low = jnp.where(is_upper, mate, coupling)
    high = jnp.where(is_upper, coupling, mate)
    c_low, c_high, g_high = (low[:rows], high[:rows], high[rows:])
    lifted = product(g_high, c_low)
    c_pair = -product(c_high, c_low)
    g_pair = low[rows:] + product(c_low.T, lifted)
    pair_half = jnp.where(is_upper, g_pair, c_pair)
    pair_half, planes = lax.optimization_barrier((pair_half, planes))
    coupling_all = gather_leaf(pair_half).reshape(leaf_count // 2, 2 * rows, rows)

    section_side = gather_along_x(planes).transpose(1, 0, 2).reshape(rhs, front_count * block)
    local_forward = product_nt(section_side, inverse_blocks)
    vectors = scatter_front(product_nt(local_forward, stacked))
    mate_vectors = lax.ppermute(vectors, "leaf", swap)
    low_vec = jnp.where(is_upper, mate_vectors, vectors)
    high_vec = jnp.where(is_upper, vectors, mate_vectors)
    u_own, w_own = (vectors[:, :rows], vectors[:, rows:])
    u_moved = -product_nt(u_own, c_high)
    w_moved = product(jnp.where(is_upper, w_own, u_own), jnp.where(is_upper, -c_low, lifted))
    own_share = jnp.concatenate(
        [
            jnp.where(is_upper, u_own, u_moved),
            jnp.where(is_upper, w_moved, w_own + w_moved),
        ],
        axis=1,
    )
    shares = gather_leaf_small(own_share)

    below_rows = lax.dynamic_slice_in_dim(below_update, front_pos * share, share, 0)
    above_rows = lax.dynamic_slice_in_dim(above_solution, front_pos * share, share, 0)
    position = jnp.stack([leaf_pos // 2, leaf_pos % 2])
    result = exchange(
        run_chain(
            position, coupling_all, shares, low, high, low_vec, high_vec,
            below_rows, above_rows, front_count,
        )
    )
    result = result.reshape(rhs, 3 * rows)
    update_share = rows // front_count
    sent_updates = lax.dynamic_slice_in_dim(
        result, 2 * rows + front_pos * update_share, update_share, 1
    )
    reduced = local_forward - product(result[:, : 2 * rows], stacked)
    spread = product(reduced, inverse_blocks)
    spread = spread.reshape(rhs, front_count, block).transpose(1, 0, 2)
    solution = jnp.sum(exchange(spread), axis=0)
    return (solution, sent_updates)


def solution(mesh):
    in_specs = (
        P(None, ("leaf", "front")),
        P(("leaf", "front"), None),
        P("leaf", "front"),
        P("leaf", None),
        P(),
        P(),
    )
    out_specs = (P(None, ("leaf", "front")), P(None, ("leaf", "front")))
    return jax.shard_map(
        on_device, mesh=mesh, in_specs=in_specs, out_specs=out_specs, check_vma=False
    )
```

```python
import functools

import jax
import jax.numpy as jnp
from jax import lax
from jax.experimental import pallas as pl
from jax.experimental.pallas import tpu as pltpu
from jax.sharding import PartitionSpec as P

exact = lax.Precision.HIGHEST
x_chips = 4
padded = 8


def product(left, right):
    return jnp.dot(left, right, precision=exact, preferred_element_type=jnp.float32)


def product_nt(left, right):
    return lax.dot_general(
        left, right, (((1,), (1,)), ((), ())), precision=exact, preferred_element_type=jnp.float32
    )


def exchange(blocks, axis="front", groups=None):
    return lax.all_to_all(blocks, axis, 0, 0, tiled=True, axis_index_groups=groups)


def copies(block, count):
    return jnp.broadcast_to(block[None], (count, *block.shape))


def gather_front(block):
    return exchange(copies(block, lax.axis_size("front")))


def scatter_front(total):
    count = lax.axis_size("front")
    pieces = total.reshape(count, total.shape[0] // count, *total.shape[1:])
    return jnp.sum(exchange(pieces), axis=0)


def gather_leaf(block):
    return lax.all_gather(block, "leaf", axis=0)


def gather_leaf_small(block):
    return exchange(copies(block, lax.axis_size("leaf")), "leaf")


def gather_along_x(block):
    count = lax.axis_size("front")
    groups = [list(range(first, first + x_chips)) for first in range(0, count, x_chips)]
    return lax.all_gather(block, "front", axis=0, axis_index_groups=groups)


def ring_along_z(block):
    count = lax.axis_size("front")
    turns = count // x_chips
    later = [(f, (f + x_chips) % count) for f in range(count)]
    earlier = [(target, source) for source, target in later]
    pieces = [(0, block)]
    behind = ahead = block
    for step in range(1, turns // 2 + 1):
        behind = lax.ppermute(behind, "front", later)
        pieces.append((turns - step, behind))
        if step < turns - step:
            ahead = lax.ppermute(ahead, "front", earlier)
            pieces.append((step, ahead))
    return pieces


def split(value):
    head = value.astype(jnp.bfloat16)
    return head, (value - head.astype(jnp.float32)).astype(jnp.bfloat16)


def two_parts(value):
    head, tail = split(value)
    return jnp.concatenate([head.astype(jnp.float32), tail.astype(jnp.float32)]).astype(
        jnp.bfloat16
    )


def dot_parts(parts, head, tail, contract):
    dims = (((1,), (contract,)), ((), ()))
    both = lax.dot_general(parts, head, dims, preferred_element_type=jnp.float32)
    both += lax.dot_general(parts, tail, dims, preferred_element_type=jnp.float32)
    return both[:padded] + both[padded:]


def forward_kernel(offsets, pos_ref, inverse_ref, stacked_ref, *refs):
    pieces, (forward_ref, vector_ref) = refs[:-2], refs[-2:]
    planes, rhs, block = pieces[0].shape
    width = planes * block
    total = jnp.zeros((2 * rhs, 2 * block), jnp.float32)
    for offset, piece in zip(offsets, pieces):
        place = lax.rem(pos_ref[0] + offset, len(offsets))
        columns = pl.ds(pl.multiple_of(place * width, width), width)
        side = jnp.concatenate([piece[x] for x in range(planes)], axis=1)
        total += lax.dot_general(
            two_parts(side),
            two_parts(inverse_ref[:, columns]),
            (((1,), (1,)), ((), ())),
            preferred_element_type=jnp.float32,
        )
    forward = fold(total, rhs, block)
    forward_ref[...] = forward
    vectors = lax.dot_general(
        two_parts(forward),
        two_parts(stacked_ref[...]),
        (((1,), (1,)), ((), ())),
        preferred_element_type=jnp.float32,
    )
    vectors = fold(vectors, rhs, stacked_ref.shape[0])
    share = vector_ref.shape[1]
    for piece in range(vector_ref.shape[0]):
        vector_ref[piece] = vectors[piece * share : (piece + 1) * share]


def fold(parts, rows, columns):
    small = parts[rows:, columns:] + (parts[rows:, :columns] + parts[:rows, columns:])
    return small + parts[:rows, :columns]


def run_forward(z_pos, pieces, inverse_blocks, stacked, targets):
    offsets = [offset for offset, _ in pieces]
    rhs = pieces[0][1].shape[1]
    block = inverse_blocks.shape[0]
    vmem = pl.BlockSpec(memory_space=pltpu.VMEM)
    return pl.pallas_call(
        functools.partial(forward_kernel, offsets),
        out_shape=(
            jax.ShapeDtypeStruct((rhs, block), jnp.float32),
            jax.ShapeDtypeStruct((targets, rhs // targets, stacked.shape[0]), jnp.float32),
        ),
        in_specs=[pl.BlockSpec(memory_space=pltpu.SMEM)] + [vmem] * (2 + len(pieces)),
        out_specs=(vmem, vmem),
        compiler_params=pltpu.CompilerParams(vmem_limit_bytes=32 * 1024 * 1024),
        cost_estimate=pl.CostEstimate(
            flops=8 * rhs * block * inverse_blocks.shape[1],
            bytes_accessed=4 * inverse_blocks.size + 4 * rhs * inverse_blocks.shape[1],
            transcendentals=0,
        ),
        name="forward",
    )(z_pos.reshape(1), inverse_blocks, stacked, *[piece for _, piece in pieces])


def chain_kernel(
    pos_ref, coupling_ref, share_ref, low_ref, high_ref, low_vec_ref, high_vec_ref,
    below_ref, above_ref, out_ref, held, head, tail, vectors, into, above, sems,
):
    pairs = held.shape[0]
    share, rows = below_ref.shape

    def fetch(y):
        return pltpu.make_async_copy(coupling_ref.at[y], held.at[y], sems.at[y])

    for y in range(pairs):
        fetch(y).start()
    vectors[...] = jnp.zeros_like(vectors)
    into[0] = jnp.zeros_like(into[0])
    above[pairs - 1] = jnp.zeros_like(into[0])
    for y in range(pairs):
        vectors[y, :share, :] = share_ref[2 * y] + share_ref[2 * y + 1]
    vectors[pairs, :share, :] = low_vec_ref[...]
    vectors[pairs + 1, :share, :] = high_vec_ref[...]
    into[0, :share, :] = below_ref[...]
    above[pairs - 1, :share, :] = above_ref[...]

    low_head, low_tail = split(low_ref[:rows])
    high_head, high_tail = split(high_ref[...])
    incoming = into[0]
    for y in range(pairs):
        fetch(y).wait()
        block_head, block_tail = split(held[y])
        head[y] = block_head[:rows]
        tail[y] = block_tail[:rows]
        result = vectors[y] - dot_parts(two_parts(incoming), block_head, block_tail, 1)
        incoming = result[:, :rows]
        if y + 1 < pairs:
            into[y + 1] = incoming
        vectors[y] = result
    from_above = above[pairs - 1]
    for y in range(pairs - 1, 0, -1):
        taken = dot_parts(two_parts(from_above), head[y], tail[y], 0)
        from_above = vectors[y, :, rows:] - taken
        above[y - 1] = from_above

    chip = pos_ref[0]
    incoming = into[chip]
    from_above = above[chip]
    middle = vectors[pairs, :, :rows] - dot_parts(two_parts(incoming), low_head, low_tail, 1)
    upper = vectors[pairs + 1] - dot_parts(two_parts(middle), high_head, high_tail, 1)
    taken = dot_parts(two_parts(from_above), high_head[:rows], high_tail[:rows], 0)
    middle_above = upper[:, rows:] - taken
    is_upper = pos_ref[1] == 1
    kept = jnp.concatenate(
        [
            jnp.where(is_upper, from_above, middle_above),
            jnp.where(is_upper, middle, incoming),
            jnp.where(is_upper, upper[:, :rows], middle),
        ],
        axis=1,
    )[:share]
    for piece in range(out_ref.shape[0]):
        out_ref[piece] = kept


def run_chain(position, coupling_all, shares, low, high, low_vec, high_vec, below, above, targets):
    share, rows = below.shape
    pairs = coupling_all.shape[0]
    vmem = pl.BlockSpec(memory_space=pltpu.VMEM)
    return pl.pallas_call(
        chain_kernel,
        out_shape=jax.ShapeDtypeStruct((targets, share, 3 * rows), jnp.float32),
        in_specs=[pl.BlockSpec(memory_space=pltpu.SMEM), pl.BlockSpec(memory_space=pl.ANY)]
        + [vmem] * 7,
        out_specs=vmem,
        scratch_shapes=[
            pltpu.VMEM((pairs, 2 * rows, rows), jnp.float32),
            pltpu.VMEM((pairs, rows, rows), jnp.bfloat16),
            pltpu.VMEM((pairs, rows, rows), jnp.bfloat16),
            pltpu.VMEM((pairs + 2, padded, 2 * rows), jnp.float32),
            pltpu.VMEM((pairs, padded, rows), jnp.float32),
            pltpu.VMEM((pairs, padded, rows), jnp.float32),
            pltpu.SemaphoreType.DMA((pairs,)),
        ],
        compiler_params=pltpu.CompilerParams(vmem_limit_bytes=32 * 1024 * 1024),
        cost_estimate=pl.CostEstimate(
            flops=12 * pairs * 16 * rows * rows,
            bytes_accessed=8 * pairs * rows * rows,
            transcendentals=0,
        ),
        name="chain",
    )(position, coupling_all, shares, low, high, low_vec, high_vec, below, above)


def on_device(right_side, inverse_blocks, panels, receive_rows, below_update, above_solution):
    rhs = right_side.shape[0]
    block = inverse_blocks.shape[0]
    rows = panels.shape[0]
    front_count = lax.axis_size("front")
    front_pos = lax.axis_index("front")
    leaf_pos = lax.axis_index("leaf")
    leaf_count = lax.axis_size("leaf")
    is_upper = leaf_pos % 2 == 1
    share = rhs // front_count
    targets = receive_rows[0]

    pieces = ring_along_z(gather_along_x(right_side))
    picked = jnp.take(inverse_blocks, targets, axis=1)
    stacked = jnp.concatenate([panels, picked.T], axis=0)
    coupling = scatter_front(product(stacked, picked))
    coupling = gather_front(coupling).reshape(2 * rows, rows)

    swap = [(s, s ^ 1) for s in range(leaf_count)]
    mate = lax.ppermute(coupling, "leaf", swap)
    low = jnp.where(is_upper, mate, coupling)
    high = jnp.where(is_upper, coupling, mate)
    c_low, c_high, g_high = (low[:rows], high[:rows], high[rows:])
    lifted = product(g_high, c_low)
    c_pair = -product(c_high, c_low)
    g_pair = low[rows:] + product(c_low.T, lifted)
    pair_half = jnp.where(is_upper, g_pair, c_pair)
    coupling_all = gather_leaf(pair_half).reshape(leaf_count // 2, 2 * rows, rows)

    local_forward, vectors = run_forward(
        front_pos // x_chips, pieces, inverse_blocks, stacked, front_count
    )
    vectors = jnp.sum(exchange(vectors), axis=0)
    mate_vectors = lax.ppermute(vectors, "leaf", swap)
    low_vec = jnp.where(is_upper, mate_vectors, vectors)
    high_vec = jnp.where(is_upper, vectors, mate_vectors)
    u_own, w_own = (vectors[:, :rows], vectors[:, rows:])
    u_moved = -product_nt(u_own, c_high)
    w_moved = product(jnp.where(is_upper, w_own, u_own), jnp.where(is_upper, -c_low, lifted))
    own_share = jnp.concatenate(
        [
            jnp.where(is_upper, u_own, u_moved),
            jnp.where(is_upper, w_moved, w_own + w_moved),
        ],
        axis=1,
    )
    shares = gather_leaf_small(own_share)

    below_rows = lax.dynamic_slice_in_dim(below_update, front_pos * share, share, 0)
    above_rows = lax.dynamic_slice_in_dim(above_solution, front_pos * share, share, 0)
    position = jnp.stack([leaf_pos // 2, leaf_pos % 2])
    result = exchange(
        run_chain(
            position, coupling_all, shares, low, high, low_vec, high_vec,
            below_rows, above_rows, front_count,
        )
    )
    result = result.reshape(rhs, 3 * rows)
    update_share = rows // front_count
    sent_updates = lax.dynamic_slice_in_dim(
        result, 2 * rows + front_pos * update_share, update_share, 1
    )
    reduced = local_forward - product(result[:, : 2 * rows], stacked)
    spread = product(reduced, inverse_blocks)
    spread = spread.reshape(rhs, front_count, block).transpose(1, 0, 2)
    solution = jnp.sum(exchange(spread), axis=0)
    return (solution, sent_updates)


def solution(mesh):
    in_specs = (
        P(None, ("leaf", "front")),
        P(("leaf", "front"), None),
        P("leaf", "front"),
        P("leaf", None),
        P(),
        P(),
    )
    out_specs = (P(None, ("leaf", "front")), P(None, ("leaf", "front")))
    return jax.shard_map(
        on_device, mesh=mesh, in_specs=in_specs, out_specs=out_specs, check_vma=False
    )
```

```python
import functools

import jax
import jax.numpy as jnp
from jax import lax
from jax.experimental import pallas as pl
from jax.experimental.pallas import tpu as pltpu
from jax.sharding import PartitionSpec as P

exact = lax.Precision.HIGHEST
x_chips = 4
padded = 8
early = 5


def product(left, right):
    return jnp.dot(left, right, precision=exact, preferred_element_type=jnp.float32)


def product_nt(left, right):
    return lax.dot_general(
        left, right, (((1,), (1,)), ((), ())), precision=exact, preferred_element_type=jnp.float32
    )


def exchange(blocks, axis="front", groups=None):
    return lax.all_to_all(blocks, axis, 0, 0, tiled=True, axis_index_groups=groups)


def copies(block, count):
    return jnp.broadcast_to(block[None], (count, *block.shape))


def gather_front(block):
    return exchange(copies(block, lax.axis_size("front")))


def scatter_front(total):
    count = lax.axis_size("front")
    pieces = total.reshape(count, total.shape[0] // count, *total.shape[1:])
    return jnp.sum(exchange(pieces), axis=0)


def gather_leaf(block):
    return lax.all_gather(block, "leaf", axis=0)


def gather_leaf_small(block):
    return exchange(copies(block, lax.axis_size("leaf")), "leaf")


def gather_along_x(block):
    count = lax.axis_size("front")
    groups = [list(range(first, first + x_chips)) for first in range(0, count, x_chips)]
    return lax.all_gather(block, "front", axis=0, axis_index_groups=groups)


def ring_along_z(block):
    count = lax.axis_size("front")
    turns = count // x_chips
    later = [(f, (f + x_chips) % count) for f in range(count)]
    earlier = [(target, source) for source, target in later]
    offsets, pieces = [0], [block]
    behind = ahead = block
    for step in range(1, turns // 2 + 1):
        behind = lax.ppermute(behind, "front", later)
        offsets.append(turns - step)
        pieces.append(behind)
        if step < turns - step:
            ahead = lax.ppermute(ahead, "front", earlier)
            offsets.append(step)
            pieces.append(ahead)
    return offsets, pieces


def split(value):
    head = value.astype(jnp.bfloat16)
    return head, (value - head.astype(jnp.float32)).astype(jnp.bfloat16)


def two_parts(value):
    head, tail = split(value)
    return jnp.concatenate([head.astype(jnp.float32), tail.astype(jnp.float32)]).astype(
        jnp.bfloat16
    )


def dot_parts(parts, head, tail, contract):
    dims = (((1,), (contract,)), ((), ()))
    both = lax.dot_general(parts, head, dims, preferred_element_type=jnp.float32)
    both += lax.dot_general(parts, tail, dims, preferred_element_type=jnp.float32)
    return both[:padded] + both[padded:]


def forward_kernel(offsets, pos_ref, inverse_ref, stacked_ref, *refs):
    pieces, (forward_ref, vector_ref) = refs[:-2], refs[-2:]
    planes, rhs, block = pieces[0].shape
    width = planes * block
    total = jnp.zeros((2 * rhs, 2 * block), jnp.float32)
    for offset, piece in zip(offsets, pieces):
        place = lax.rem(pos_ref[0] + offset, len(offsets))
        columns = pl.ds(pl.multiple_of(place * width, width), width)
        side = jnp.concatenate([piece[x] for x in range(planes)], axis=1)
        total += lax.dot_general(
            two_parts(side),
            two_parts(inverse_ref[:, columns]),
            (((1,), (1,)), ((), ())),
            preferred_element_type=jnp.float32,
        )
    forward = fold(total, rhs, block)
    forward_ref[...] = forward
    vectors = lax.dot_general(
        two_parts(forward),
        two_parts(stacked_ref[...]),
        (((1,), (1,)), ((), ())),
        preferred_element_type=jnp.float32,
    )
    vectors = fold(vectors, rhs, stacked_ref.shape[0])
    share = vector_ref.shape[1]
    for piece in range(vector_ref.shape[0]):
        vector_ref[piece] = vectors[piece * share : (piece + 1) * share]


def fold(parts, rows, columns):
    small = parts[rows:, columns:] + (parts[rows:, :columns] + parts[:rows, columns:])
    return small + parts[:rows, :columns]


def run_forward(z_pos, offsets, pieces, inverse_blocks, stacked, targets):
    rhs = pieces[0].shape[1]
    block = inverse_blocks.shape[0]
    vmem = pl.BlockSpec(memory_space=pltpu.VMEM)
    return pl.pallas_call(
        functools.partial(forward_kernel, offsets),
        out_shape=(
            jax.ShapeDtypeStruct((rhs, block), jnp.float32),
            jax.ShapeDtypeStruct((targets, rhs // targets, stacked.shape[0]), jnp.float32),
        ),
        in_specs=[pl.BlockSpec(memory_space=pltpu.SMEM)] + [vmem] * (2 + len(pieces)),
        out_specs=(vmem, vmem),
        compiler_params=pltpu.CompilerParams(vmem_limit_bytes=32 * 1024 * 1024),
        cost_estimate=pl.CostEstimate(
            flops=8 * rhs * block * inverse_blocks.shape[1],
            bytes_accessed=4 * inverse_blocks.size + 4 * rhs * inverse_blocks.shape[1],
            transcendentals=0,
        ),
        name="forward",
    )(z_pos.reshape(1), inverse_blocks, stacked, *pieces)


def chain_kernel(
    pos_ref, coupling_ref, share_ref, low_ref, high_ref, low_vec_ref, high_vec_ref,
    below_ref, above_ref, out_ref, held, head, tail, vectors, into, above, sems,
):
    pairs = held.shape[0]
    share, rows = below_ref.shape

    def fetch(y):
        return pltpu.make_async_copy(coupling_ref.at[y], held.at[y], sems.at[y])

    for y in range(pairs):
        fetch(y).start()
    vectors[...] = jnp.zeros_like(vectors)
    into[0] = jnp.zeros_like(into[0])
    above[pairs - 1] = jnp.zeros_like(into[0])
    for y in range(pairs):
        vectors[y, :share, :] = share_ref[2 * y] + share_ref[2 * y + 1]
    vectors[pairs, :share, :] = low_vec_ref[...]
    vectors[pairs + 1, :share, :] = high_vec_ref[...]
    into[0, :share, :] = below_ref[...]
    above[pairs - 1, :share, :] = above_ref[...]

    low_head, low_tail = split(low_ref[:rows])
    high_head, high_tail = split(high_ref[...])
    incoming = into[0]
    for y in range(pairs):
        fetch(y).wait()
        block_head, block_tail = split(held[y])
        head[y] = block_head[:rows]
        tail[y] = block_tail[:rows]
        result = vectors[y] - dot_parts(two_parts(incoming), block_head, block_tail, 1)
        incoming = result[:, :rows]
        if y + 1 < pairs:
            into[y + 1] = incoming
        vectors[y] = result
    from_above = above[pairs - 1]
    for y in range(pairs - 1, 0, -1):
        taken = dot_parts(two_parts(from_above), head[y], tail[y], 0)
        from_above = vectors[y, :, rows:] - taken
        above[y - 1] = from_above

    chip = pos_ref[0]
    incoming = into[chip]
    from_above = above[chip]
    middle = vectors[pairs, :, :rows] - dot_parts(two_parts(incoming), low_head, low_tail, 1)
    upper = vectors[pairs + 1] - dot_parts(two_parts(middle), high_head, high_tail, 1)
    taken = dot_parts(two_parts(from_above), high_head[:rows], high_tail[:rows], 0)
    middle_above = upper[:, rows:] - taken
    is_upper = pos_ref[1] == 1
    kept = jnp.concatenate(
        [
            jnp.where(is_upper, from_above, middle_above),
            jnp.where(is_upper, middle, incoming),
            jnp.where(is_upper, upper[:, :rows], middle),
        ],
        axis=1,
    )[:share]
    for piece in range(out_ref.shape[0]):
        out_ref[piece] = kept


def run_chain(position, coupling_all, shares, low, high, low_vec, high_vec, below, above, targets):
    share, rows = below.shape
    pairs = coupling_all.shape[0]
    vmem = pl.BlockSpec(memory_space=pltpu.VMEM)
    return pl.pallas_call(
        chain_kernel,
        out_shape=jax.ShapeDtypeStruct((targets, share, 3 * rows), jnp.float32),
        in_specs=[pl.BlockSpec(memory_space=pltpu.SMEM), pl.BlockSpec(memory_space=pl.ANY)]
        + [vmem] * 7,
        out_specs=vmem,
        scratch_shapes=[
            pltpu.VMEM((pairs, 2 * rows, rows), jnp.float32),
            pltpu.VMEM((pairs, rows, rows), jnp.bfloat16),
            pltpu.VMEM((pairs, rows, rows), jnp.bfloat16),
            pltpu.VMEM((pairs + 2, padded, 2 * rows), jnp.float32),
            pltpu.VMEM((pairs, padded, rows), jnp.float32),
            pltpu.VMEM((pairs, padded, rows), jnp.float32),
            pltpu.SemaphoreType.DMA((pairs,)),
        ],
        compiler_params=pltpu.CompilerParams(vmem_limit_bytes=32 * 1024 * 1024),
        cost_estimate=pl.CostEstimate(
            flops=12 * pairs * 16 * rows * rows,
            bytes_accessed=8 * pairs * rows * rows,
            transcendentals=0,
        ),
        name="chain",
    )(position, coupling_all, shares, low, high, low_vec, high_vec, below, above)


def on_device(right_side, inverse_blocks, panels, receive_rows, below_update, above_solution):
    rhs = right_side.shape[0]
    block = inverse_blocks.shape[0]
    rows = panels.shape[0]
    front_count = lax.axis_size("front")
    front_pos = lax.axis_index("front")
    leaf_pos = lax.axis_index("leaf")
    leaf_count = lax.axis_size("leaf")
    is_upper = leaf_pos % 2 == 1
    share = rhs // front_count
    targets = receive_rows[0]

    plane = gather_along_x(right_side)
    picked = jnp.take(inverse_blocks, targets, axis=1)
    stacked = jnp.concatenate([panels, picked.T], axis=0)
    coupling = scatter_front(product(stacked, picked))
    coupling, plane = lax.optimization_barrier((coupling, plane))
    offsets, pieces = ring_along_z(plane)
    coupling = gather_front(coupling).reshape(2 * rows, rows)
    coupling, *pieces[:early] = lax.optimization_barrier((coupling, *pieces[:early]))

    swap = [(s, s ^ 1) for s in range(leaf_count)]
    mate = lax.ppermute(coupling, "leaf", swap)
    low = jnp.where(is_upper, mate, coupling)
    high = jnp.where(is_upper, coupling, mate)
    c_low, c_high, g_high = (low[:rows], high[:rows], high[rows:])
    lifted = product(g_high, c_low)
    c_pair = -product(c_high, c_low)
    g_pair = low[rows:] + product(c_low.T, lifted)
    pair_half = jnp.where(is_upper, g_pair, c_pair)
    coupling_all = gather_leaf(pair_half).reshape(leaf_count // 2, 2 * rows, rows)

    local_forward, vectors = run_forward(
        front_pos // x_chips, offsets, pieces, inverse_blocks, stacked, front_count
    )
    vectors = jnp.sum(exchange(vectors), axis=0)
    mate_vectors = lax.ppermute(vectors, "leaf", swap)
    low_vec = jnp.where(is_upper, mate_vectors, vectors)
    high_vec = jnp.where(is_upper, vectors, mate_vectors)
    u_own, w_own = (vectors[:, :rows], vectors[:, rows:])
    u_moved = -product_nt(u_own, c_high)
    w_moved = product(jnp.where(is_upper, w_own, u_own), jnp.where(is_upper, -c_low, lifted))
    own_share = jnp.concatenate(
        [
            jnp.where(is_upper, u_own, u_moved),
            jnp.where(is_upper, w_moved, w_own + w_moved),
        ],
        axis=1,
    )
    shares = gather_leaf_small(own_share)

    below_rows = lax.dynamic_slice_in_dim(below_update, front_pos * share, share, 0)
    above_rows = lax.dynamic_slice_in_dim(above_solution, front_pos * share, share, 0)
    position = jnp.stack([leaf_pos // 2, leaf_pos % 2])
    result = exchange(
        run_chain(
            position, coupling_all, shares, low, high, low_vec, high_vec,
            below_rows, above_rows, front_count,
        )
    )
    result = result.reshape(rhs, 3 * rows)
    update_share = rows // front_count
    sent_updates = lax.dynamic_slice_in_dim(
        result, 2 * rows + front_pos * update_share, update_share, 1
    )
    reduced = local_forward - product(result[:, : 2 * rows], stacked)
    spread = product(reduced, inverse_blocks)
    spread = spread.reshape(rhs, front_count, block).transpose(1, 0, 2)
    solution = jnp.sum(exchange(spread), axis=0)
    return (solution, sent_updates)


def solution(mesh):
    in_specs = (
        P(None, ("leaf", "front")),
        P(("leaf", "front"), None),
        P("leaf", "front"),
        P("leaf", None),
        P(),
        P(),
    )
    out_specs = (P(None, ("leaf", "front")), P(None, ("leaf", "front")))
    return jax.shard_map(
        on_device, mesh=mesh, in_specs=in_specs, out_specs=out_specs, check_vma=False
    )
```

```python
import jax
import jax.numpy as jnp
from jax import lax
from jax.experimental import pallas as pl
from jax.experimental.pallas import tpu as pltpu
from jax.sharding import PartitionSpec as P

exact = lax.Precision.HIGHEST
x_chips = 4
padded = 8


def product(left, right):
    return jnp.dot(left, right, precision=exact, preferred_element_type=jnp.float32)


def product_nt(left, right):
    return lax.dot_general(
        left, right, (((1,), (1,)), ((), ())), precision=exact, preferred_element_type=jnp.float32
    )


def exchange(blocks, axis="front", groups=None):
    return lax.all_to_all(blocks, axis, 0, 0, tiled=True, axis_index_groups=groups)


def copies(block, count):
    return jnp.broadcast_to(block[None], (count, *block.shape))


def gather_front(block):
    return exchange(copies(block, lax.axis_size("front")))


def gather_leaf(block):
    return lax.all_gather(block, "leaf", axis=0)


def gather_leaf_small(block):
    return exchange(copies(block, lax.axis_size("leaf")), "leaf")


def gather_along_x(block):
    count = lax.axis_size("front")
    groups = [list(range(first, first + x_chips)) for first in range(0, count, x_chips)]
    return exchange(copies(block, x_chips), "front", groups)


def split(value):
    head = value.astype(jnp.bfloat16)
    return head, (value - head.astype(jnp.float32)).astype(jnp.bfloat16)


def two_parts(value):
    head, tail = split(value)
    return jnp.concatenate([head.astype(jnp.float32), tail.astype(jnp.float32)]).astype(
        jnp.bfloat16
    )


def dot_parts(parts, head, tail, contract):
    dims = (((1,), (contract,)), ((), ()))
    both = lax.dot_general(parts, head, dims, preferred_element_type=jnp.float32)
    both += lax.dot_general(parts, tail, dims, preferred_element_type=jnp.float32)
    return both[:padded] + both[padded:]


def fold(parts, rows, columns):
    small = parts[rows:, columns:] + (parts[rows:, :columns] + parts[:rows, columns:])
    return small + parts[:rows, :columns]


def two_columns(value):
    head, tail = split(value)
    return jnp.concatenate([head, tail], axis=1)


def forward_kernel(side_ref, inverse_ref, stacked_ref, forward_ref, vector_ref):
    chunks, blocks, chunk, block = side_ref.shape
    rhs = chunks * chunk
    group = 4
    nt = (((1,), (1,)), ((), ()))
    total = jnp.zeros((2 * rhs, 2 * block), jnp.float32)
    for first in range(0, blocks, group):
        side = jnp.concatenate(
            [
                jnp.concatenate([side_ref[c, first + j] for j in range(group)], axis=1)
                for c in range(chunks)
            ]
        )
        weights = two_parts(inverse_ref[:, first * block : (first + group) * block])
        total += lax.dot_general(
            two_parts(side), weights, nt, preferred_element_type=jnp.float32
        )
    forward = fold(total, rhs, block)
    forward_ref[...] = forward
    vectors = lax.dot_general(
        two_parts(forward), two_parts(stacked_ref[...]), nt, preferred_element_type=jnp.float32
    )
    vectors = fold(vectors, rhs, stacked_ref.shape[0])
    share = vector_ref.shape[1]
    for piece in range(vector_ref.shape[0]):
        vector_ref[piece] = vectors[piece * share : (piece + 1) * share]


def run_forward(side, inverse_blocks, stacked, targets):
    rhs = side.shape[0] * side.shape[2]
    block = inverse_blocks.shape[0]
    vmem = pl.BlockSpec(memory_space=pltpu.VMEM)
    return pl.pallas_call(
        forward_kernel,
        out_shape=(
            jax.ShapeDtypeStruct((rhs, block), jnp.float32),
            jax.ShapeDtypeStruct((targets, rhs // targets, stacked.shape[0]), jnp.float32),
        ),
        in_specs=[vmem] * 3,
        out_specs=(vmem, vmem),
        compiler_params=pltpu.CompilerParams(vmem_limit_bytes=32 * 1024 * 1024),
        cost_estimate=pl.CostEstimate(
            flops=8 * rhs * block * inverse_blocks.shape[1],
            bytes_accessed=4 * inverse_blocks.size + 4 * side.size,
            transcendentals=0,
        ),
        name="forward",
    )(side, inverse_blocks, stacked)


def spread_kernel(result_ref, forward_ref, stacked_ref, inverse_ref, out_ref, held):
    share = result_ref.shape[1]
    rhs, block = forward_ref.shape
    for piece in range(result_ref.shape[0]):
        held[piece * share : (piece + 1) * share, :] = result_ref[piece, :, : held.shape[1]]
    taken = jnp.dot(
        two_parts(held[...]), two_columns(stacked_ref[...]), preferred_element_type=jnp.float32
    )
    reduced = two_parts(forward_ref[...] - fold(taken, rhs, block))
    group = 2
    for first in range(0, out_ref.shape[0], group):
        weights = two_columns(inverse_ref[:, first * block : (first + group) * block])
        parts = jnp.dot(reduced, weights, preferred_element_type=jnp.float32)
        parts = fold(parts, rhs, group * block)
        for j in range(group):
            out_ref[first + j] = parts[:, j * block : (j + 1) * block]


def run_spread(result, forward, stacked, inverse_blocks):
    rhs, block = forward.shape
    vmem = pl.BlockSpec(memory_space=pltpu.VMEM)
    return pl.pallas_call(
        spread_kernel,
        out_shape=jax.ShapeDtypeStruct((inverse_blocks.shape[1] // block, rhs, block), jnp.float32),
        in_specs=[vmem] * 4,
        out_specs=vmem,
        scratch_shapes=[pltpu.VMEM((rhs, stacked.shape[0]), jnp.float32)],
        compiler_params=pltpu.CompilerParams(vmem_limit_bytes=32 * 1024 * 1024),
        cost_estimate=pl.CostEstimate(
            flops=8 * rhs * block * inverse_blocks.shape[1],
            bytes_accessed=4 * inverse_blocks.size + 4 * rhs * inverse_blocks.shape[1],
            transcendentals=0,
        ),
        name="spread",
    )(result, forward, stacked, inverse_blocks)


def chain_kernel(
    pos_ref, coupling_ref, share_ref, low_ref, high_ref, low_vec_ref, high_vec_ref,
    below_ref, above_ref, out_ref, held, head, tail, vectors, into, above, sems,
):
    pairs = held.shape[0]
    share, rows = below_ref.shape

    def fetch(y):
        return pltpu.make_async_copy(coupling_ref.at[y], held.at[y], sems.at[y])

    for y in range(pairs):
        fetch(y).start()
    vectors[...] = jnp.zeros_like(vectors)
    into[0] = jnp.zeros_like(into[0])
    above[pairs - 1] = jnp.zeros_like(into[0])
    for y in range(pairs):
        vectors[y, :share, :] = share_ref[2 * y] + share_ref[2 * y + 1]
    vectors[pairs, :share, :] = low_vec_ref[...]
    vectors[pairs + 1, :share, :] = high_vec_ref[...]
    into[0, :share, :] = below_ref[...]
    above[pairs - 1, :share, :] = above_ref[...]

    low_head, low_tail = split(low_ref[:rows])
    high_head, high_tail = split(high_ref[...])
    incoming = into[0]
    for y in range(pairs):
        fetch(y).wait()
        block_head, block_tail = split(held[y])
        head[y] = block_head[:rows]
        tail[y] = block_tail[:rows]
        result = vectors[y] - dot_parts(two_parts(incoming), block_head, block_tail, 1)
        incoming = result[:, :rows]
        if y + 1 < pairs:
            into[y + 1] = incoming
        vectors[y] = result
    from_above = above[pairs - 1]
    for y in range(pairs - 1, 0, -1):
        taken = dot_parts(two_parts(from_above), head[y], tail[y], 0)
        from_above = vectors[y, :, rows:] - taken
        above[y - 1] = from_above

    chip = pos_ref[0]
    incoming = into[chip]
    from_above = above[chip]
    middle = vectors[pairs, :, :rows] - dot_parts(two_parts(incoming), low_head, low_tail, 1)
    upper = vectors[pairs + 1] - dot_parts(two_parts(middle), high_head, high_tail, 1)
    taken = dot_parts(two_parts(from_above), high_head[:rows], high_tail[:rows], 0)
    middle_above = upper[:, rows:] - taken
    is_upper = pos_ref[1] == 1
    kept = jnp.concatenate(
        [
            jnp.where(is_upper, from_above, middle_above),
            jnp.where(is_upper, middle, incoming),
            jnp.where(is_upper, upper[:, :rows], middle),
        ],
        axis=1,
    )[:share]
    for piece in range(out_ref.shape[0]):
        out_ref[piece] = kept


def run_chain(position, coupling_all, shares, low, high, low_vec, high_vec, below, above, targets):
    share, rows = below.shape
    pairs = coupling_all.shape[0]
    vmem = pl.BlockSpec(memory_space=pltpu.VMEM)
    return pl.pallas_call(
        chain_kernel,
        out_shape=jax.ShapeDtypeStruct((targets, share, 3 * rows), jnp.float32),
        in_specs=[pl.BlockSpec(memory_space=pltpu.SMEM), pl.BlockSpec(memory_space=pltpu.HBM)]
        + [vmem] * 7,
        out_specs=vmem,
        scratch_shapes=[
            pltpu.VMEM((pairs, 2 * rows, rows), jnp.float32),
            pltpu.VMEM((pairs, rows, rows), jnp.bfloat16),
            pltpu.VMEM((pairs, rows, rows), jnp.bfloat16),
            pltpu.VMEM((pairs + 2, padded, 2 * rows), jnp.float32),
            pltpu.VMEM((pairs, padded, rows), jnp.float32),
            pltpu.VMEM((pairs, padded, rows), jnp.float32),
            pltpu.SemaphoreType.DMA((pairs,)),
        ],
        compiler_params=pltpu.CompilerParams(vmem_limit_bytes=32 * 1024 * 1024),
        cost_estimate=pl.CostEstimate(
            flops=12 * pairs * 16 * rows * rows,
            bytes_accessed=8 * pairs * rows * rows,
            transcendentals=0,
        ),
        name="chain",
    )(position, coupling_all, shares, low, high, low_vec, high_vec, below, above)


def on_device(right_side, inverse_blocks, panels, receive_rows, below_update, above_solution):
    rhs = right_side.shape[0]
    block = inverse_blocks.shape[0]
    rows = panels.shape[0]
    front_count = lax.axis_size("front")
    front_pos = lax.axis_index("front")
    leaf_pos = lax.axis_index("leaf")
    leaf_count = lax.axis_size("leaf")
    is_upper = leaf_pos % 2 == 1
    share = rhs // front_count
    targets = receive_rows[0]

    chunk = rhs // x_chips
    slice_rows = 2 * rows // front_count
    picked = jnp.take(inverse_blocks, targets, axis=1)
    stacked = jnp.concatenate([panels, picked.T], axis=0)
    own_coupling = product(stacked, picked).reshape(front_count, slice_rows, rows)
    own_chunks = jnp.tile(right_side.reshape(x_chips, chunk, block), (front_count // x_chips, 1, 1))
    arrived = exchange(jnp.concatenate([own_coupling, own_chunks], axis=2))
    coupling = jnp.sum(arrived[:, :, :rows], axis=0)
    side_chunk = arrived[:, :, rows:]
    coupling = gather_front(coupling).reshape(2 * rows, rows)

    swap = [(s, s ^ 1) for s in range(leaf_count)]
    mate = lax.ppermute(coupling, "leaf", swap)
    low = jnp.where(is_upper, mate, coupling)
    high = jnp.where(is_upper, coupling, mate)
    c_low, c_high, g_high = (low[:rows], high[:rows], high[rows:])
    lifted = product(g_high, c_low)
    c_pair = -product(c_high, c_low)
    g_pair = low[rows:] + product(c_low.T, lifted)
    pair_half = jnp.where(is_upper, g_pair, c_pair)
    pair_half, side_chunk = lax.optimization_barrier((pair_half, side_chunk))
    coupling_all = gather_leaf(pair_half).reshape(leaf_count // 2, 2 * rows, rows)

    local_forward, vectors = run_forward(
        gather_along_x(side_chunk), inverse_blocks, stacked, front_count
    )
    vectors = jnp.sum(exchange(vectors), axis=0)
    mate_vectors = lax.ppermute(vectors, "leaf", swap)
    low_vec = jnp.where(is_upper, mate_vectors, vectors)
    high_vec = jnp.where(is_upper, vectors, mate_vectors)
    u_own, w_own = (vectors[:, :rows], vectors[:, rows:])
    u_moved = -product_nt(u_own, c_high)
    w_moved = product(jnp.where(is_upper, w_own, u_own), jnp.where(is_upper, -c_low, lifted))
    own_share = jnp.concatenate(
        [
            jnp.where(is_upper, u_own, u_moved),
            jnp.where(is_upper, w_moved, w_own + w_moved),
        ],
        axis=1,
    )
    shares = gather_leaf_small(own_share)

    below_rows = lax.dynamic_slice_in_dim(below_update, front_pos * share, share, 0)
    above_rows = lax.dynamic_slice_in_dim(above_solution, front_pos * share, share, 0)
    position = jnp.stack([leaf_pos // 2, leaf_pos % 2])
    result = exchange(
        run_chain(
            position, coupling_all, shares, low, high, low_vec, high_vec,
            below_rows, above_rows, front_count,
        )
    )
    spread = run_spread(result, local_forward, stacked, inverse_blocks)
    solution = jnp.sum(exchange(spread), axis=0)
    update_share = rows // front_count
    updates = result[:, :, 2 * rows :].reshape(rhs, rows)
    sent_updates = lax.dynamic_slice_in_dim(updates, front_pos * update_share, update_share, 1)
    return (solution, sent_updates)


def solution(mesh):
    in_specs = (
        P(None, ("leaf", "front")),
        P(("leaf", "front"), None),
        P("leaf", "front"),
        P("leaf", None),
        P(),
        P(),
    )
    out_specs = (P(None, ("leaf", "front")), P(None, ("leaf", "front")))
    return jax.shard_map(
        on_device, mesh=mesh, in_specs=in_specs, out_specs=out_specs, check_vma=False
    )
```

```python
import jax
import jax.numpy as jnp
from jax import lax
from jax.experimental import pallas as pl
from jax.experimental.pallas import tpu as pltpu
from jax.sharding import PartitionSpec as P

exact = lax.Precision.HIGHEST
x_chips = 4
padded = 8


def product(left, right):
    return jnp.dot(left, right, precision=exact, preferred_element_type=jnp.float32)


def product_nt(left, right):
    return lax.dot_general(
        left, right, (((1,), (1,)), ((), ())), precision=exact, preferred_element_type=jnp.float32
    )


def exchange(blocks, axis="front", groups=None):
    return lax.all_to_all(blocks, axis, 0, 0, tiled=True, axis_index_groups=groups)


def copies(block, count):
    return jnp.broadcast_to(block[None], (count, *block.shape))


def gather_front(block):
    return exchange(copies(block, lax.axis_size("front")))


def gather_leaf(block):
    return lax.all_gather(block, "leaf", axis=0)


def gather_leaf_small(block):
    return exchange(copies(block, lax.axis_size("leaf")), "leaf")


def gather_along_x(block):
    count = lax.axis_size("front")
    groups = [list(range(first, first + x_chips)) for first in range(0, count, x_chips)]
    return lax.all_gather(block, "front", axis=0, axis_index_groups=groups)


def split(value):
    head = value.astype(jnp.bfloat16)
    return head, (value - head.astype(jnp.float32)).astype(jnp.bfloat16)


def two_parts(value):
    head, tail = split(value)
    return jnp.concatenate([head.astype(jnp.float32), tail.astype(jnp.float32)]).astype(
        jnp.bfloat16
    )


def dot_parts(parts, head, tail, contract):
    dims = (((1,), (contract,)), ((), ()))
    both = lax.dot_general(parts, head, dims, preferred_element_type=jnp.float32)
    both += lax.dot_general(parts, tail, dims, preferred_element_type=jnp.float32)
    return both[:padded] + both[padded:]


def fold(parts, rows, columns):
    small = parts[rows:, columns:] + (parts[rows:, :columns] + parts[:rows, columns:])
    return small + parts[:rows, :columns]


def two_columns(value):
    head, tail = split(value)
    return jnp.concatenate([head, tail], axis=1)


def forward_kernel(side_ref, inverse_ref, stacked_ref, forward_ref, vector_ref):
    chunks, blocks, chunk, block = side_ref.shape
    rhs = chunks * chunk
    group = 4
    nt = (((1,), (1,)), ((), ()))
    total = jnp.zeros((2 * rhs, 2 * block), jnp.float32)
    for first in range(0, blocks, group):
        side = jnp.concatenate(
            [
                jnp.concatenate([side_ref[c, first + j] for j in range(group)], axis=1)
                for c in range(chunks)
            ]
        )
        weights = two_parts(inverse_ref[:, first * block : (first + group) * block])
        total += lax.dot_general(
            two_parts(side), weights, nt, preferred_element_type=jnp.float32
        )
    forward = fold(total, rhs, block)
    forward_ref[...] = forward
    vectors = lax.dot_general(
        two_parts(forward), two_parts(stacked_ref[...]), nt, preferred_element_type=jnp.float32
    )
    vectors = fold(vectors, rhs, stacked_ref.shape[0])
    share = vector_ref.shape[1]
    for piece in range(vector_ref.shape[0]):
        vector_ref[piece] = vectors[piece * share : (piece + 1) * share]


def run_forward(side, inverse_blocks, stacked, targets):
    rhs = side.shape[0] * side.shape[2]
    block = inverse_blocks.shape[0]
    vmem = pl.BlockSpec(memory_space=pltpu.VMEM)
    return pl.pallas_call(
        forward_kernel,
        out_shape=(
            jax.ShapeDtypeStruct((rhs, block), jnp.float32),
            jax.ShapeDtypeStruct((targets, rhs // targets, stacked.shape[0]), jnp.float32),
        ),
        in_specs=[vmem] * 3,
        out_specs=(vmem, vmem),
        compiler_params=pltpu.CompilerParams(vmem_limit_bytes=32 * 1024 * 1024),
        cost_estimate=pl.CostEstimate(
            flops=8 * rhs * block * inverse_blocks.shape[1],
            bytes_accessed=4 * inverse_blocks.size + 4 * side.size,
            transcendentals=0,
        ),
        name="forward",
    )(side, inverse_blocks, stacked)


def spread_kernel(result_ref, forward_ref, stacked_ref, inverse_ref, out_ref, held):
    share = result_ref.shape[1]
    rhs, block = forward_ref.shape
    for piece in range(result_ref.shape[0]):
        held[piece * share : (piece + 1) * share, :] = result_ref[piece, :, : held.shape[1]]
    taken = jnp.dot(
        two_parts(held[...]), two_columns(stacked_ref[...]), preferred_element_type=jnp.float32
    )
    reduced = two_parts(forward_ref[...] - fold(taken, rhs, block))
    group = 2
    for first in range(0, out_ref.shape[0], group):
        weights = two_columns(inverse_ref[:, first * block : (first + group) * block])
        parts = jnp.dot(reduced, weights, preferred_element_type=jnp.float32)
        parts = fold(parts, rhs, group * block)
        for j in range(group):
            out_ref[first + j] = parts[:, j * block : (j + 1) * block]


def run_spread(result, forward, stacked, inverse_blocks):
    rhs, block = forward.shape
    vmem = pl.BlockSpec(memory_space=pltpu.VMEM)
    return pl.pallas_call(
        spread_kernel,
        out_shape=jax.ShapeDtypeStruct((inverse_blocks.shape[1] // block, rhs, block), jnp.float32),
        in_specs=[vmem] * 4,
        out_specs=vmem,
        scratch_shapes=[pltpu.VMEM((rhs, stacked.shape[0]), jnp.float32)],
        compiler_params=pltpu.CompilerParams(vmem_limit_bytes=32 * 1024 * 1024),
        cost_estimate=pl.CostEstimate(
            flops=8 * rhs * block * inverse_blocks.shape[1],
            bytes_accessed=4 * inverse_blocks.size + 4 * rhs * inverse_blocks.shape[1],
            transcendentals=0,
        ),
        name="spread",
    )(result, forward, stacked, inverse_blocks)


def chain_kernel(
    pos_ref, coupling_ref, share_ref, low_ref, high_ref, below_ref, above_ref, out_ref,
    held, head, tail, vectors, into, above, sems,
):
    pairs = held.shape[0]
    share, rows = below_ref.shape

    def fetch(y):
        return pltpu.make_async_copy(coupling_ref.at[y], held.at[y], sems.at[y])

    for y in range(pairs):
        fetch(y).start()
    vectors[...] = jnp.zeros_like(vectors)
    into[0] = jnp.zeros_like(into[0])
    above[pairs - 1] = jnp.zeros_like(into[0])
    for y in range(pairs):
        both = share_ref[2 * y] + share_ref[2 * y + 1]
        vectors[y, :share, :] = both[:, : 2 * rows]
    chip = pos_ref[0]
    vectors[pairs, :share, :] = share_ref[2 * chip][:, 2 * rows :]
    vectors[pairs + 1, :share, :] = share_ref[2 * chip + 1][:, 2 * rows :]
    into[0, :share, :] = below_ref[...]
    above[pairs - 1, :share, :] = above_ref[...]

    low_head, low_tail = split(low_ref[:rows])
    high_head, high_tail = split(high_ref[...])
    incoming = into[0]
    for y in range(pairs):
        fetch(y).wait()
        block_head, block_tail = split(held[y])
        head[y] = block_head[:rows]
        tail[y] = block_tail[:rows]
        result = vectors[y] - dot_parts(two_parts(incoming), block_head, block_tail, 1)
        incoming = result[:, :rows]
        if y + 1 < pairs:
            into[y + 1] = incoming
        vectors[y] = result
    from_above = above[pairs - 1]
    for y in range(pairs - 1, 0, -1):
        taken = dot_parts(two_parts(from_above), head[y], tail[y], 0)
        from_above = vectors[y, :, rows:] - taken
        above[y - 1] = from_above

    incoming = into[chip]
    from_above = above[chip]
    middle = vectors[pairs, :, :rows] - dot_parts(two_parts(incoming), low_head, low_tail, 1)
    upper = vectors[pairs + 1] - dot_parts(two_parts(middle), high_head, high_tail, 1)
    taken = dot_parts(two_parts(from_above), high_head[:rows], high_tail[:rows], 0)
    middle_above = upper[:, rows:] - taken
    is_upper = pos_ref[1] == 1
    kept = jnp.concatenate(
        [
            jnp.where(is_upper, from_above, middle_above),
            jnp.where(is_upper, middle, incoming),
            jnp.where(is_upper, upper[:, :rows], middle),
        ],
        axis=1,
    )[:share]
    for piece in range(out_ref.shape[0]):
        out_ref[piece] = kept


def run_chain(position, coupling_all, shares, low, high, below, above, targets):
    share, rows = below.shape
    pairs = coupling_all.shape[0]
    vmem = pl.BlockSpec(memory_space=pltpu.VMEM)
    return pl.pallas_call(
        chain_kernel,
        out_shape=jax.ShapeDtypeStruct((targets, share, 3 * rows), jnp.float32),
        in_specs=[pl.BlockSpec(memory_space=pltpu.SMEM), pl.BlockSpec(memory_space=pltpu.HBM)]
        + [vmem] * 5,
        out_specs=vmem,
        scratch_shapes=[
            pltpu.VMEM((pairs, 2 * rows, rows), jnp.float32),
            pltpu.VMEM((pairs, rows, rows), jnp.bfloat16),
            pltpu.VMEM((pairs, rows, rows), jnp.bfloat16),
            pltpu.VMEM((pairs + 2, padded, 2 * rows), jnp.float32),
            pltpu.VMEM((pairs, padded, rows), jnp.float32),
            pltpu.VMEM((pairs, padded, rows), jnp.float32),
            pltpu.SemaphoreType.DMA((pairs,)),
        ],
        compiler_params=pltpu.CompilerParams(vmem_limit_bytes=57 * 1024 * 1024),
        cost_estimate=pl.CostEstimate(
            flops=12 * pairs * 16 * rows * rows,
            bytes_accessed=8 * pairs * rows * rows,
            transcendentals=0,
        ),
        name="chain",
    )(position, coupling_all, shares, low, high, below, above)


def on_device(right_side, inverse_blocks, panels, receive_rows, below_update, above_solution):
    rhs = right_side.shape[0]
    block = inverse_blocks.shape[0]
    rows = panels.shape[0]
    front_count = lax.axis_size("front")
    front_pos = lax.axis_index("front")
    leaf_pos = lax.axis_index("leaf")
    leaf_count = lax.axis_size("leaf")
    is_upper = leaf_pos % 2 == 1
    share = rhs // front_count
    targets = receive_rows[0]

    chunk = rhs // x_chips
    slice_rows = 2 * rows // front_count
    picked = jnp.take(inverse_blocks, targets, axis=1)
    stacked = jnp.concatenate([panels, picked.T], axis=0)
    own_coupling = product(stacked, picked).reshape(front_count, slice_rows, rows)
    own_chunks = jnp.tile(right_side.reshape(x_chips, chunk, block), (front_count // x_chips, 1, 1))
    arrived = exchange(jnp.concatenate([own_coupling, own_chunks], axis=2))
    coupling = jnp.sum(arrived[:, :, :rows], axis=0)
    side_chunk = arrived[:, :, rows:]
    coupling = gather_front(coupling).reshape(2 * rows, rows)

    swap = [(s, s ^ 1) for s in range(leaf_count)]
    mate = lax.ppermute(coupling, "leaf", swap)
    low = jnp.where(is_upper, mate, coupling)
    high = jnp.where(is_upper, coupling, mate)
    c_low, c_high, g_high = (low[:rows], high[:rows], high[rows:])
    lifted = product(g_high, c_low)
    c_pair = -product(c_high, c_low)
    g_pair = low[rows:] + product(c_low.T, lifted)
    pair_half = jnp.where(is_upper, g_pair, c_pair)
    coupling_all = gather_leaf(pair_half).reshape(leaf_count // 2, 2 * rows, rows)

    local_forward, vectors = run_forward(
        gather_along_x(side_chunk), inverse_blocks, stacked, front_count
    )
    vectors = jnp.sum(exchange(vectors), axis=0)
    u_own, w_own = (vectors[:, :rows], vectors[:, rows:])
    u_moved = -product_nt(u_own, c_high)
    w_moved = product(jnp.where(is_upper, w_own, u_own), jnp.where(is_upper, -c_low, lifted))
    own_share = jnp.concatenate(
        [
            jnp.where(is_upper, u_own, u_moved),
            jnp.where(is_upper, w_moved, w_own + w_moved),
            vectors,
        ],
        axis=1,
    )
    shares = gather_leaf_small(own_share)

    below_rows = lax.dynamic_slice_in_dim(below_update, front_pos * share, share, 0)
    above_rows = lax.dynamic_slice_in_dim(above_solution, front_pos * share, share, 0)
    position = jnp.stack([leaf_pos // 2, leaf_pos % 2])
    result = exchange(
        run_chain(
            position, coupling_all, shares, low, high,
            below_rows, above_rows, front_count,
        )
    )
    spread = run_spread(result, local_forward, stacked, inverse_blocks)
    solution = jnp.sum(exchange(spread), axis=0)
    update_share = rows // front_count
    updates = result[:, :, 2 * rows :].reshape(rhs, rows)
    sent_updates = lax.dynamic_slice_in_dim(updates, front_pos * update_share, update_share, 1)
    return (solution, sent_updates)


def solution(mesh):
    in_specs = (
        P(None, ("leaf", "front")),
        P(("leaf", "front"), None),
        P("leaf", "front"),
        P("leaf", None),
        P(),
        P(),
    )
    out_specs = (P(None, ("leaf", "front")), P(None, ("leaf", "front")))
    return jax.shard_map(
        on_device, mesh=mesh, in_specs=in_specs, out_specs=out_specs, check_vma=False
    )
```

```python
import jax
import jax.numpy as jnp
from jax import lax
from jax.experimental import pallas as pl
from jax.experimental.pallas import tpu as pltpu
from jax.sharding import PartitionSpec as P

exact = lax.Precision.HIGHEST
x_chips = 4
padded = 8
in_flight = 3


def product(left, right):
    return jnp.dot(left, right, precision=exact, preferred_element_type=jnp.float32)


def product_nt(left, right):
    return lax.dot_general(
        left, right, (((1,), (1,)), ((), ())), precision=exact, preferred_element_type=jnp.float32
    )


def exchange(blocks, axis="front", groups=None):
    return lax.all_to_all(blocks, axis, 0, 0, tiled=True, axis_index_groups=groups)


def copies(block, count):
    return jnp.broadcast_to(block[None], (count, *block.shape))


def gather_front(block):
    return exchange(copies(block, lax.axis_size("front")))


def gather_leaf(block):
    return lax.all_gather(block, "leaf", axis=0)


def gather_leaf_small(block):
    return exchange(copies(block, lax.axis_size("leaf")), "leaf")


def gather_along_x(block):
    count = lax.axis_size("front")
    groups = [list(range(first, first + x_chips)) for first in range(0, count, x_chips)]
    return exchange(copies(block, x_chips), "front", groups)


def split(value):
    head = value.astype(jnp.bfloat16)
    return head, (value - head.astype(jnp.float32)).astype(jnp.bfloat16)


def two_parts(value):
    head, tail = split(value)
    return jnp.concatenate([head.astype(jnp.float32), tail.astype(jnp.float32)]).astype(
        jnp.bfloat16
    )


def dot_parts(parts, head, tail, contract):
    dims = (((1,), (contract,)), ((), ()))
    both = lax.dot_general(parts, head, dims, preferred_element_type=jnp.float32)
    both += lax.dot_general(parts, tail, dims, preferred_element_type=jnp.float32)
    return both[:padded] + both[padded:]


def fold(parts, rows, columns):
    small = parts[rows:, columns:] + (parts[rows:, :columns] + parts[:rows, columns:])
    return small + parts[:rows, :columns]


def two_columns(value):
    head, tail = split(value)
    return jnp.concatenate([head, tail], axis=1)


def forward_kernel(side_ref, inverse_ref, stacked_ref, forward_ref, vector_ref):
    chunks, blocks, chunk, block = side_ref.shape
    rhs = chunks * chunk
    group = 4
    nt = (((1,), (1,)), ((), ()))
    total = jnp.zeros((2 * rhs, 2 * block), jnp.float32)
    for first in range(0, blocks, group):
        side = jnp.concatenate(
            [
                jnp.concatenate([side_ref[c, first + j] for j in range(group)], axis=1)
                for c in range(chunks)
            ]
        )
        weights = two_parts(inverse_ref[:, first * block : (first + group) * block])
        total += lax.dot_general(
            two_parts(side), weights, nt, preferred_element_type=jnp.float32
        )
    forward = fold(total, rhs, block)
    forward_ref[...] = forward
    vectors = lax.dot_general(
        two_parts(forward), two_parts(stacked_ref[...]), nt, preferred_element_type=jnp.float32
    )
    vectors = fold(vectors, rhs, stacked_ref.shape[0])
    share = vector_ref.shape[1]
    for piece in range(vector_ref.shape[0]):
        vector_ref[piece] = vectors[piece * share : (piece + 1) * share]


def run_forward(side, inverse_blocks, stacked, targets):
    rhs = side.shape[0] * side.shape[2]
    block = inverse_blocks.shape[0]
    vmem = pl.BlockSpec(memory_space=pltpu.VMEM)
    return pl.pallas_call(
        forward_kernel,
        out_shape=(
            jax.ShapeDtypeStruct((rhs, block), jnp.float32),
            jax.ShapeDtypeStruct((targets, rhs // targets, stacked.shape[0]), jnp.float32),
        ),
        in_specs=[vmem] * 3,
        out_specs=(vmem, vmem),
        compiler_params=pltpu.CompilerParams(vmem_limit_bytes=32 * 1024 * 1024),
        cost_estimate=pl.CostEstimate(
            flops=8 * rhs * block * inverse_blocks.shape[1],
            bytes_accessed=4 * inverse_blocks.size + 4 * side.size,
            transcendentals=0,
        ),
        name="forward",
    )(side, inverse_blocks, stacked)


def spread_kernel(result_ref, forward_ref, stacked_ref, inverse_ref, out_ref, held):
    share = result_ref.shape[1]
    rhs, block = forward_ref.shape
    for piece in range(result_ref.shape[0]):
        held[piece * share : (piece + 1) * share, :] = result_ref[piece, :, : held.shape[1]]
    taken = jnp.dot(
        two_parts(held[...]), two_columns(stacked_ref[...]), preferred_element_type=jnp.float32
    )
    reduced = two_parts(forward_ref[...] - fold(taken, rhs, block))
    group = 2
    for first in range(0, out_ref.shape[0], group):
        weights = two_columns(inverse_ref[:, first * block : (first + group) * block])
        parts = jnp.dot(reduced, weights, preferred_element_type=jnp.float32)
        parts = fold(parts, rhs, group * block)
        for j in range(group):
            out_ref[first + j] = parts[:, j * block : (j + 1) * block]


def run_spread(result, forward, stacked, inverse_blocks):
    rhs, block = forward.shape
    vmem = pl.BlockSpec(memory_space=pltpu.VMEM)
    return pl.pallas_call(
        spread_kernel,
        out_shape=jax.ShapeDtypeStruct((inverse_blocks.shape[1] // block, rhs, block), jnp.float32),
        in_specs=[vmem] * 4,
        out_specs=vmem,
        scratch_shapes=[pltpu.VMEM((rhs, stacked.shape[0]), jnp.float32)],
        compiler_params=pltpu.CompilerParams(vmem_limit_bytes=32 * 1024 * 1024),
        cost_estimate=pl.CostEstimate(
            flops=8 * rhs * block * inverse_blocks.shape[1],
            bytes_accessed=4 * inverse_blocks.size + 4 * rhs * inverse_blocks.shape[1],
            transcendentals=0,
        ),
        name="spread",
    )(result, forward, stacked, inverse_blocks)


def chain_kernel(
    pos_ref, coupling_ref, vector_ref, below_ref, above_ref, out_ref,
    held, head, tail, vectors, into, above, sems,
):
    sections, share, _ = vector_ref.shape
    rows = below_ref.shape[1]

    def fetch(s):
        return pltpu.make_async_copy(coupling_ref.at[s], held.at[s], sems.at[s])

    for s in range(in_flight):
        fetch(s).start()
    vectors[...] = jnp.zeros_like(vectors)
    into[0] = jnp.zeros_like(into[0])
    above[sections - 1] = jnp.zeros_like(into[0])
    for s in range(sections):
        vectors[s, :share, :] = vector_ref[s]
    into[0, :share, :] = below_ref[...]
    above[sections - 1, :share, :] = above_ref[...]

    incoming = into[0]
    for s in range(sections):
        fetch(s).wait()
        if s + in_flight < sections:
            fetch(s + in_flight).start()
        block_head, block_tail = split(held[s])
        head[s] = block_head[:rows]
        tail[s] = block_tail[:rows]
        result = vectors[s] - dot_parts(two_parts(incoming), block_head, block_tail, 1)
        incoming = result[:, :rows]
        into[s + 1] = incoming
        vectors[s] = result
    from_above = above[sections - 1]
    for s in range(sections - 1, 0, -1):
        taken = dot_parts(two_parts(from_above), head[s], tail[s], 0)
        from_above = vectors[s, :, rows:] - taken
        above[s - 1] = from_above

    own = pos_ref[0]
    kept = jnp.concatenate([above[own], into[own], into[own + 1]], axis=1)[:share]
    for piece in range(out_ref.shape[0]):
        out_ref[piece] = kept


def run_chain(position, coupling_all, vector_all, below_rows, above_rows, targets):
    sections, share, _ = vector_all.shape
    rows = below_rows.shape[1]
    vmem = pl.BlockSpec(memory_space=pltpu.VMEM)
    return pl.pallas_call(
        chain_kernel,
        out_shape=jax.ShapeDtypeStruct((targets, share, 3 * rows), jnp.float32),
        in_specs=[
            pl.BlockSpec(memory_space=pltpu.SMEM),
            pl.BlockSpec(memory_space=pltpu.HBM),
            vmem,
            vmem,
            vmem,
        ],
        out_specs=vmem,
        scratch_shapes=[
            pltpu.VMEM((sections, 2 * rows, rows), jnp.float32),
            pltpu.VMEM((sections, rows, rows), jnp.bfloat16),
            pltpu.VMEM((sections, rows, rows), jnp.bfloat16),
            pltpu.VMEM((sections, padded, 2 * rows), jnp.float32),
            pltpu.VMEM((sections + 1, padded, rows), jnp.float32),
            pltpu.VMEM((sections, padded, rows), jnp.float32),
            pltpu.SemaphoreType.DMA((sections,)),
        ],
        compiler_params=pltpu.CompilerParams(vmem_limit_bytes=56 * 1024 * 1024),
        cost_estimate=pl.CostEstimate(
            flops=12 * sections * 16 * rows * rows,
            bytes_accessed=8 * sections * rows * rows,
            transcendentals=0,
        ),
        name="chain",
    )(position.reshape(1), coupling_all, vector_all, below_rows, above_rows)


def on_device(right_side, inverse_blocks, panels, receive_rows, below_update, above_solution):
    rhs = right_side.shape[0]
    block = inverse_blocks.shape[0]
    rows = panels.shape[0]
    front_count = lax.axis_size("front")
    front_pos = lax.axis_index("front")
    leaf_pos = lax.axis_index("leaf")
    share = rhs // front_count
    targets = receive_rows[0]

    chunk = rhs // x_chips
    slice_rows = 2 * rows // front_count
    picked = jnp.take(inverse_blocks, targets, axis=1)
    stacked = jnp.concatenate([panels, picked.T], axis=0)
    own_coupling = product(stacked, picked).reshape(front_count, slice_rows, rows)
    own_chunks = jnp.tile(right_side.reshape(x_chips, chunk, block), (front_count // x_chips, 1, 1))
    arrived = exchange(jnp.concatenate([own_coupling, own_chunks], axis=2))
    coupling = jnp.sum(arrived[:, :, :rows], axis=0)
    side_chunk = arrived[:, :, rows:]
    coupling = gather_front(coupling).reshape(2 * rows, rows)

    coupling, side_chunk = lax.optimization_barrier((coupling, side_chunk))
    coupling_all = gather_leaf(coupling)
    local_forward, vectors = run_forward(
        gather_along_x(side_chunk), inverse_blocks, stacked, front_count
    )
    vectors = jnp.sum(exchange(vectors), axis=0)
    vector_all = gather_leaf_small(vectors)

    below_rows = lax.dynamic_slice_in_dim(below_update, front_pos * share, share, 0)
    above_rows = lax.dynamic_slice_in_dim(above_solution, front_pos * share, share, 0)
    result = exchange(
        run_chain(leaf_pos, coupling_all, vector_all, below_rows, above_rows, front_count)
    )
    spread = run_spread(result, local_forward, stacked, inverse_blocks)
    solution = jnp.sum(exchange(spread), axis=0)
    update_share = rows // front_count
    updates = result[:, :, 2 * rows :].reshape(rhs, rows)
    sent_updates = lax.dynamic_slice_in_dim(updates, front_pos * update_share, update_share, 1)
    return (solution, sent_updates)


def solution(mesh):
    in_specs = (
        P(None, ("leaf", "front")),
        P(("leaf", "front"), None),
        P("leaf", "front"),
        P("leaf", None),
        P(),
        P(),
    )
    out_specs = (P(None, ("leaf", "front")), P(None, ("leaf", "front")))
    return jax.shard_map(
        on_device, mesh=mesh, in_specs=in_specs, out_specs=out_specs, check_vma=False
    )
```

```python
import jax
import jax.numpy as jnp
from jax import lax
from jax.experimental import pallas as pl
from jax.experimental.pallas import tpu as pltpu
from jax.sharding import PartitionSpec as P

exact = lax.Precision.HIGHEST
x_chips = 4
padded = 8


def product(left, right):
    return jnp.dot(left, right, precision=exact, preferred_element_type=jnp.float32)


def product_nt(left, right):
    return lax.dot_general(
        left, right, (((1,), (1,)), ((), ())), precision=exact, preferred_element_type=jnp.float32
    )


def exchange(blocks, axis="front", groups=None):
    return lax.all_to_all(blocks, axis, 0, 0, tiled=True, axis_index_groups=groups)


def copies(block, count):
    return jnp.broadcast_to(block[None], (count, *block.shape))


def gather_front(block):
    return exchange(copies(block, lax.axis_size("front")))


def gather_leaf(block):
    return lax.all_gather(block, "leaf", axis=0)


def gather_leaf_small(block):
    return exchange(copies(block, lax.axis_size("leaf")), "leaf")


def gather_along_x(block):
    count = lax.axis_size("front")
    groups = [list(range(first, first + x_chips)) for first in range(0, count, x_chips)]
    return exchange(copies(block, x_chips), "front", groups)


def split(value):
    head = value.astype(jnp.bfloat16)
    return head, (value - head.astype(jnp.float32)).astype(jnp.bfloat16)


def two_parts(value):
    head, tail = split(value)
    return jnp.concatenate([head.astype(jnp.float32), tail.astype(jnp.float32)]).astype(
        jnp.bfloat16
    )


def dot_parts(parts, head, tail, contract):
    dims = (((1,), (contract,)), ((), ()))
    both = lax.dot_general(parts, head, dims, preferred_element_type=jnp.float32)
    both += lax.dot_general(parts, tail, dims, preferred_element_type=jnp.float32)
    return both[:padded] + both[padded:]


def fold(parts, rows, columns):
    small = parts[rows:, columns:] + (parts[rows:, :columns] + parts[:rows, columns:])
    return small + parts[:rows, :columns]


def two_columns(value):
    head, tail = split(value)
    return jnp.concatenate([head, tail], axis=1)


def forward_kernel(side_ref, inverse_ref, stacked_ref, forward_ref, vector_ref):
    chunks, blocks, chunk, block = side_ref.shape
    rhs = chunks * chunk
    group = 4
    nt = (((1,), (1,)), ((), ()))
    total = jnp.zeros((2 * rhs, 2 * block), jnp.float32)
    for first in range(0, blocks, group):
        side = jnp.concatenate(
            [
                jnp.concatenate([side_ref[c, first + j] for j in range(group)], axis=1)
                for c in range(chunks)
            ]
        )
        weights = two_parts(inverse_ref[:, first * block : (first + group) * block])
        total += lax.dot_general(
            two_parts(side), weights, nt, preferred_element_type=jnp.float32
        )
    forward = fold(total, rhs, block)
    forward_ref[...] = forward
    vectors = lax.dot_general(
        two_parts(forward), two_parts(stacked_ref[...]), nt, preferred_element_type=jnp.float32
    )
    vectors = fold(vectors, rhs, stacked_ref.shape[0])
    share = vector_ref.shape[1]
    for piece in range(vector_ref.shape[0]):
        vector_ref[piece] = vectors[piece * share : (piece + 1) * share]


def run_forward(side, inverse_blocks, stacked, targets):
    rhs = side.shape[0] * side.shape[2]
    block = inverse_blocks.shape[0]
    vmem = pl.BlockSpec(memory_space=pltpu.VMEM)
    return pl.pallas_call(
        forward_kernel,
        out_shape=(
            jax.ShapeDtypeStruct((rhs, block), jnp.float32),
            jax.ShapeDtypeStruct((targets, rhs // targets, stacked.shape[0]), jnp.float32),
        ),
        in_specs=[vmem] * 3,
        out_specs=(vmem, vmem),
        compiler_params=pltpu.CompilerParams(vmem_limit_bytes=16 * 1024 * 1024),
        cost_estimate=pl.CostEstimate(
            flops=8 * rhs * block * inverse_blocks.shape[1],
            bytes_accessed=4 * inverse_blocks.size + 4 * side.size,
            transcendentals=0,
        ),
        name="forward",
    )(side, inverse_blocks, stacked)


def spread_kernel(result_ref, forward_ref, stacked_ref, inverse_ref, out_ref, held):
    share = result_ref.shape[1]
    rhs, block = forward_ref.shape
    for piece in range(result_ref.shape[0]):
        held[piece * share : (piece + 1) * share, :] = result_ref[piece, :, : held.shape[1]]
    taken = jnp.dot(
        two_parts(held[...]), two_columns(stacked_ref[...]), preferred_element_type=jnp.float32
    )
    reduced = two_parts(forward_ref[...] - fold(taken, rhs, block))
    group = 2
    for first in range(0, out_ref.shape[0], group):
        weights = two_columns(inverse_ref[:, first * block : (first + group) * block])
        parts = jnp.dot(reduced, weights, preferred_element_type=jnp.float32)
        parts = fold(parts, rhs, group * block)
        for j in range(group):
            out_ref[first + j] = parts[:, j * block : (j + 1) * block]


def run_spread(result, forward, stacked, inverse_blocks):
    rhs, block = forward.shape
    vmem = pl.BlockSpec(memory_space=pltpu.VMEM)
    return pl.pallas_call(
        spread_kernel,
        out_shape=jax.ShapeDtypeStruct((inverse_blocks.shape[1] // block, rhs, block), jnp.float32),
        in_specs=[vmem] * 4,
        out_specs=vmem,
        scratch_shapes=[pltpu.VMEM((rhs, stacked.shape[0]), jnp.float32)],
        compiler_params=pltpu.CompilerParams(vmem_limit_bytes=16 * 1024 * 1024),
        cost_estimate=pl.CostEstimate(
            flops=8 * rhs * block * inverse_blocks.shape[1],
            bytes_accessed=4 * inverse_blocks.size + 4 * rhs * inverse_blocks.shape[1],
            transcendentals=0,
        ),
        name="spread",
    )(result, forward, stacked, inverse_blocks)


def chain_kernel(
    pos_ref, coupling_ref, share_ref, low_ref, high_ref, below_ref, above_ref, out_ref,
    held, head, tail, vectors, into, above, sems,
):
    pairs = held.shape[0]
    share, rows = below_ref.shape

    def fetch(y):
        return pltpu.make_async_copy(coupling_ref.at[y], held.at[y], sems.at[y])

    for y in range(pairs):
        fetch(y).start()
    vectors[...] = jnp.zeros_like(vectors)
    into[0] = jnp.zeros_like(into[0])
    above[pairs - 1] = jnp.zeros_like(into[0])
    for y in range(pairs):
        both = share_ref[2 * y] + share_ref[2 * y + 1]
        vectors[y, :share, :] = both[:, : 2 * rows]
    chip = pos_ref[0]
    vectors[pairs, :share, :] = share_ref[2 * chip][:, 2 * rows :]
    vectors[pairs + 1, :share, :] = share_ref[2 * chip + 1][:, 2 * rows :]
    into[0, :share, :] = below_ref[...]
    above[pairs - 1, :share, :] = above_ref[...]

    low_head, low_tail = split(low_ref[:rows])
    high_head, high_tail = split(high_ref[...])
    incoming = into[0]
    for y in range(pairs):
        fetch(y).wait()
        block_head, block_tail = split(held[y])
        head[y] = block_head[:rows]
        tail[y] = block_tail[:rows]
        result = vectors[y] - dot_parts(two_parts(incoming), block_head, block_tail, 1)
        incoming = result[:, :rows]
        if y + 1 < pairs:
            into[y + 1] = incoming
        vectors[y] = result
    from_above = above[pairs - 1]
    for y in range(pairs - 1, 0, -1):
        taken = dot_parts(two_parts(from_above), head[y], tail[y], 0)
        from_above = vectors[y, :, rows:] - taken
        above[y - 1] = from_above

    incoming = into[chip]
    from_above = above[chip]
    middle = vectors[pairs, :, :rows] - dot_parts(two_parts(incoming), low_head, low_tail, 1)
    upper = vectors[pairs + 1] - dot_parts(two_parts(middle), high_head, high_tail, 1)
    taken = dot_parts(two_parts(from_above), high_head[:rows], high_tail[:rows], 0)
    middle_above = upper[:, rows:] - taken
    is_upper = pos_ref[1] == 1
    kept = jnp.concatenate(
        [
            jnp.where(is_upper, from_above, middle_above),
            jnp.where(is_upper, middle, incoming),
            jnp.where(is_upper, upper[:, :rows], middle),
        ],
        axis=1,
    )[:share]
    for piece in range(out_ref.shape[0]):
        out_ref[piece] = kept


def run_chain(position, coupling_all, shares, low, high, below, above, targets):
    share, rows = below.shape
    pairs = coupling_all.shape[0]
    vmem = pl.BlockSpec(memory_space=pltpu.VMEM)
    return pl.pallas_call(
        chain_kernel,
        out_shape=jax.ShapeDtypeStruct((targets, share, 3 * rows), jnp.float32),
        in_specs=[pl.BlockSpec(memory_space=pltpu.SMEM), pl.BlockSpec(memory_space=pltpu.HBM)]
        + [vmem] * 5,
        out_specs=vmem,
        scratch_shapes=[
            pltpu.VMEM((pairs, 2 * rows, rows), jnp.float32),
            pltpu.VMEM((pairs, rows, rows), jnp.bfloat16),
            pltpu.VMEM((pairs, rows, rows), jnp.bfloat16),
            pltpu.VMEM((pairs + 2, padded, 2 * rows), jnp.float32),
            pltpu.VMEM((pairs, padded, rows), jnp.float32),
            pltpu.VMEM((pairs, padded, rows), jnp.float32),
            pltpu.SemaphoreType.DMA((pairs,)),
        ],
        compiler_params=pltpu.CompilerParams(vmem_limit_bytes=(56 * 1024 + 640) * 1024),
        cost_estimate=pl.CostEstimate(
            flops=12 * pairs * 16 * rows * rows,
            bytes_accessed=8 * pairs * rows * rows,
            transcendentals=0,
        ),
        name="chain",
    )(position, coupling_all, shares, low, high, below, above)


def on_device(right_side, inverse_blocks, panels, receive_rows, below_update, above_solution):
    rhs = right_side.shape[0]
    block = inverse_blocks.shape[0]
    rows = panels.shape[0]
    front_count = lax.axis_size("front")
    front_pos = lax.axis_index("front")
    leaf_pos = lax.axis_index("leaf")
    leaf_count = lax.axis_size("leaf")
    is_upper = leaf_pos % 2 == 1
    share = rhs // front_count
    targets = receive_rows[0]

    chunk = rhs // x_chips
    slice_rows = 2 * rows // front_count
    picked = jnp.take(inverse_blocks, targets, axis=1)
    stacked = jnp.concatenate([panels, picked.T], axis=0)
    own_coupling = product(stacked, picked).reshape(front_count, slice_rows, rows)
    own_chunks = jnp.tile(right_side.reshape(x_chips, chunk, block), (front_count // x_chips, 1, 1))
    arrived = exchange(jnp.concatenate([own_coupling, own_chunks], axis=2))
    coupling = jnp.sum(arrived[:, :, :rows], axis=0)
    side_chunk = arrived[:, :, rows:]
    coupling = gather_front(coupling).reshape(2 * rows, rows)

    swap = [(s, s ^ 1) for s in range(leaf_count)]
    mate = lax.ppermute(coupling, "leaf", swap)
    low = jnp.where(is_upper, mate, coupling)
    high = jnp.where(is_upper, coupling, mate)
    c_low, c_high, g_high = (low[:rows], high[:rows], high[rows:])
    lifted = product(g_high, c_low)
    c_pair = -product(c_high, c_low)
    g_pair = low[rows:] + product(c_low.T, lifted)
    pair_half = jnp.where(is_upper, g_pair, c_pair)
    pair_half, side_chunk = lax.optimization_barrier((pair_half, side_chunk))
    coupling_all = gather_leaf(pair_half).reshape(leaf_count // 2, 2 * rows, rows)

    local_forward, vectors = run_forward(
        gather_along_x(side_chunk), inverse_blocks, stacked, front_count
    )
    vectors = jnp.sum(exchange(vectors), axis=0)
    u_own, w_own = (vectors[:, :rows], vectors[:, rows:])
    u_moved = -product_nt(u_own, c_high)
    w_moved = product(jnp.where(is_upper, w_own, u_own), jnp.where(is_upper, -c_low, lifted))
    own_share = jnp.concatenate(
        [
            jnp.where(is_upper, u_own, u_moved),
            jnp.where(is_upper, w_moved, w_own + w_moved),
            vectors,
        ],
        axis=1,
    )
    shares = gather_leaf_small(own_share)

    below_rows = lax.dynamic_slice_in_dim(below_update, front_pos * share, share, 0)
    above_rows = lax.dynamic_slice_in_dim(above_solution, front_pos * share, share, 0)
    position = jnp.stack([leaf_pos // 2, leaf_pos % 2])
    result = exchange(
        run_chain(
            position, coupling_all, shares, low, high,
            below_rows, above_rows, front_count,
        )
    )
    spread = run_spread(result, local_forward, stacked, inverse_blocks)
    solution = jnp.sum(exchange(spread), axis=0)
    update_share = rows // front_count
    updates = result[:, :, 2 * rows :].reshape(rhs, rows)
    sent_updates = lax.dynamic_slice_in_dim(updates, front_pos * update_share, update_share, 1)
    return (solution, sent_updates)


def solution(mesh):
    in_specs = (
        P(None, ("leaf", "front")),
        P(("leaf", "front"), None),
        P("leaf", "front"),
        P("leaf", None),
        P(),
        P(),
    )
    out_specs = (P(None, ("leaf", "front")), P(None, ("leaf", "front")))
    return jax.shard_map(
        on_device, mesh=mesh, in_specs=in_specs, out_specs=out_specs, check_vma=False
    )
```

```python
import jax
import jax.numpy as jnp
from jax import lax
from jax.experimental import pallas as pl
from jax.experimental.pallas import tpu as pltpu
from jax.sharding import PartitionSpec as P

exact = lax.Precision.HIGHEST
x_chips = 4
padded = 8
forward_weight = 1000


def product(left, right):
    return jnp.dot(left, right, precision=exact, preferred_element_type=jnp.float32)


def product_nt(left, right):
    return lax.dot_general(
        left, right, (((1,), (1,)), ((), ())), precision=exact, preferred_element_type=jnp.float32
    )


def exchange(blocks, axis="front", groups=None):
    return lax.all_to_all(blocks, axis, 0, 0, tiled=True, axis_index_groups=groups)


def copies(block, count):
    return jnp.broadcast_to(block[None], (count, *block.shape))


def gather_front(block):
    return exchange(copies(block, lax.axis_size("front")))


def gather_leaf(block):
    return lax.all_gather(block, "leaf", axis=0)


def gather_leaf_small(block):
    return exchange(copies(block, lax.axis_size("leaf")), "leaf")


def gather_along_x(block):
    count = lax.axis_size("front")
    groups = [list(range(first, first + x_chips)) for first in range(0, count, x_chips)]
    return exchange(copies(block, x_chips), "front", groups)


def split(value):
    head = value.astype(jnp.bfloat16)
    return head, (value - head.astype(jnp.float32)).astype(jnp.bfloat16)


def two_parts(value):
    head, tail = split(value)
    return jnp.concatenate([head.astype(jnp.float32), tail.astype(jnp.float32)]).astype(
        jnp.bfloat16
    )


def dot_parts(parts, head, tail, contract):
    dims = (((1,), (contract,)), ((), ()))
    both = lax.dot_general(parts, head, dims, preferred_element_type=jnp.float32)
    both += lax.dot_general(parts, tail, dims, preferred_element_type=jnp.float32)
    return both[:padded] + both[padded:]


def fold(parts, rows, columns):
    small = parts[rows:, columns:] + (parts[rows:, :columns] + parts[:rows, columns:])
    return small + parts[:rows, :columns]


def two_columns(value):
    head, tail = split(value)
    return jnp.concatenate([head, tail], axis=1)


def forward_kernel(side_ref, inverse_ref, stacked_ref, forward_ref, vector_ref):
    chunks, blocks, chunk, block = side_ref.shape
    rhs = chunks * chunk
    group = 4
    nt = (((1,), (1,)), ((), ()))
    total = jnp.zeros((2 * rhs, 2 * block), jnp.float32)
    for first in range(0, blocks, group):
        side = jnp.concatenate(
            [
                jnp.concatenate([side_ref[c, first + j] for j in range(group)], axis=1)
                for c in range(chunks)
            ]
        )
        weights = two_parts(inverse_ref[:, first * block : (first + group) * block])
        total += lax.dot_general(
            two_parts(side), weights, nt, preferred_element_type=jnp.float32
        )
    forward = fold(total, rhs, block)
    forward_ref[...] = forward
    vectors = lax.dot_general(
        two_parts(forward), two_parts(stacked_ref[...]), nt, preferred_element_type=jnp.float32
    )
    vectors = fold(vectors, rhs, stacked_ref.shape[0])
    share = vector_ref.shape[1]
    for piece in range(vector_ref.shape[0]):
        vector_ref[piece] = vectors[piece * share : (piece + 1) * share]


def run_forward(side, inverse_blocks, stacked, targets):
    rhs = side.shape[0] * side.shape[2]
    block = inverse_blocks.shape[0]
    vmem = pl.BlockSpec(memory_space=pltpu.VMEM)
    return pl.pallas_call(
        forward_kernel,
        out_shape=(
            jax.ShapeDtypeStruct((rhs, block), jnp.float32),
            jax.ShapeDtypeStruct((targets, rhs // targets, stacked.shape[0]), jnp.float32),
        ),
        in_specs=[vmem] * 3,
        out_specs=(vmem, vmem),
        compiler_params=pltpu.CompilerParams(vmem_limit_bytes=16 * 1024 * 1024),
        cost_estimate=pl.CostEstimate(
            flops=8 * rhs * block * inverse_blocks.shape[1] * forward_weight,
            bytes_accessed=4 * inverse_blocks.size + 4 * side.size,
            transcendentals=0,
        ),
        name="forward",
    )(side, inverse_blocks, stacked)


def spread_kernel(result_ref, forward_ref, stacked_ref, inverse_ref, out_ref, held):
    share = result_ref.shape[1]
    rhs, block = forward_ref.shape
    for piece in range(result_ref.shape[0]):
        held[piece * share : (piece + 1) * share, :] = result_ref[piece, :, : held.shape[1]]
    taken = jnp.dot(
        two_parts(held[...]), two_columns(stacked_ref[...]), preferred_element_type=jnp.float32
    )
    reduced = two_parts(forward_ref[...] - fold(taken, rhs, block))
    group = 2
    for first in range(0, out_ref.shape[0], group):
        weights = two_columns(inverse_ref[:, first * block : (first + group) * block])
        parts = jnp.dot(reduced, weights, preferred_element_type=jnp.float32)
        parts = fold(parts, rhs, group * block)
        for j in range(group):
            out_ref[first + j] = parts[:, j * block : (j + 1) * block]


def run_spread(result, forward, stacked, inverse_blocks):
    rhs, block = forward.shape
    vmem = pl.BlockSpec(memory_space=pltpu.VMEM)
    return pl.pallas_call(
        spread_kernel,
        out_shape=jax.ShapeDtypeStruct((inverse_blocks.shape[1] // block, rhs, block), jnp.float32),
        in_specs=[vmem] * 4,
        out_specs=vmem,
        scratch_shapes=[pltpu.VMEM((rhs, stacked.shape[0]), jnp.float32)],
        compiler_params=pltpu.CompilerParams(vmem_limit_bytes=16 * 1024 * 1024),
        cost_estimate=pl.CostEstimate(
            flops=8 * rhs * block * inverse_blocks.shape[1],
            bytes_accessed=4 * inverse_blocks.size + 4 * rhs * inverse_blocks.shape[1],
            transcendentals=0,
        ),
        name="spread",
    )(result, forward, stacked, inverse_blocks)


def chain_kernel(
    pos_ref, coupling_ref, share_ref, low_ref, high_ref, below_ref, above_ref, out_ref,
    held, head, tail, vectors, into, above, sems,
):
    pairs = held.shape[0]
    share, rows = below_ref.shape

    def fetch(y):
        return pltpu.make_async_copy(coupling_ref.at[y], held.at[y], sems.at[y])

    for y in range(pairs):
        fetch(y).start()
    vectors[...] = jnp.zeros_like(vectors)
    into[0] = jnp.zeros_like(into[0])
    above[pairs - 1] = jnp.zeros_like(into[0])
    for y in range(pairs):
        both = share_ref[2 * y] + share_ref[2 * y + 1]
        vectors[y, :share, :] = both[:, : 2 * rows]
    chip = pos_ref[0]
    vectors[pairs, :share, :] = share_ref[2 * chip][:, 2 * rows :]
    vectors[pairs + 1, :share, :] = share_ref[2 * chip + 1][:, 2 * rows :]
    into[0, :share, :] = below_ref[...]
    above[pairs - 1, :share, :] = above_ref[...]

    low_head, low_tail = split(low_ref[:rows])
    high_head, high_tail = split(high_ref[...])
    incoming = into[0]
    for y in range(pairs):
        fetch(y).wait()
        block_head, block_tail = split(held[y])
        head[y] = block_head[:rows]
        tail[y] = block_tail[:rows]
        result = vectors[y] - dot_parts(two_parts(incoming), block_head, block_tail, 1)
        incoming = result[:, :rows]
        if y + 1 < pairs:
            into[y + 1] = incoming
        vectors[y] = result
    from_above = above[pairs - 1]
    for y in range(pairs - 1, 0, -1):
        taken = dot_parts(two_parts(from_above), head[y], tail[y], 0)
        from_above = vectors[y, :, rows:] - taken
        above[y - 1] = from_above

    incoming = into[chip]
    from_above = above[chip]
    middle = vectors[pairs, :, :rows] - dot_parts(two_parts(incoming), low_head, low_tail, 1)
    upper = vectors[pairs + 1] - dot_parts(two_parts(middle), high_head, high_tail, 1)
    taken = dot_parts(two_parts(from_above), high_head[:rows], high_tail[:rows], 0)
    middle_above = upper[:, rows:] - taken
    is_upper = pos_ref[1] == 1
    kept = jnp.concatenate(
        [
            jnp.where(is_upper, from_above, middle_above),
            jnp.where(is_upper, middle, incoming),
            jnp.where(is_upper, upper[:, :rows], middle),
        ],
        axis=1,
    )[:share]
    for piece in range(out_ref.shape[0]):
        out_ref[piece] = kept


def run_chain(position, coupling_all, shares, low, high, below, above, targets):
    share, rows = below.shape
    pairs = coupling_all.shape[0]
    vmem = pl.BlockSpec(memory_space=pltpu.VMEM)
    return pl.pallas_call(
        chain_kernel,
        out_shape=jax.ShapeDtypeStruct((targets, share, 3 * rows), jnp.float32),
        in_specs=[pl.BlockSpec(memory_space=pltpu.SMEM), pl.BlockSpec(memory_space=pltpu.HBM)]
        + [vmem] * 5,
        out_specs=vmem,
        scratch_shapes=[
            pltpu.VMEM((pairs, 2 * rows, rows), jnp.float32),
            pltpu.VMEM((pairs, rows, rows), jnp.bfloat16),
            pltpu.VMEM((pairs, rows, rows), jnp.bfloat16),
            pltpu.VMEM((pairs + 2, padded, 2 * rows), jnp.float32),
            pltpu.VMEM((pairs, padded, rows), jnp.float32),
            pltpu.VMEM((pairs, padded, rows), jnp.float32),
            pltpu.SemaphoreType.DMA((pairs,)),
        ],
        compiler_params=pltpu.CompilerParams(vmem_limit_bytes=(56 * 1024 + 640) * 1024),
        cost_estimate=pl.CostEstimate(
            flops=12 * pairs * 16 * rows * rows,
            bytes_accessed=8 * pairs * rows * rows,
            transcendentals=0,
        ),
        name="chain",
    )(position, coupling_all, shares, low, high, below, above)


def on_device(right_side, inverse_blocks, panels, receive_rows, below_update, above_solution):
    rhs = right_side.shape[0]
    block = inverse_blocks.shape[0]
    rows = panels.shape[0]
    front_count = lax.axis_size("front")
    front_pos = lax.axis_index("front")
    leaf_pos = lax.axis_index("leaf")
    leaf_count = lax.axis_size("leaf")
    is_upper = leaf_pos % 2 == 1
    share = rhs // front_count
    targets = receive_rows[0]

    chunk = rhs // x_chips
    slice_rows = 2 * rows // front_count
    picked = jnp.take(inverse_blocks, targets, axis=1)
    stacked = jnp.concatenate([panels, picked.T], axis=0)
    own_coupling = product(stacked, picked).reshape(front_count, slice_rows, rows)
    own_chunks = jnp.tile(right_side.reshape(x_chips, chunk, block), (front_count // x_chips, 1, 1))
    arrived = exchange(jnp.concatenate([own_coupling, own_chunks], axis=2))
    coupling = jnp.sum(arrived[:, :, :rows], axis=0)
    side_chunk = arrived[:, :, rows:]
    coupling = gather_front(coupling).reshape(2 * rows, rows)
    coupling, side_chunk = lax.optimization_barrier((coupling, side_chunk))
    side = gather_along_x(side_chunk)

    swap = [(s, s ^ 1) for s in range(leaf_count)]
    mate = lax.ppermute(coupling, "leaf", swap)
    low = jnp.where(is_upper, mate, coupling)
    high = jnp.where(is_upper, coupling, mate)
    c_low, c_high, g_high = (low[:rows], high[:rows], high[rows:])
    lifted = product(g_high, c_low)
    c_pair = -product(c_high, c_low)
    g_pair = low[rows:] + product(c_low.T, lifted)
    pair_half = jnp.where(is_upper, g_pair, c_pair)
    coupling_all = gather_leaf(pair_half).reshape(leaf_count // 2, 2 * rows, rows)

    local_forward, vectors = run_forward(side, inverse_blocks, stacked, front_count)
    vectors = jnp.sum(exchange(vectors), axis=0)
    u_own, w_own = (vectors[:, :rows], vectors[:, rows:])
    u_moved = -product_nt(u_own, c_high)
    w_moved = product(jnp.where(is_upper, w_own, u_own), jnp.where(is_upper, -c_low, lifted))
    own_share = jnp.concatenate(
        [
            jnp.where(is_upper, u_own, u_moved),
            jnp.where(is_upper, w_moved, w_own + w_moved),
            vectors,
        ],
        axis=1,
    )
    shares = gather_leaf_small(own_share)

    below_rows = lax.dynamic_slice_in_dim(below_update, front_pos * share, share, 0)
    above_rows = lax.dynamic_slice_in_dim(above_solution, front_pos * share, share, 0)
    position = jnp.stack([leaf_pos // 2, leaf_pos % 2])
    result = exchange(
        run_chain(
            position, coupling_all, shares, low, high,
            below_rows, above_rows, front_count,
        )
    )
    spread = run_spread(result, local_forward, stacked, inverse_blocks)
    solution = jnp.sum(exchange(spread), axis=0)
    update_share = rows // front_count
    updates = result[:, :, 2 * rows :].reshape(rhs, rows)
    sent_updates = lax.dynamic_slice_in_dim(updates, front_pos * update_share, update_share, 1)
    return (solution, sent_updates)


def solution(mesh):
    in_specs = (
        P(None, ("leaf", "front")),
        P(("leaf", "front"), None),
        P("leaf", "front"),
        P("leaf", None),
        P(),
        P(),
    )
    out_specs = (P(None, ("leaf", "front")), P(None, ("leaf", "front")))
    return jax.shard_map(
        on_device, mesh=mesh, in_specs=in_specs, out_specs=out_specs, check_vma=False
    )
```

```python
import jax
import jax.numpy as jnp
from jax import lax
from jax.experimental import pallas as pl
from jax.experimental.pallas import tpu as pltpu
from jax.sharding import PartitionSpec as P

exact = lax.Precision.HIGHEST
x_chips = 4
padded = 8
forward_weight = 1000


def product(left, right):
    return jnp.dot(left, right, precision=exact, preferred_element_type=jnp.float32)


def product_nt(left, right):
    return lax.dot_general(
        left, right, (((1,), (1,)), ((), ())), precision=exact, preferred_element_type=jnp.float32
    )


def exchange(blocks, axis="front", groups=None):
    return lax.all_to_all(blocks, axis, 0, 0, tiled=True, axis_index_groups=groups)


def copies(block, count):
    return jnp.broadcast_to(block[None], (count, *block.shape))


def gather_front(block):
    return exchange(copies(block, lax.axis_size("front")))


def gather_leaf(block):
    return lax.all_gather(block, "leaf", axis=0)


def gather_along_x(block):
    count = lax.axis_size("front")
    groups = [list(range(first, first + x_chips)) for first in range(0, count, x_chips)]
    return exchange(copies(block, x_chips), "front", groups)


def split(value):
    head = value.astype(jnp.bfloat16)
    return head, (value - head.astype(jnp.float32)).astype(jnp.bfloat16)


def two_parts(value):
    head, tail = split(value)
    return jnp.concatenate([head.astype(jnp.float32), tail.astype(jnp.float32)]).astype(
        jnp.bfloat16
    )


def dot_parts(parts, head, tail, contract):
    dims = (((1,), (contract,)), ((), ()))
    both = lax.dot_general(parts, head, dims, preferred_element_type=jnp.float32)
    both += lax.dot_general(parts, tail, dims, preferred_element_type=jnp.float32)
    return both[:padded] + both[padded:]


def fold(parts, rows, columns):
    small = parts[rows:, columns:] + (parts[rows:, :columns] + parts[:rows, columns:])
    return small + parts[:rows, :columns]


def two_columns(value):
    head, tail = split(value)
    return jnp.concatenate([head, tail], axis=1)


def forward_kernel(side_ref, inverse_ref, stacked_ref, forward_ref, vector_ref):
    chunks, blocks, chunk, block = side_ref.shape
    rhs = chunks * chunk
    group = 4
    nt = (((1,), (1,)), ((), ()))
    total = jnp.zeros((2 * rhs, 2 * block), jnp.float32)
    for first in range(0, blocks, group):
        side = jnp.concatenate(
            [
                jnp.concatenate([side_ref[c, first + j] for j in range(group)], axis=1)
                for c in range(chunks)
            ]
        )
        weights = two_parts(inverse_ref[:, first * block : (first + group) * block])
        total += lax.dot_general(
            two_parts(side), weights, nt, preferred_element_type=jnp.float32
        )
    forward = fold(total, rhs, block)
    forward_ref[...] = forward
    vectors = lax.dot_general(
        two_parts(forward), two_parts(stacked_ref[...]), nt, preferred_element_type=jnp.float32
    )
    vectors = fold(vectors, rhs, stacked_ref.shape[0])
    share = vector_ref.shape[1]
    for piece in range(vector_ref.shape[0]):
        vector_ref[piece] = vectors[piece * share : (piece + 1) * share]


def run_forward(side, inverse_blocks, stacked, targets):
    rhs = side.shape[0] * side.shape[2]
    block = inverse_blocks.shape[0]
    vmem = pl.BlockSpec(memory_space=pltpu.VMEM)
    return pl.pallas_call(
        forward_kernel,
        out_shape=(
            jax.ShapeDtypeStruct((rhs, block), jnp.float32),
            jax.ShapeDtypeStruct((targets, rhs // targets, stacked.shape[0]), jnp.float32),
        ),
        in_specs=[vmem] * 3,
        out_specs=(vmem, vmem),
        compiler_params=pltpu.CompilerParams(vmem_limit_bytes=16 * 1024 * 1024),
        cost_estimate=pl.CostEstimate(
            flops=8 * rhs * block * inverse_blocks.shape[1] * forward_weight,
            bytes_accessed=4 * inverse_blocks.size + 4 * side.size,
            transcendentals=0,
        ),
        name="forward",
    )(side, inverse_blocks, stacked)


def spread_kernel(result_ref, forward_ref, stacked_ref, inverse_ref, out_ref, held):
    share = result_ref.shape[1]
    rhs, block = forward_ref.shape
    for piece in range(result_ref.shape[0]):
        held[piece * share : (piece + 1) * share, :] = result_ref[piece, :, : held.shape[1]]
    taken = jnp.dot(
        two_parts(held[...]), two_columns(stacked_ref[...]), preferred_element_type=jnp.float32
    )
    reduced = two_parts(forward_ref[...] - fold(taken, rhs, block))
    group = 2
    for first in range(0, out_ref.shape[0], group):
        weights = two_columns(inverse_ref[:, first * block : (first + group) * block])
        parts = jnp.dot(reduced, weights, preferred_element_type=jnp.float32)
        parts = fold(parts, rhs, group * block)
        for j in range(group):
            out_ref[first + j] = parts[:, j * block : (j + 1) * block]


def run_spread(result, forward, stacked, inverse_blocks):
    rhs, block = forward.shape
    vmem = pl.BlockSpec(memory_space=pltpu.VMEM)
    return pl.pallas_call(
        spread_kernel,
        out_shape=jax.ShapeDtypeStruct((inverse_blocks.shape[1] // block, rhs, block), jnp.float32),
        in_specs=[vmem] * 4,
        out_specs=vmem,
        scratch_shapes=[pltpu.VMEM((rhs, stacked.shape[0]), jnp.float32)],
        compiler_params=pltpu.CompilerParams(vmem_limit_bytes=16 * 1024 * 1024),
        cost_estimate=pl.CostEstimate(
            flops=8 * rhs * block * inverse_blocks.shape[1],
            bytes_accessed=4 * inverse_blocks.size + 4 * rhs * inverse_blocks.shape[1],
            transcendentals=0,
        ),
        name="spread",
    )(result, forward, stacked, inverse_blocks)


def share_kernel(pos_ref, arrived_ref, high_ref, moved_ref, out_ref, held):
    share, width = arrived_ref.shape[1:]
    rows = width // 2
    held[...] = jnp.zeros_like(held)
    held[:share, :] = jnp.sum(arrived_ref[...], axis=0)
    vectors = held[...]
    own_u, own_w = vectors[:, :rows], vectors[:, rows:]
    is_upper = pos_ref[1] == 1
    u_moved = -dot_parts(two_parts(own_u), *split(high_ref[...]), 1)
    turned = two_parts(jnp.where(is_upper, own_w, own_u))
    w_moved = dot_parts(turned, *split(moved_ref[...]), 0)
    kept = jnp.concatenate(
        [
            jnp.where(is_upper, own_u, u_moved),
            jnp.where(is_upper, w_moved, own_w + w_moved),
            vectors,
        ],
        axis=1,
    )[:share]
    for piece in range(out_ref.shape[0]):
        out_ref[piece] = kept


def run_share(position, arrived, c_high, moved, targets):
    share, width = arrived.shape[1:]
    vmem = pl.BlockSpec(memory_space=pltpu.VMEM)
    return pl.pallas_call(
        share_kernel,
        out_shape=jax.ShapeDtypeStruct((targets, share, 2 * width), jnp.float32),
        in_specs=[pl.BlockSpec(memory_space=pltpu.SMEM)] + [vmem] * 3,
        out_specs=vmem,
        scratch_shapes=[pltpu.VMEM((padded, width), jnp.float32)],
        compiler_params=pltpu.CompilerParams(vmem_limit_bytes=16 * 1024 * 1024),
        cost_estimate=pl.CostEstimate(
            flops=128 * width * width, bytes_accessed=8 * width * width, transcendentals=0
        ),
        name="share",
    )(position, arrived, c_high, moved)


def chain_kernel(
    pos_ref, coupling_ref, share_ref, low_ref, high_ref, below_ref, above_ref, out_ref,
    held, own, head, tail, vectors, into, above, sems,
):
    pairs = held.shape[0]
    share, rows = below_ref.shape

    def fetch(y):
        return pltpu.make_async_copy(coupling_ref.at[y], held.at[y], sems.at[y])

    for y in range(pairs):
        fetch(y).start()
    own_low = pltpu.make_async_copy(low_ref, own.at[0], sems.at[pairs])
    own_high = pltpu.make_async_copy(high_ref, own.at[1], sems.at[pairs + 1])
    own_low.start()
    own_high.start()
    vectors[...] = jnp.zeros_like(vectors)
    into[0] = jnp.zeros_like(into[0])
    above[pairs - 1] = jnp.zeros_like(into[0])
    for y in range(pairs):
        both = share_ref[2 * y] + share_ref[2 * y + 1]
        vectors[y, :share, :] = both[:, : 2 * rows]
    chip = pos_ref[0]
    vectors[pairs, :share, :] = share_ref[2 * chip][:, 2 * rows :]
    vectors[pairs + 1, :share, :] = share_ref[2 * chip + 1][:, 2 * rows :]
    into[0, :share, :] = below_ref[...]
    above[pairs - 1, :share, :] = above_ref[...]

    incoming = into[0]
    for y in range(pairs):
        fetch(y).wait()
        block_head, block_tail = split(held[y])
        head[y] = block_head[:rows]
        tail[y] = block_tail[:rows]
        result = vectors[y] - dot_parts(two_parts(incoming), block_head, block_tail, 1)
        incoming = result[:, :rows]
        if y + 1 < pairs:
            into[y + 1] = incoming
        vectors[y] = result
    from_above = above[pairs - 1]
    for y in range(pairs - 1, 0, -1):
        taken = dot_parts(two_parts(from_above), head[y], tail[y], 0)
        from_above = vectors[y, :, rows:] - taken
        above[y - 1] = from_above

    own_low.wait()
    own_high.wait()
    low_head, low_tail = split(own[0, :rows])
    high_head, high_tail = split(own[1])
    incoming = into[chip]
    from_above = above[chip]
    middle = vectors[pairs, :, :rows] - dot_parts(two_parts(incoming), low_head, low_tail, 1)
    upper = vectors[pairs + 1] - dot_parts(two_parts(middle), high_head, high_tail, 1)
    taken = dot_parts(two_parts(from_above), high_head[:rows], high_tail[:rows], 0)
    middle_above = upper[:, rows:] - taken
    is_upper = pos_ref[1] == 1
    kept = jnp.concatenate(
        [
            jnp.where(is_upper, from_above, middle_above),
            jnp.where(is_upper, middle, incoming),
            jnp.where(is_upper, upper[:, :rows], middle),
        ],
        axis=1,
    )[:share]
    for piece in range(out_ref.shape[0]):
        out_ref[piece] = kept


def run_chain(position, coupling_all, shares, low, high, below, above, targets):
    share, rows = below.shape
    pairs = coupling_all.shape[0]
    vmem = pl.BlockSpec(memory_space=pltpu.VMEM)
    hbm = pl.BlockSpec(memory_space=pltpu.HBM)
    return pl.pallas_call(
        chain_kernel,
        out_shape=jax.ShapeDtypeStruct((targets, share, 3 * rows), jnp.float32),
        in_specs=[pl.BlockSpec(memory_space=pltpu.SMEM), hbm, vmem, hbm, hbm, vmem, vmem],
        out_specs=vmem,
        scratch_shapes=[
            pltpu.VMEM((pairs, 2 * rows, rows), jnp.float32),
            pltpu.VMEM((2, 2 * rows, rows), jnp.float32),
            pltpu.VMEM((pairs, rows, rows), jnp.bfloat16),
            pltpu.VMEM((pairs, rows, rows), jnp.bfloat16),
            pltpu.VMEM((pairs + 2, padded, 2 * rows), jnp.float32),
            pltpu.VMEM((pairs, padded, rows), jnp.float32),
            pltpu.VMEM((pairs, padded, rows), jnp.float32),
            pltpu.SemaphoreType.DMA((pairs + 2,)),
        ],
        compiler_params=pltpu.CompilerParams(vmem_limit_bytes=(56 * 1024 + 640) * 1024),
        cost_estimate=pl.CostEstimate(
            flops=12 * pairs * 16 * rows * rows,
            bytes_accessed=8 * pairs * rows * rows,
            transcendentals=0,
        ),
        name="chain",
    )(position, coupling_all, shares, low, high, below, above)


def on_device(right_side, inverse_blocks, panels, receive_rows, below_update, above_solution):
    rhs = right_side.shape[0]
    block = inverse_blocks.shape[0]
    rows = panels.shape[0]
    front_count = lax.axis_size("front")
    front_pos = lax.axis_index("front")
    leaf_pos = lax.axis_index("leaf")
    leaf_count = lax.axis_size("leaf")
    is_upper = leaf_pos % 2 == 1
    share = rhs // front_count
    targets = receive_rows[0]

    chunk = rhs // x_chips
    slice_rows = 2 * rows // front_count
    picked = jnp.take(inverse_blocks, targets, axis=1)
    stacked = jnp.concatenate([panels, picked.T], axis=0)
    own_coupling = product(stacked, picked).reshape(front_count, slice_rows, rows)
    own_chunks = jnp.tile(right_side.reshape(x_chips, chunk, block), (front_count // x_chips, 1, 1))
    arrived = exchange(jnp.concatenate([own_coupling, own_chunks], axis=2))
    coupling = jnp.sum(arrived[:, :, :rows], axis=0)
    side_chunk = arrived[:, :, rows:]
    coupling = gather_front(coupling).reshape(2 * rows, rows)
    coupling, side_chunk = lax.optimization_barrier((coupling, side_chunk))
    side = gather_along_x(side_chunk)

    swap = [(s, s ^ 1) for s in range(leaf_count)]
    mate = lax.ppermute(coupling, "leaf", swap)
    low = jnp.where(is_upper, mate, coupling)
    high = jnp.where(is_upper, coupling, mate)
    c_low, c_high, g_high = (low[:rows], high[:rows], high[rows:])
    lifted = product(g_high, c_low)
    c_pair = -product(c_high, c_low)
    g_pair = low[rows:] + product(c_low.T, lifted)
    pair_half = jnp.where(is_upper, g_pair, c_pair)
    coupling_all = gather_leaf(pair_half).reshape(leaf_count // 2, 2 * rows, rows)

    local_forward, vectors = run_forward(side, inverse_blocks, stacked, front_count)
    position = jnp.stack([leaf_pos // 2, leaf_pos % 2])
    moved = jnp.where(is_upper, -c_low, lifted)
    shares = exchange(run_share(position, exchange(vectors), c_high, moved, leaf_count), "leaf")

    below_rows = lax.dynamic_slice_in_dim(below_update, front_pos * share, share, 0)
    above_rows = lax.dynamic_slice_in_dim(above_solution, front_pos * share, share, 0)
    result = exchange(
        run_chain(
            position, coupling_all, shares, low, high,
            below_rows, above_rows, front_count,
        )
    )
    spread = run_spread(result, local_forward, stacked, inverse_blocks)
    solution = jnp.sum(exchange(spread), axis=0)
    update_share = rows // front_count
    updates = result[:, :, 2 * rows :].reshape(rhs, rows)
    sent_updates = lax.dynamic_slice_in_dim(updates, front_pos * update_share, update_share, 1)
    return (solution, sent_updates)


def solution(mesh):
    in_specs = (
        P(None, ("leaf", "front")),
        P(("leaf", "front"), None),
        P("leaf", "front"),
        P("leaf", None),
        P(),
        P(),
    )
    out_specs = (P(None, ("leaf", "front")), P(None, ("leaf", "front")))
    return jax.shard_map(
        on_device, mesh=mesh, in_specs=in_specs, out_specs=out_specs, check_vma=False
    )
```

```python
import jax
import jax.numpy as jnp
from jax import lax
from jax.experimental import pallas as pl
from jax.experimental.pallas import tpu as pltpu
from jax.sharding import PartitionSpec as P

exact = lax.Precision.HIGHEST
x_chips = 4
padded = 8
forward_weight = 1000


def product(left, right):
    return jnp.dot(left, right, precision=exact, preferred_element_type=jnp.float32)


def product_nt(left, right):
    return lax.dot_general(
        left, right, (((1,), (1,)), ((), ())), precision=exact, preferred_element_type=jnp.float32
    )


def exchange(blocks, axis="front", groups=None):
    return lax.all_to_all(blocks, axis, 0, 0, tiled=True, axis_index_groups=groups)


def copies(block, count):
    return jnp.broadcast_to(block[None], (count, *block.shape))


def gather_front(block):
    return exchange(copies(block, lax.axis_size("front")))


def gather_leaf(block):
    return lax.all_gather(block, "leaf", axis=0)


def turn_along_x(block, steps):
    count = lax.axis_size("front")
    pairs = [(f, f - f % x_chips + (f + steps) % x_chips) for f in range(count)]
    return lax.ppermute(block, "front", pairs)


def split(value):
    head = value.astype(jnp.bfloat16)
    return head, (value - head.astype(jnp.float32)).astype(jnp.bfloat16)


def two_parts(value):
    head, tail = split(value)
    return jnp.concatenate([head.astype(jnp.float32), tail.astype(jnp.float32)]).astype(
        jnp.bfloat16
    )


def dot_parts(parts, head, tail, contract):
    dims = (((1,), (contract,)), ((), ()))
    both = lax.dot_general(parts, head, dims, preferred_element_type=jnp.float32)
    both += lax.dot_general(parts, tail, dims, preferred_element_type=jnp.float32)
    return both[:padded] + both[padded:]


def fold(parts, rows, columns):
    small = parts[rows:, columns:] + (parts[rows:, :columns] + parts[:rows, columns:])
    return small + parts[:rows, :columns]


def two_columns(value):
    head, tail = split(value)
    return jnp.concatenate([head, tail], axis=1)


def forward_kernel(pos_ref, inverse_ref, stacked_ref, *refs):
    pieces, (forward_ref, vector_ref, side_ref) = refs[:-3], refs[-3:]
    chunks, blocks, chunk, block = side_ref.shape
    for steps, piece in enumerate(pieces):
        side_ref[lax.rem(pos_ref[0] + chunks - steps, chunks)] = piece[...]
    rhs = chunks * chunk
    group = 4
    nt = (((1,), (1,)), ((), ()))
    total = jnp.zeros((2 * rhs, 2 * block), jnp.float32)
    for first in range(0, blocks, group):
        side = jnp.concatenate(
            [
                jnp.concatenate([side_ref[c, first + j] for j in range(group)], axis=1)
                for c in range(chunks)
            ]
        )
        weights = two_parts(inverse_ref[:, first * block : (first + group) * block])
        total += lax.dot_general(
            two_parts(side), weights, nt, preferred_element_type=jnp.float32
        )
    forward = fold(total, rhs, block)
    forward_ref[...] = forward
    vectors = lax.dot_general(
        two_parts(forward), two_parts(stacked_ref[...]), nt, preferred_element_type=jnp.float32
    )
    vectors = fold(vectors, rhs, stacked_ref.shape[0])
    share = vector_ref.shape[1]
    for piece in range(vector_ref.shape[0]):
        vector_ref[piece] = vectors[piece * share : (piece + 1) * share]


def run_forward(x_pos, pieces, inverse_blocks, stacked, targets):
    side_shape = (len(pieces), *pieces[0].shape)
    rhs = side_shape[0] * side_shape[2]
    block = inverse_blocks.shape[0]
    vmem = pl.BlockSpec(memory_space=pltpu.VMEM)
    return pl.pallas_call(
        forward_kernel,
        out_shape=(
            jax.ShapeDtypeStruct((rhs, block), jnp.float32),
            jax.ShapeDtypeStruct((targets, rhs // targets, stacked.shape[0]), jnp.float32),
        ),
        in_specs=[pl.BlockSpec(memory_space=pltpu.SMEM)] + [vmem] * (2 + len(pieces)),
        out_specs=(vmem, vmem),
        scratch_shapes=[pltpu.VMEM(side_shape, jnp.float32)],
        compiler_params=pltpu.CompilerParams(vmem_limit_bytes=16 * 1024 * 1024),
        cost_estimate=pl.CostEstimate(
            flops=8 * rhs * block * inverse_blocks.shape[1] * forward_weight,
            bytes_accessed=4 * inverse_blocks.size + 16 * pieces[0].size,
            transcendentals=0,
        ),
        name="forward",
    )(x_pos.reshape(1), inverse_blocks, stacked, *pieces)


def spread_kernel(result_ref, forward_ref, stacked_ref, inverse_ref, out_ref, held):
    share = result_ref.shape[1]
    rhs, block = forward_ref.shape
    for piece in range(result_ref.shape[0]):
        held[piece * share : (piece + 1) * share, :] = result_ref[piece, :, : held.shape[1]]
    taken = jnp.dot(
        two_parts(held[...]), two_columns(stacked_ref[...]), preferred_element_type=jnp.float32
    )
    reduced = two_parts(forward_ref[...] - fold(taken, rhs, block))
    group = 2
    for first in range(0, out_ref.shape[0], group):
        weights = two_columns(inverse_ref[:, first * block : (first + group) * block])
        parts = jnp.dot(reduced, weights, preferred_element_type=jnp.float32)
        parts = fold(parts, rhs, group * block)
        for j in range(group):
            out_ref[first + j] = parts[:, j * block : (j + 1) * block]


def run_spread(result, forward, stacked, inverse_blocks):
    rhs, block = forward.shape
    vmem = pl.BlockSpec(memory_space=pltpu.VMEM)
    return pl.pallas_call(
        spread_kernel,
        out_shape=jax.ShapeDtypeStruct((inverse_blocks.shape[1] // block, rhs, block), jnp.float32),
        in_specs=[vmem] * 4,
        out_specs=vmem,
        scratch_shapes=[pltpu.VMEM((rhs, stacked.shape[0]), jnp.float32)],
        compiler_params=pltpu.CompilerParams(vmem_limit_bytes=16 * 1024 * 1024),
        cost_estimate=pl.CostEstimate(
            flops=8 * rhs * block * inverse_blocks.shape[1],
            bytes_accessed=4 * inverse_blocks.size + 4 * rhs * inverse_blocks.shape[1],
            transcendentals=0,
        ),
        name="spread",
    )(result, forward, stacked, inverse_blocks)


def share_kernel(pos_ref, arrived_ref, high_ref, moved_ref, out_ref, held):
    share, width = arrived_ref.shape[1:]
    rows = width // 2
    held[...] = jnp.zeros_like(held)
    held[:share, :] = jnp.sum(arrived_ref[...], axis=0)
    vectors = held[...]
    own_u, own_w = vectors[:, :rows], vectors[:, rows:]
    is_upper = pos_ref[1] == 1
    u_moved = -dot_parts(two_parts(own_u), *split(high_ref[...]), 1)
    turned = two_parts(jnp.where(is_upper, own_w, own_u))
    w_moved = dot_parts(turned, *split(moved_ref[...]), 0)
    kept = jnp.concatenate(
        [
            jnp.where(is_upper, own_u, u_moved),
            jnp.where(is_upper, w_moved, own_w + w_moved),
            vectors,
        ],
        axis=1,
    )[:share]
    for piece in range(out_ref.shape[0]):
        out_ref[piece] = kept


def run_share(position, arrived, c_high, moved, targets):
    share, width = arrived.shape[1:]
    vmem = pl.BlockSpec(memory_space=pltpu.VMEM)
    return pl.pallas_call(
        share_kernel,
        out_shape=jax.ShapeDtypeStruct((targets, share, 2 * width), jnp.float32),
        in_specs=[pl.BlockSpec(memory_space=pltpu.SMEM)] + [vmem] * 3,
        out_specs=vmem,
        scratch_shapes=[pltpu.VMEM((padded, width), jnp.float32)],
        compiler_params=pltpu.CompilerParams(vmem_limit_bytes=16 * 1024 * 1024),
        cost_estimate=pl.CostEstimate(
            flops=128 * width * width, bytes_accessed=8 * width * width, transcendentals=0
        ),
        name="share",
    )(position, arrived, c_high, moved)


def chain_kernel(
    pos_ref, coupling_ref, share_ref, low_ref, high_ref, below_ref, above_ref, out_ref,
    held, own, head, tail, vectors, into, above, sems,
):
    pairs = held.shape[0]
    share, rows = below_ref.shape

    def fetch(y):
        return pltpu.make_async_copy(coupling_ref.at[y], held.at[y], sems.at[y])

    for y in range(pairs):
        fetch(y).start()
    own_low = pltpu.make_async_copy(low_ref, own.at[0], sems.at[pairs])
    own_high = pltpu.make_async_copy(high_ref, own.at[1], sems.at[pairs + 1])
    own_low.start()
    own_high.start()
    vectors[...] = jnp.zeros_like(vectors)
    into[0] = jnp.zeros_like(into[0])
    above[pairs - 1] = jnp.zeros_like(into[0])
    for y in range(pairs):
        both = share_ref[2 * y] + share_ref[2 * y + 1]
        vectors[y, :share, :] = both[:, : 2 * rows]
    chip = pos_ref[0]
    vectors[pairs, :share, :] = share_ref[2 * chip][:, 2 * rows :]
    vectors[pairs + 1, :share, :] = share_ref[2 * chip + 1][:, 2 * rows :]
    into[0, :share, :] = below_ref[...]
    above[pairs - 1, :share, :] = above_ref[...]

    incoming = into[0]
    for y in range(pairs):
        fetch(y).wait()
        block_head, block_tail = split(held[y])
        head[y] = block_head[:rows]
        tail[y] = block_tail[:rows]
        result = vectors[y] - dot_parts(two_parts(incoming), block_head, block_tail, 1)
        incoming = result[:, :rows]
        if y + 1 < pairs:
            into[y + 1] = incoming
        vectors[y] = result
    from_above = above[pairs - 1]
    for y in range(pairs - 1, 0, -1):
        taken = dot_parts(two_parts(from_above), head[y], tail[y], 0)
        from_above = vectors[y, :, rows:] - taken
        above[y - 1] = from_above

    own_low.wait()
    own_high.wait()
    low_head, low_tail = split(own[0, :rows])
    high_head, high_tail = split(own[1])
    incoming = into[chip]
    from_above = above[chip]
    middle = vectors[pairs, :, :rows] - dot_parts(two_parts(incoming), low_head, low_tail, 1)
    upper = vectors[pairs + 1] - dot_parts(two_parts(middle), high_head, high_tail, 1)
    taken = dot_parts(two_parts(from_above), high_head[:rows], high_tail[:rows], 0)
    middle_above = upper[:, rows:] - taken
    is_upper = pos_ref[1] == 1
    kept = jnp.concatenate(
        [
            jnp.where(is_upper, from_above, middle_above),
            jnp.where(is_upper, middle, incoming),
            jnp.where(is_upper, upper[:, :rows], middle),
        ],
        axis=1,
    )[:share]
    for piece in range(out_ref.shape[0]):
        out_ref[piece] = kept


def run_chain(position, coupling_all, shares, low, high, below, above, targets):
    share, rows = below.shape
    pairs = coupling_all.shape[0]
    vmem = pl.BlockSpec(memory_space=pltpu.VMEM)
    hbm = pl.BlockSpec(memory_space=pltpu.HBM)
    return pl.pallas_call(
        chain_kernel,
        out_shape=jax.ShapeDtypeStruct((targets, share, 3 * rows), jnp.float32),
        in_specs=[pl.BlockSpec(memory_space=pltpu.SMEM), hbm, vmem, hbm, hbm, vmem, vmem],
        out_specs=vmem,
        scratch_shapes=[
            pltpu.VMEM((pairs, 2 * rows, rows), jnp.float32),
            pltpu.VMEM((2, 2 * rows, rows), jnp.float32),
            pltpu.VMEM((pairs, rows, rows), jnp.bfloat16),
            pltpu.VMEM((pairs, rows, rows), jnp.bfloat16),
            pltpu.VMEM((pairs + 2, padded, 2 * rows), jnp.float32),
            pltpu.VMEM((pairs, padded, rows), jnp.float32),
            pltpu.VMEM((pairs, padded, rows), jnp.float32),
            pltpu.SemaphoreType.DMA((pairs + 2,)),
        ],
        compiler_params=pltpu.CompilerParams(vmem_limit_bytes=(56 * 1024 + 640) * 1024),
        cost_estimate=pl.CostEstimate(
            flops=12 * pairs * 16 * rows * rows,
            bytes_accessed=8 * pairs * rows * rows,
            transcendentals=0,
        ),
        name="chain",
    )(position, coupling_all, shares, low, high, below, above)


def on_device(right_side, inverse_blocks, panels, receive_rows, below_update, above_solution):
    rhs = right_side.shape[0]
    block = inverse_blocks.shape[0]
    rows = panels.shape[0]
    front_count = lax.axis_size("front")
    front_pos = lax.axis_index("front")
    leaf_pos = lax.axis_index("leaf")
    leaf_count = lax.axis_size("leaf")
    is_upper = leaf_pos % 2 == 1
    share = rhs // front_count
    targets = receive_rows[0]

    chunk = rhs // x_chips
    slice_rows = 2 * rows // front_count
    picked = jnp.take(inverse_blocks, targets, axis=1)
    stacked = jnp.concatenate([panels, picked.T], axis=0)
    own_coupling = product(stacked, picked).reshape(front_count, slice_rows, rows)
    own_chunks = jnp.tile(right_side.reshape(x_chips, chunk, block), (front_count // x_chips, 1, 1))
    arrived = exchange(jnp.concatenate([own_coupling, own_chunks], axis=2))
    coupling = jnp.sum(arrived[:, :, :rows], axis=0)
    side_chunk = arrived[:, :, rows:]
    coupling = gather_front(coupling).reshape(2 * rows, rows)
    turned = [turn_along_x(side_chunk, steps) for steps in range(1, x_chips)]
    coupling, *turned = lax.optimization_barrier((coupling, *turned))

    swap = [(s, s ^ 1) for s in range(leaf_count)]
    mate = lax.ppermute(coupling, "leaf", swap)
    low = jnp.where(is_upper, mate, coupling)
    high = jnp.where(is_upper, coupling, mate)
    c_low, c_high, g_high = (low[:rows], high[:rows], high[rows:])
    lifted = product(g_high, c_low)
    c_pair = -product(c_high, c_low)
    g_pair = low[rows:] + product(c_low.T, lifted)
    pair_half = jnp.where(is_upper, g_pair, c_pair)
    coupling_all = gather_leaf(pair_half).reshape(leaf_count // 2, 2 * rows, rows)

    local_forward, vectors = run_forward(
        front_pos % x_chips, [side_chunk, *turned], inverse_blocks, stacked, front_count
    )
    position = jnp.stack([leaf_pos // 2, leaf_pos % 2])
    moved = jnp.where(is_upper, -c_low, lifted)
    shares = exchange(run_share(position, exchange(vectors), c_high, moved, leaf_count), "leaf")

    below_rows = lax.dynamic_slice_in_dim(below_update, front_pos * share, share, 0)
    above_rows = lax.dynamic_slice_in_dim(above_solution, front_pos * share, share, 0)
    result = exchange(
        run_chain(
            position, coupling_all, shares, low, high,
            below_rows, above_rows, front_count,
        )
    )
    spread = run_spread(result, local_forward, stacked, inverse_blocks)
    solution = jnp.sum(exchange(spread), axis=0)
    update_share = rows // front_count
    updates = result[:, :, 2 * rows :].reshape(rhs, rows)
    sent_updates = lax.dynamic_slice_in_dim(updates, front_pos * update_share, update_share, 1)
    return (solution, sent_updates)


def solution(mesh):
    in_specs = (
        P(None, ("leaf", "front")),
        P(("leaf", "front"), None),
        P("leaf", "front"),
        P("leaf", None),
        P(),
        P(),
    )
    out_specs = (P(None, ("leaf", "front")), P(None, ("leaf", "front")))
    return jax.shard_map(
        on_device, mesh=mesh, in_specs=in_specs, out_specs=out_specs, check_vma=False
    )
```

```python
import jax
import jax.numpy as jnp
from jax import lax
from jax.experimental import pallas as pl
from jax.experimental.pallas import tpu as pltpu
from jax.sharding import PartitionSpec as P

exact = lax.Precision.HIGHEST
x_chips = 4
padded = 8


def product(left, right):
    return jnp.dot(left, right, precision=exact, preferred_element_type=jnp.float32)


def product_nt(left, right):
    return lax.dot_general(
        left, right, (((1,), (1,)), ((), ())), precision=exact, preferred_element_type=jnp.float32
    )


def exchange(blocks, axis="front", groups=None):
    return lax.all_to_all(blocks, axis, 0, 0, tiled=True, axis_index_groups=groups)


def copies(block, count):
    return jnp.broadcast_to(block[None], (count, *block.shape))


def gather_front(block):
    return exchange(copies(block, lax.axis_size("front")))


def gather_leaf(block):
    return lax.all_gather(block, "leaf", axis=0)


def turn_along_x(block, steps):
    count = lax.axis_size("front")
    pairs = [(f, f - f % x_chips + (f + steps) % x_chips) for f in range(count)]
    return lax.ppermute(block, "front", pairs)


def split(value):
    head = value.astype(jnp.bfloat16)
    return head, (value - head.astype(jnp.float32)).astype(jnp.bfloat16)


def two_parts(value):
    head, tail = split(value)
    return jnp.concatenate([head.astype(jnp.float32), tail.astype(jnp.float32)]).astype(
        jnp.bfloat16
    )


def dot_parts(parts, head, tail, contract):
    dims = (((1,), (contract,)), ((), ()))
    both = lax.dot_general(parts, head, dims, preferred_element_type=jnp.float32)
    both += lax.dot_general(parts, tail, dims, preferred_element_type=jnp.float32)
    return both[:padded] + both[padded:]


def fold(parts, rows, columns):
    small = parts[rows:, columns:] + (parts[rows:, :columns] + parts[:rows, columns:])
    return small + parts[:rows, :columns]


def two_columns(value):
    head, tail = split(value)
    return jnp.concatenate([head, tail], axis=1)


def forward_kernel(pos_ref, inverse_ref, stacked_ref, *refs):
    pieces, (forward_ref, vector_ref, side_ref) = refs[:-3], refs[-3:]
    chunks, blocks, chunk, block = side_ref.shape
    for steps, piece in enumerate(pieces):
        side_ref[lax.rem(pos_ref[0] + chunks - steps, chunks)] = piece[...]
    rhs = chunks * chunk
    group = 4
    nt = (((1,), (1,)), ((), ()))
    total = jnp.zeros((2 * rhs, 2 * block), jnp.float32)
    for first in range(0, blocks, group):
        side = jnp.concatenate(
            [
                jnp.concatenate([side_ref[c, first + j] for j in range(group)], axis=1)
                for c in range(chunks)
            ]
        )
        weights = two_parts(inverse_ref[:, first * block : (first + group) * block])
        total += lax.dot_general(
            two_parts(side), weights, nt, preferred_element_type=jnp.float32
        )
    forward = fold(total, rhs, block)
    forward_ref[...] = forward
    vectors = lax.dot_general(
        two_parts(forward), two_parts(stacked_ref[...]), nt, preferred_element_type=jnp.float32
    )
    vectors = fold(vectors, rhs, stacked_ref.shape[0])
    share = vector_ref.shape[1]
    for piece in range(vector_ref.shape[0]):
        vector_ref[piece] = vectors[piece * share : (piece + 1) * share]


def run_forward(x_pos, pieces, inverse_blocks, stacked, targets):
    side_shape = (len(pieces), *pieces[0].shape)
    rhs = side_shape[0] * side_shape[2]
    block = inverse_blocks.shape[0]
    vmem = pl.BlockSpec(memory_space=pltpu.VMEM)
    return pl.pallas_call(
        forward_kernel,
        out_shape=(
            jax.ShapeDtypeStruct((rhs, block), jnp.float32),
            jax.ShapeDtypeStruct((targets, rhs // targets, stacked.shape[0]), jnp.float32),
        ),
        in_specs=[pl.BlockSpec(memory_space=pltpu.SMEM)] + [vmem] * (2 + len(pieces)),
        out_specs=(vmem, vmem),
        scratch_shapes=[pltpu.VMEM(side_shape, jnp.float32)],
        compiler_params=pltpu.CompilerParams(vmem_limit_bytes=16 * 1024 * 1024),
        cost_estimate=pl.CostEstimate(
            flops=8 * rhs * block * inverse_blocks.shape[1],
            bytes_accessed=4 * inverse_blocks.size + 16 * pieces[0].size,
            transcendentals=0,
        ),
        name="forward",
    )(x_pos.reshape(1), inverse_blocks, stacked, *pieces)


def spread_kernel(result_ref, forward_ref, stacked_ref, inverse_ref, out_ref, held):
    share = result_ref.shape[1]
    rhs, block = forward_ref.shape
    for piece in range(result_ref.shape[0]):
        held[piece * share : (piece + 1) * share, :] = result_ref[piece, :, : held.shape[1]]
    taken = jnp.dot(
        two_parts(held[...]), two_columns(stacked_ref[...]), preferred_element_type=jnp.float32
    )
    reduced = two_parts(forward_ref[...] - fold(taken, rhs, block))
    group = 2
    for first in range(0, out_ref.shape[0], group):
        weights = two_columns(inverse_ref[:, first * block : (first + group) * block])
        parts = jnp.dot(reduced, weights, preferred_element_type=jnp.float32)
        parts = fold(parts, rhs, group * block)
        for j in range(group):
            out_ref[first + j] = parts[:, j * block : (j + 1) * block]


def run_spread(result, forward, stacked, inverse_blocks):
    rhs, block = forward.shape
    vmem = pl.BlockSpec(memory_space=pltpu.VMEM)
    return pl.pallas_call(
        spread_kernel,
        out_shape=jax.ShapeDtypeStruct((inverse_blocks.shape[1] // block, rhs, block), jnp.float32),
        in_specs=[vmem] * 4,
        out_specs=vmem,
        scratch_shapes=[pltpu.VMEM((rhs, stacked.shape[0]), jnp.float32)],
        compiler_params=pltpu.CompilerParams(vmem_limit_bytes=16 * 1024 * 1024),
        cost_estimate=pl.CostEstimate(
            flops=8 * rhs * block * inverse_blocks.shape[1],
            bytes_accessed=4 * inverse_blocks.size + 4 * rhs * inverse_blocks.shape[1],
            transcendentals=0,
        ),
        name="spread",
    )(result, forward, stacked, inverse_blocks)


def share_kernel(pos_ref, arrived_ref, high_ref, moved_ref, out_ref, held):
    share, width = arrived_ref.shape[1:]
    rows = width // 2
    held[...] = jnp.zeros_like(held)
    held[:share, :] = jnp.sum(arrived_ref[...], axis=0)
    vectors = held[...]
    own_u, own_w = vectors[:, :rows], vectors[:, rows:]
    is_upper = pos_ref[1] == 1
    u_moved = -dot_parts(two_parts(own_u), *split(high_ref[...]), 1)
    turned = two_parts(jnp.where(is_upper, own_w, own_u))
    w_moved = dot_parts(turned, *split(moved_ref[...]), 0)
    kept = jnp.concatenate(
        [
            jnp.where(is_upper, own_u, u_moved),
            jnp.where(is_upper, w_moved, own_w + w_moved),
            vectors,
        ],
        axis=1,
    )[:share]
    for piece in range(out_ref.shape[0]):
        out_ref[piece] = kept


def run_share(position, arrived, c_high, moved, targets):
    share, width = arrived.shape[1:]
    vmem = pl.BlockSpec(memory_space=pltpu.VMEM)
    return pl.pallas_call(
        share_kernel,
        out_shape=jax.ShapeDtypeStruct((targets, share, 2 * width), jnp.float32),
        in_specs=[pl.BlockSpec(memory_space=pltpu.SMEM)] + [vmem] * 3,
        out_specs=vmem,
        scratch_shapes=[pltpu.VMEM((padded, width), jnp.float32)],
        compiler_params=pltpu.CompilerParams(vmem_limit_bytes=16 * 1024 * 1024),
        cost_estimate=pl.CostEstimate(
            flops=128 * width * width, bytes_accessed=8 * width * width, transcendentals=0
        ),
        name="share",
    )(position, arrived, c_high, moved)


def chain_kernel(
    pos_ref, coupling_ref, share_ref, low_ref, high_ref, below_ref, above_ref, out_ref,
    held, own, head, tail, vectors, into, above, sems,
):
    pairs = held.shape[0]
    share, rows = below_ref.shape

    def fetch(y):
        return pltpu.make_async_copy(coupling_ref.at[y], held.at[y], sems.at[y])

    for y in range(pairs):
        fetch(y).start()
    own_low = pltpu.make_async_copy(low_ref, own.at[0], sems.at[pairs])
    own_high = pltpu.make_async_copy(high_ref, own.at[1], sems.at[pairs + 1])
    own_low.start()
    own_high.start()
    vectors[...] = jnp.zeros_like(vectors)
    into[0] = jnp.zeros_like(into[0])
    above[pairs - 1] = jnp.zeros_like(into[0])
    for y in range(pairs):
        both = share_ref[2 * y] + share_ref[2 * y + 1]
        vectors[y, :share, :] = both[:, : 2 * rows]
    chip = pos_ref[0]
    vectors[pairs, :share, :] = share_ref[2 * chip][:, 2 * rows :]
    vectors[pairs + 1, :share, :] = share_ref[2 * chip + 1][:, 2 * rows :]
    into[0, :share, :] = below_ref[...]
    above[pairs - 1, :share, :] = above_ref[...]

    incoming = into[0]
    for y in range(pairs):
        fetch(y).wait()
        block_head, block_tail = split(held[y])
        head[y] = block_head[:rows]
        tail[y] = block_tail[:rows]
        result = vectors[y] - dot_parts(two_parts(incoming), block_head, block_tail, 1)
        incoming = result[:, :rows]
        if y + 1 < pairs:
            into[y + 1] = incoming
        vectors[y] = result
    from_above = above[pairs - 1]
    for y in range(pairs - 1, 0, -1):
        taken = dot_parts(two_parts(from_above), head[y], tail[y], 0)
        from_above = vectors[y, :, rows:] - taken
        above[y - 1] = from_above

    own_low.wait()
    own_high.wait()
    low_head, low_tail = split(own[0, :rows])
    high_head, high_tail = split(own[1])
    incoming = into[chip]
    from_above = above[chip]
    middle = vectors[pairs, :, :rows] - dot_parts(two_parts(incoming), low_head, low_tail, 1)
    upper = vectors[pairs + 1] - dot_parts(two_parts(middle), high_head, high_tail, 1)
    taken = dot_parts(two_parts(from_above), high_head[:rows], high_tail[:rows], 0)
    middle_above = upper[:, rows:] - taken
    is_upper = pos_ref[1] == 1
    kept = jnp.concatenate(
        [
            jnp.where(is_upper, from_above, middle_above),
            jnp.where(is_upper, middle, incoming),
            jnp.where(is_upper, upper[:, :rows], middle),
        ],
        axis=1,
    )[:share]
    for piece in range(out_ref.shape[0]):
        out_ref[piece] = kept


def run_chain(position, coupling_all, shares, low, high, below, above, targets):
    share, rows = below.shape
    pairs = coupling_all.shape[0]
    vmem = pl.BlockSpec(memory_space=pltpu.VMEM)
    hbm = pl.BlockSpec(memory_space=pltpu.HBM)
    return pl.pallas_call(
        chain_kernel,
        out_shape=jax.ShapeDtypeStruct((targets, share, 3 * rows), jnp.float32),
        in_specs=[pl.BlockSpec(memory_space=pltpu.SMEM), hbm, vmem, hbm, hbm, vmem, vmem],
        out_specs=vmem,
        scratch_shapes=[
            pltpu.VMEM((pairs, 2 * rows, rows), jnp.float32),
            pltpu.VMEM((2, 2 * rows, rows), jnp.float32),
            pltpu.VMEM((pairs, rows, rows), jnp.bfloat16),
            pltpu.VMEM((pairs, rows, rows), jnp.bfloat16),
            pltpu.VMEM((pairs + 2, padded, 2 * rows), jnp.float32),
            pltpu.VMEM((pairs, padded, rows), jnp.float32),
            pltpu.VMEM((pairs, padded, rows), jnp.float32),
            pltpu.SemaphoreType.DMA((pairs + 2,)),
        ],
        compiler_params=pltpu.CompilerParams(vmem_limit_bytes=(56 * 1024 + 640) * 1024),
        cost_estimate=pl.CostEstimate(
            flops=12 * pairs * 16 * rows * rows,
            bytes_accessed=8 * pairs * rows * rows,
            transcendentals=0,
        ),
        name="chain",
    )(position, coupling_all, shares, low, high, below, above)


def on_device(right_side, inverse_blocks, panels, receive_rows, below_update, above_solution):
    rhs = right_side.shape[0]
    block = inverse_blocks.shape[0]
    rows = panels.shape[0]
    front_count = lax.axis_size("front")
    front_pos = lax.axis_index("front")
    leaf_pos = lax.axis_index("leaf")
    leaf_count = lax.axis_size("leaf")
    is_upper = leaf_pos % 2 == 1
    share = rhs // front_count
    targets = receive_rows[0]

    chunk = rhs // x_chips
    slice_rows = 2 * rows // front_count
    picked = jnp.take(inverse_blocks, targets, axis=1)
    stacked = jnp.concatenate([panels, picked.T], axis=0)
    own_coupling = product(stacked, picked).reshape(front_count, slice_rows, rows)
    own_chunks = jnp.tile(right_side.reshape(x_chips, chunk, block), (front_count // x_chips, 1, 1))
    arrived = exchange(jnp.concatenate([own_coupling, own_chunks], axis=2))
    coupling = jnp.sum(arrived[:, :, :rows], axis=0)
    side_chunk = arrived[:, :, rows:]
    coupling = gather_front(coupling).reshape(2 * rows, rows)

    swap = [(s, s ^ 1) for s in range(leaf_count)]
    mate = lax.ppermute(coupling, "leaf", swap)
    low = jnp.where(is_upper, mate, coupling)
    high = jnp.where(is_upper, coupling, mate)
    c_low, c_high, g_high = (low[:rows], high[:rows], high[rows:])
    lifted = product(g_high, c_low)
    c_pair = -product(c_high, c_low)
    g_pair = low[rows:] + product(c_low.T, lifted)
    pair_half = jnp.where(is_upper, g_pair, c_pair)
    pair_half, side_chunk = lax.optimization_barrier((pair_half, side_chunk))
    turned = [turn_along_x(side_chunk, steps) for steps in range(1, x_chips)]
    coupling_all = gather_leaf(pair_half).reshape(leaf_count // 2, 2 * rows, rows)

    local_forward, vectors = run_forward(
        front_pos % x_chips, [side_chunk, *turned], inverse_blocks, stacked, front_count
    )
    position = jnp.stack([leaf_pos // 2, leaf_pos % 2])
    moved = jnp.where(is_upper, -c_low, lifted)
    shares = exchange(run_share(position, exchange(vectors), c_high, moved, leaf_count), "leaf")

    below_rows = lax.dynamic_slice_in_dim(below_update, front_pos * share, share, 0)
    above_rows = lax.dynamic_slice_in_dim(above_solution, front_pos * share, share, 0)
    result = exchange(
        run_chain(
            position, coupling_all, shares, low, high,
            below_rows, above_rows, front_count,
        )
    )
    spread = run_spread(result, local_forward, stacked, inverse_blocks)
    solution = jnp.sum(exchange(spread), axis=0)
    update_share = rows // front_count
    updates = result[:, :, 2 * rows :].reshape(rhs, rows)
    sent_updates = lax.dynamic_slice_in_dim(updates, front_pos * update_share, update_share, 1)
    return (solution, sent_updates)


def solution(mesh):
    in_specs = (
        P(None, ("leaf", "front")),
        P(("leaf", "front"), None),
        P("leaf", "front"),
        P("leaf", None),
        P(),
        P(),
    )
    out_specs = (P(None, ("leaf", "front")), P(None, ("leaf", "front")))
    return jax.shard_map(
        on_device, mesh=mesh, in_specs=in_specs, out_specs=out_specs, check_vma=False
    )
```

```python
import jax
import jax.numpy as jnp
from jax import lax
from jax.experimental import pallas as pl
from jax.experimental.pallas import tpu as pltpu
from jax.sharding import PartitionSpec as P

exact = lax.Precision.HIGHEST
x_chips = 4
padded = 8


def product(left, right):
    return jnp.dot(left, right, precision=exact, preferred_element_type=jnp.float32)


def product_nt(left, right):
    return lax.dot_general(
        left, right, (((1,), (1,)), ((), ())), precision=exact, preferred_element_type=jnp.float32
    )


def exchange(blocks, axis="front", groups=None):
    return lax.all_to_all(blocks, axis, 0, 0, tiled=True, axis_index_groups=groups)


def copies(block, count):
    return jnp.broadcast_to(block[None], (count, *block.shape))


def gather_front(block):
    return exchange(copies(block, lax.axis_size("front")))


def gather_leaf(block):
    return lax.all_gather(block, "leaf", axis=0)


def turn_along_x(block, steps):
    count = lax.axis_size("front")
    pairs = [(f, f - f % x_chips + (f + steps) % x_chips) for f in range(count)]
    return lax.ppermute(block, "front", pairs)


def split(value):
    head = value.astype(jnp.bfloat16)
    return head, (value - head.astype(jnp.float32)).astype(jnp.bfloat16)


def two_parts(value):
    head, tail = split(value)
    return jnp.concatenate([head.astype(jnp.float32), tail.astype(jnp.float32)]).astype(
        jnp.bfloat16
    )


def dot_parts(parts, head, tail, contract):
    dims = (((1,), (contract,)), ((), ()))
    both = lax.dot_general(parts, head, dims, preferred_element_type=jnp.float32)
    both += lax.dot_general(parts, tail, dims, preferred_element_type=jnp.float32)
    return both[:padded] + both[padded:]


def fold(parts, rows, columns):
    small = parts[rows:, columns:] + (parts[rows:, :columns] + parts[:rows, columns:])
    return small + parts[:rows, :columns]


def two_columns(value):
    head, tail = split(value)
    return jnp.concatenate([head, tail], axis=1)


def forward_kernel(pos_ref, inverse_ref, stacked_ref, *refs):
    pieces, (forward_ref, vector_ref, side_ref) = refs[:-3], refs[-3:]
    chunks, blocks, chunk, block = side_ref.shape
    for steps, piece in enumerate(pieces):
        side_ref[lax.rem(pos_ref[0] + chunks - steps, chunks)] = piece[...]
    rhs = chunks * chunk
    group = 4
    nt = (((1,), (1,)), ((), ()))
    total = jnp.zeros((2 * rhs, 2 * block), jnp.float32)
    for first in range(0, blocks, group):
        side = jnp.concatenate(
            [
                jnp.concatenate([side_ref[c, first + j] for j in range(group)], axis=1)
                for c in range(chunks)
            ]
        )
        weights = two_parts(inverse_ref[:, first * block : (first + group) * block])
        total += lax.dot_general(
            two_parts(side), weights, nt, preferred_element_type=jnp.float32
        )
    forward = fold(total, rhs, block)
    forward_ref[...] = forward
    vectors = lax.dot_general(
        two_parts(forward), two_parts(stacked_ref[...]), nt, preferred_element_type=jnp.float32
    )
    vectors = fold(vectors, rhs, stacked_ref.shape[0])
    share = vector_ref.shape[1]
    for piece in range(vector_ref.shape[0]):
        vector_ref[piece] = vectors[piece * share : (piece + 1) * share]


def run_forward(x_pos, pieces, inverse_blocks, stacked, targets):
    side_shape = (len(pieces), *pieces[0].shape)
    rhs = side_shape[0] * side_shape[2]
    block = inverse_blocks.shape[0]
    vmem = pl.BlockSpec(memory_space=pltpu.VMEM)
    return pl.pallas_call(
        forward_kernel,
        out_shape=(
            jax.ShapeDtypeStruct((rhs, block), jnp.float32),
            jax.ShapeDtypeStruct((targets, rhs // targets, stacked.shape[0]), jnp.float32),
        ),
        in_specs=[pl.BlockSpec(memory_space=pltpu.SMEM)] + [vmem] * (2 + len(pieces)),
        out_specs=(vmem, vmem),
        scratch_shapes=[pltpu.VMEM(side_shape, jnp.float32)],
        compiler_params=pltpu.CompilerParams(vmem_limit_bytes=16 * 1024 * 1024),
        cost_estimate=pl.CostEstimate(
            flops=8 * rhs * block * inverse_blocks.shape[1],
            bytes_accessed=4 * inverse_blocks.size + 16 * pieces[0].size,
            transcendentals=0,
        ),
        name="forward",
    )(x_pos.reshape(1), inverse_blocks, stacked, *pieces)


def spread_kernel(result_ref, forward_ref, stacked_ref, inverse_ref, out_ref, held):
    share = result_ref.shape[1]
    rhs, block = forward_ref.shape
    for piece in range(result_ref.shape[0]):
        held[piece * share : (piece + 1) * share, :] = result_ref[piece, :, : held.shape[1]]
    taken = jnp.dot(
        two_parts(held[...]), two_columns(stacked_ref[...]), preferred_element_type=jnp.float32
    )
    reduced = two_parts(forward_ref[...] - fold(taken, rhs, block))
    group = 2
    for first in range(0, out_ref.shape[0], group):
        weights = two_columns(inverse_ref[:, first * block : (first + group) * block])
        parts = jnp.dot(reduced, weights, preferred_element_type=jnp.float32)
        parts = fold(parts, rhs, group * block)
        for j in range(group):
            out_ref[first + j] = parts[:, j * block : (j + 1) * block]


def run_spread(result, forward, stacked, inverse_blocks):
    rhs, block = forward.shape
    vmem = pl.BlockSpec(memory_space=pltpu.VMEM)
    return pl.pallas_call(
        spread_kernel,
        out_shape=jax.ShapeDtypeStruct((inverse_blocks.shape[1] // block, rhs, block), jnp.float32),
        in_specs=[vmem] * 4,
        out_specs=vmem,
        scratch_shapes=[pltpu.VMEM((rhs, stacked.shape[0]), jnp.float32)],
        compiler_params=pltpu.CompilerParams(vmem_limit_bytes=16 * 1024 * 1024),
        cost_estimate=pl.CostEstimate(
            flops=8 * rhs * block * inverse_blocks.shape[1],
            bytes_accessed=4 * inverse_blocks.size + 4 * rhs * inverse_blocks.shape[1],
            transcendentals=0,
        ),
        name="spread",
    )(result, forward, stacked, inverse_blocks)


def share_kernel(pos_ref, arrived_ref, high_ref, moved_ref, out_ref, held):
    share, width = arrived_ref.shape[1:]
    rows = width // 2
    held[...] = jnp.zeros_like(held)
    held[:share, :] = jnp.sum(arrived_ref[...], axis=0)
    vectors = held[...]
    own_u, own_w = vectors[:, :rows], vectors[:, rows:]
    is_upper = pos_ref[1] == 1
    u_moved = -dot_parts(two_parts(own_u), *split(high_ref[...]), 1)
    turned = two_parts(jnp.where(is_upper, own_w, own_u))
    w_moved = dot_parts(turned, *split(moved_ref[...]), 0)
    kept = jnp.concatenate(
        [
            jnp.where(is_upper, own_u, u_moved),
            jnp.where(is_upper, w_moved, own_w + w_moved),
            vectors,
        ],
        axis=1,
    )[:share]
    for piece in range(out_ref.shape[0]):
        out_ref[piece] = kept


def run_share(position, arrived, c_high, moved, targets):
    share, width = arrived.shape[1:]
    vmem = pl.BlockSpec(memory_space=pltpu.VMEM)
    return pl.pallas_call(
        share_kernel,
        out_shape=jax.ShapeDtypeStruct((targets, share, 2 * width), jnp.float32),
        in_specs=[pl.BlockSpec(memory_space=pltpu.SMEM)] + [vmem] * 3,
        out_specs=vmem,
        scratch_shapes=[pltpu.VMEM((padded, width), jnp.float32)],
        compiler_params=pltpu.CompilerParams(vmem_limit_bytes=16 * 1024 * 1024),
        cost_estimate=pl.CostEstimate(
            flops=128 * width * width, bytes_accessed=8 * width * width, transcendentals=0
        ),
        name="share",
    )(position, arrived, c_high, moved)


def chain_kernel(
    pos_ref, coupling_ref, share_ref, low_ref, high_ref, below_ref, above_ref, out_ref,
    held, own, head, tail, vectors, into, above, sems,
):
    pairs = held.shape[0]
    share, rows = below_ref.shape

    def fetch(y):
        return pltpu.make_async_copy(coupling_ref.at[y], held.at[y], sems.at[y])

    for y in range(pairs):
        fetch(y).start()
    own_low = pltpu.make_async_copy(low_ref, own.at[0], sems.at[pairs])
    own_high = pltpu.make_async_copy(high_ref, own.at[1], sems.at[pairs + 1])
    own_low.start()
    own_high.start()
    vectors[...] = jnp.zeros_like(vectors)
    into[0] = jnp.zeros_like(into[0])
    above[pairs - 1] = jnp.zeros_like(into[0])
    for y in range(pairs):
        both = share_ref[2 * y] + share_ref[2 * y + 1]
        vectors[y, :share, :] = both[:, : 2 * rows]
    chip = pos_ref[0]
    vectors[pairs, :share, :] = share_ref[2 * chip][:, 2 * rows :]
    vectors[pairs + 1, :share, :] = share_ref[2 * chip + 1][:, 2 * rows :]
    into[0, :share, :] = below_ref[...]
    above[pairs - 1, :share, :] = above_ref[...]

    incoming = into[0]
    for y in range(pairs):
        fetch(y).wait()
        block_head, block_tail = split(held[y])
        head[y] = block_head[:rows]
        tail[y] = block_tail[:rows]
        result = vectors[y] - dot_parts(two_parts(incoming), block_head, block_tail, 1)
        incoming = result[:, :rows]
        if y + 1 < pairs:
            into[y + 1] = incoming
        vectors[y] = result
    from_above = above[pairs - 1]
    for y in range(pairs - 1, 0, -1):
        taken = dot_parts(two_parts(from_above), head[y], tail[y], 0)
        from_above = vectors[y, :, rows:] - taken
        above[y - 1] = from_above

    own_low.wait()
    own_high.wait()
    low_head, low_tail = split(own[0, :rows])
    high_head, high_tail = split(own[1])
    incoming = into[chip]
    from_above = above[chip]
    middle = vectors[pairs, :, :rows] - dot_parts(two_parts(incoming), low_head, low_tail, 1)
    upper = vectors[pairs + 1] - dot_parts(two_parts(middle), high_head, high_tail, 1)
    taken = dot_parts(two_parts(from_above), high_head[:rows], high_tail[:rows], 0)
    middle_above = upper[:, rows:] - taken
    is_upper = pos_ref[1] == 1
    kept = jnp.concatenate(
        [
            jnp.where(is_upper, from_above, middle_above),
            jnp.where(is_upper, middle, incoming),
            jnp.where(is_upper, upper[:, :rows], middle),
        ],
        axis=1,
    )[:share]
    for piece in range(out_ref.shape[0]):
        out_ref[piece] = kept


def run_chain(position, coupling_all, shares, low, high, below, above, targets):
    share, rows = below.shape
    pairs = coupling_all.shape[0]
    vmem = pl.BlockSpec(memory_space=pltpu.VMEM)
    hbm = pl.BlockSpec(memory_space=pltpu.HBM)
    return pl.pallas_call(
        chain_kernel,
        out_shape=jax.ShapeDtypeStruct((targets, share, 3 * rows), jnp.float32),
        in_specs=[pl.BlockSpec(memory_space=pltpu.SMEM), hbm, vmem, hbm, hbm, vmem, vmem],
        out_specs=vmem,
        scratch_shapes=[
            pltpu.VMEM((pairs, 2 * rows, rows), jnp.float32),
            pltpu.VMEM((2, 2 * rows, rows), jnp.float32),
            pltpu.VMEM((pairs, rows, rows), jnp.bfloat16),
            pltpu.VMEM((pairs, rows, rows), jnp.bfloat16),
            pltpu.VMEM((pairs + 2, padded, 2 * rows), jnp.float32),
            pltpu.VMEM((pairs, padded, rows), jnp.float32),
            pltpu.VMEM((pairs, padded, rows), jnp.float32),
            pltpu.SemaphoreType.DMA((pairs + 2,)),
        ],
        compiler_params=pltpu.CompilerParams(vmem_limit_bytes=(56 * 1024 + 640) * 1024),
        cost_estimate=pl.CostEstimate(
            flops=12 * pairs * 16 * rows * rows,
            bytes_accessed=8 * pairs * rows * rows,
            transcendentals=0,
        ),
        name="chain",
    )(position, coupling_all, shares, low, high, below, above)


def on_device(right_side, inverse_blocks, panels, receive_rows, below_update, above_solution):
    rhs = right_side.shape[0]
    block = inverse_blocks.shape[0]
    rows = panels.shape[0]
    front_count = lax.axis_size("front")
    front_pos = lax.axis_index("front")
    leaf_pos = lax.axis_index("leaf")
    leaf_count = lax.axis_size("leaf")
    is_upper = leaf_pos % 2 == 1
    share = rhs // front_count
    targets = receive_rows[0]

    chunk = rhs // x_chips
    slice_rows = 2 * rows // front_count
    picked = jnp.take(inverse_blocks, targets, axis=1)
    stacked = jnp.concatenate([panels, picked.T], axis=0)
    own_coupling = product(stacked, picked).reshape(front_count, slice_rows, rows)
    own_chunks = jnp.tile(right_side.reshape(x_chips, chunk, block), (front_count // x_chips, 1, 1))
    arrived = exchange(jnp.concatenate([own_coupling, own_chunks], axis=2))
    coupling = jnp.sum(arrived[:, :, :rows], axis=0)
    side_chunk = arrived[:, :, rows:]
    coupling = gather_front(coupling).reshape(2 * rows, rows)
    turned = [turn_along_x(side_chunk, steps) for steps in (1, x_chips - 1)]
    coupling, *turned = lax.optimization_barrier((coupling, *turned))

    swap = [(s, s ^ 1) for s in range(leaf_count)]
    mate = lax.ppermute(coupling, "leaf", swap)
    low = jnp.where(is_upper, mate, coupling)
    high = jnp.where(is_upper, coupling, mate)
    c_low, c_high, g_high = (low[:rows], high[:rows], high[rows:])
    lifted = product(g_high, c_low)
    c_pair = -product(c_high, c_low)
    g_pair = low[rows:] + product(c_low.T, lifted)
    pair_half = jnp.where(is_upper, g_pair, c_pair)
    pair_half, side_chunk = lax.optimization_barrier((pair_half, side_chunk))
    turned.insert(1, turn_along_x(side_chunk, 2))
    coupling_all = gather_leaf(pair_half).reshape(leaf_count // 2, 2 * rows, rows)

    local_forward, vectors = run_forward(
        front_pos % x_chips, [side_chunk, *turned], inverse_blocks, stacked, front_count
    )
    position = jnp.stack([leaf_pos // 2, leaf_pos % 2])
    moved = jnp.where(is_upper, -c_low, lifted)
    shares = exchange(run_share(position, exchange(vectors), c_high, moved, leaf_count), "leaf")

    below_rows = lax.dynamic_slice_in_dim(below_update, front_pos * share, share, 0)
    above_rows = lax.dynamic_slice_in_dim(above_solution, front_pos * share, share, 0)
    result = exchange(
        run_chain(
            position, coupling_all, shares, low, high,
            below_rows, above_rows, front_count,
        )
    )
    spread = run_spread(result, local_forward, stacked, inverse_blocks)
    solution = jnp.sum(exchange(spread), axis=0)
    update_share = rows // front_count
    updates = result[:, :, 2 * rows :].reshape(rhs, rows)
    sent_updates = lax.dynamic_slice_in_dim(updates, front_pos * update_share, update_share, 1)
    return (solution, sent_updates)


def solution(mesh):
    in_specs = (
        P(None, ("leaf", "front")),
        P(("leaf", "front"), None),
        P("leaf", "front"),
        P("leaf", None),
        P(),
        P(),
    )
    out_specs = (P(None, ("leaf", "front")), P(None, ("leaf", "front")))
    return jax.shard_map(
        on_device, mesh=mesh, in_specs=in_specs, out_specs=out_specs, check_vma=False
    )
```

```python
import jax
import jax.numpy as jnp
from jax import lax
from jax.experimental import pallas as pl
from jax.experimental.pallas import tpu as pltpu
from jax.sharding import PartitionSpec as P

exact = lax.Precision.HIGHEST
x_chips = 4
padded = 8


def product(left, right):
    return jnp.dot(left, right, precision=exact, preferred_element_type=jnp.float32)


def product_nt(left, right):
    return lax.dot_general(
        left, right, (((1,), (1,)), ((), ())), precision=exact, preferred_element_type=jnp.float32
    )


def exchange(blocks, axis="front", groups=None):
    return lax.all_to_all(blocks, axis, 0, 0, tiled=True, axis_index_groups=groups)


def copies(block, count):
    return jnp.broadcast_to(block[None], (count, *block.shape))


def gather_front(block):
    return exchange(copies(block, lax.axis_size("front")))


def gather_leaf(block):
    return lax.all_gather(block, "leaf", axis=0)


def turn_along_x(block, steps):
    count = lax.axis_size("front")
    pairs = [(f, f - f % x_chips + (f + steps) % x_chips) for f in range(count)]
    return lax.ppermute(block, "front", pairs)


def split(value):
    head = value.astype(jnp.bfloat16)
    return head, (value - head.astype(jnp.float32)).astype(jnp.bfloat16)


def two_parts(value):
    head, tail = split(value)
    return jnp.concatenate([head.astype(jnp.float32), tail.astype(jnp.float32)]).astype(
        jnp.bfloat16
    )


def dot_parts(parts, head, tail, contract):
    dims = (((1,), (contract,)), ((), ()))
    both = lax.dot_general(parts, head, dims, preferred_element_type=jnp.float32)
    both += lax.dot_general(parts, tail, dims, preferred_element_type=jnp.float32)
    return both[:padded] + both[padded:]


def fold(parts, rows, columns):
    small = parts[rows:, columns:] + (parts[rows:, :columns] + parts[:rows, columns:])
    return small + parts[:rows, :columns]


def two_columns(value):
    head, tail = split(value)
    return jnp.concatenate([head, tail], axis=1)


def forward_kernel(pos_ref, inverse_ref, stacked_ref, *refs):
    pieces, (forward_ref, vector_ref, side_ref) = refs[:-3], refs[-3:]
    chunks, blocks, chunk, block = side_ref.shape
    for steps, piece in enumerate(pieces):
        side_ref[lax.rem(pos_ref[0] + chunks - steps, chunks)] = piece[...]
    rhs = chunks * chunk
    group = 4
    nt = (((1,), (1,)), ((), ()))
    total = jnp.zeros((2 * rhs, 2 * block), jnp.float32)
    for first in range(0, blocks, group):
        side = jnp.concatenate(
            [
                jnp.concatenate([side_ref[c, first + j] for j in range(group)], axis=1)
                for c in range(chunks)
            ]
        )
        weights = two_parts(inverse_ref[:, first * block : (first + group) * block])
        total += lax.dot_general(
            two_parts(side), weights, nt, preferred_element_type=jnp.float32
        )
    forward = fold(total, rhs, block)
    forward_ref[...] = forward
    vectors = lax.dot_general(
        two_parts(forward), two_parts(stacked_ref[...]), nt, preferred_element_type=jnp.float32
    )
    vectors = fold(vectors, rhs, stacked_ref.shape[0])
    share = vector_ref.shape[1]
    for piece in range(vector_ref.shape[0]):
        vector_ref[piece] = vectors[piece * share : (piece + 1) * share]


def run_forward(x_pos, pieces, inverse_blocks, stacked, targets):
    side_shape = (len(pieces), *pieces[0].shape)
    rhs = side_shape[0] * side_shape[2]
    block = inverse_blocks.shape[0]
    vmem = pl.BlockSpec(memory_space=pltpu.VMEM)
    return pl.pallas_call(
        forward_kernel,
        out_shape=(
            jax.ShapeDtypeStruct((rhs, block), jnp.float32),
            jax.ShapeDtypeStruct((targets, rhs // targets, stacked.shape[0]), jnp.float32),
        ),
        in_specs=[pl.BlockSpec(memory_space=pltpu.SMEM)] + [vmem] * (2 + len(pieces)),
        out_specs=(vmem, vmem),
        scratch_shapes=[pltpu.VMEM(side_shape, jnp.float32)],
        compiler_params=pltpu.CompilerParams(vmem_limit_bytes=16 * 1024 * 1024),
        cost_estimate=pl.CostEstimate(
            flops=8 * rhs * block * inverse_blocks.shape[1],
            bytes_accessed=4 * inverse_blocks.size + 16 * pieces[0].size,
            transcendentals=0,
        ),
        name="forward",
    )(x_pos.reshape(1), inverse_blocks, stacked, *pieces)


def spread_kernel(result_ref, forward_ref, stacked_ref, inverse_ref, out_ref, held):
    share = result_ref.shape[1]
    rhs, block = forward_ref.shape
    for piece in range(result_ref.shape[0]):
        held[piece * share : (piece + 1) * share, :] = result_ref[piece, :, : held.shape[1]]
    taken = jnp.dot(
        two_parts(held[...]), two_columns(stacked_ref[...]), preferred_element_type=jnp.float32
    )
    reduced = two_parts(forward_ref[...] - fold(taken, rhs, block))
    group = 2
    for first in range(0, out_ref.shape[0], group):
        weights = two_columns(inverse_ref[:, first * block : (first + group) * block])
        parts = jnp.dot(reduced, weights, preferred_element_type=jnp.float32)
        parts = fold(parts, rhs, group * block)
        for j in range(group):
            out_ref[first + j] = parts[:, j * block : (j + 1) * block]


def run_spread(result, forward, stacked, inverse_blocks):
    rhs, block = forward.shape
    vmem = pl.BlockSpec(memory_space=pltpu.VMEM)
    return pl.pallas_call(
        spread_kernel,
        out_shape=jax.ShapeDtypeStruct((inverse_blocks.shape[1] // block, rhs, block), jnp.float32),
        in_specs=[vmem] * 4,
        out_specs=vmem,
        scratch_shapes=[pltpu.VMEM((rhs, stacked.shape[0]), jnp.float32)],
        compiler_params=pltpu.CompilerParams(vmem_limit_bytes=16 * 1024 * 1024),
        cost_estimate=pl.CostEstimate(
            flops=8 * rhs * block * inverse_blocks.shape[1],
            bytes_accessed=4 * inverse_blocks.size + 4 * rhs * inverse_blocks.shape[1],
            transcendentals=0,
        ),
        name="spread",
    )(result, forward, stacked, inverse_blocks)


def share_kernel(pos_ref, arrived_ref, high_ref, moved_ref, out_ref, held):
    share, width = arrived_ref.shape[1:]
    rows = width // 2
    held[...] = jnp.zeros_like(held)
    held[:share, :] = jnp.sum(arrived_ref[...], axis=0)
    vectors = held[...]
    own_u, own_w = vectors[:, :rows], vectors[:, rows:]
    is_upper = pos_ref[1] == 1
    u_moved = -dot_parts(two_parts(own_u), *split(high_ref[...]), 1)
    turned = two_parts(jnp.where(is_upper, own_w, own_u))
    w_moved = dot_parts(turned, *split(moved_ref[...]), 0)
    kept = jnp.concatenate(
        [
            jnp.where(is_upper, own_u, u_moved),
            jnp.where(is_upper, w_moved, own_w + w_moved),
            vectors,
        ],
        axis=1,
    )[:share]
    for piece in range(out_ref.shape[0]):
        out_ref[piece] = kept


def run_share(position, arrived, c_high, moved, targets):
    share, width = arrived.shape[1:]
    vmem = pl.BlockSpec(memory_space=pltpu.VMEM)
    return pl.pallas_call(
        share_kernel,
        out_shape=jax.ShapeDtypeStruct((targets, share, 2 * width), jnp.float32),
        in_specs=[pl.BlockSpec(memory_space=pltpu.SMEM)] + [vmem] * 3,
        out_specs=vmem,
        scratch_shapes=[pltpu.VMEM((padded, width), jnp.float32)],
        compiler_params=pltpu.CompilerParams(vmem_limit_bytes=16 * 1024 * 1024),
        cost_estimate=pl.CostEstimate(
            flops=128 * width * width, bytes_accessed=8 * width * width, transcendentals=0
        ),
        name="share",
    )(position, arrived, c_high, moved)


def chain_kernel(
    pos_ref, coupling_ref, share_ref, low_ref, high_ref, below_ref, above_ref, out_ref,
    held, own, head, tail, vectors, into, above, sems,
):
    pairs = held.shape[0]
    share, rows = below_ref.shape

    def fetch(y, half):
        part = pl.ds(half * rows, rows)
        return pltpu.make_async_copy(
            coupling_ref.at[y, part], held.at[y, part], sems.at[half * pairs + y]
        )

    for half in range(2):
        for y in range(pairs):
            fetch(y, half).start()
    own_low = pltpu.make_async_copy(low_ref, own.at[0], sems.at[2 * pairs])
    own_high = pltpu.make_async_copy(high_ref, own.at[1], sems.at[2 * pairs + 1])
    own_low.start()
    own_high.start()
    vectors[...] = jnp.zeros_like(vectors)
    into[0] = jnp.zeros_like(into[0])
    above[pairs - 1] = jnp.zeros_like(into[0])
    for y in range(pairs):
        both = share_ref[2 * y] + share_ref[2 * y + 1]
        vectors[y, :share, :] = both[:, : 2 * rows]
    chip = pos_ref[0]
    vectors[pairs, :share, :] = share_ref[2 * chip][:, 2 * rows :]
    vectors[pairs + 1, :share, :] = share_ref[2 * chip + 1][:, 2 * rows :]
    into[0, :share, :] = below_ref[...]
    above[pairs - 1, :share, :] = above_ref[...]

    incoming = into[0]
    for y in range(pairs - 1):
        fetch(y, 0).wait()
        head[y], tail[y] = split(held[y, :rows])
        taken = dot_parts(two_parts(incoming), head[y], tail[y], 1)
        incoming = vectors[y, :, :rows] - taken
        into[y + 1] = incoming
    fetch(pairs - 1, 0).wait()
    head[pairs - 1], tail[pairs - 1] = split(held[pairs - 1, :rows])
    for y in range(pairs):
        fetch(y, 1).wait()
        taken = dot_parts(two_parts(into[y]), *split(held[y, rows:]), 0)
        vectors[y, :, rows:] = vectors[y, :, rows:] - taken
    from_above = above[pairs - 1]
    for y in range(pairs - 1, 0, -1):
        taken = dot_parts(two_parts(from_above), head[y], tail[y], 0)
        from_above = vectors[y, :, rows:] - taken
        above[y - 1] = from_above

    own_low.wait()
    own_high.wait()
    low_head, low_tail = split(own[0, :rows])
    high_head, high_tail = split(own[1])
    incoming = into[chip]
    from_above = above[chip]
    middle = vectors[pairs, :, :rows] - dot_parts(two_parts(incoming), low_head, low_tail, 1)
    upper = vectors[pairs + 1] - dot_parts(two_parts(middle), high_head, high_tail, 1)
    taken = dot_parts(two_parts(from_above), high_head[:rows], high_tail[:rows], 0)
    middle_above = upper[:, rows:] - taken
    is_upper = pos_ref[1] == 1
    kept = jnp.concatenate(
        [
            jnp.where(is_upper, from_above, middle_above),
            jnp.where(is_upper, middle, incoming),
            jnp.where(is_upper, upper[:, :rows], middle),
        ],
        axis=1,
    )[:share]
    for piece in range(out_ref.shape[0]):
        out_ref[piece] = kept


def run_chain(position, coupling_all, shares, low, high, below, above, targets):
    share, rows = below.shape
    pairs = coupling_all.shape[0]
    vmem = pl.BlockSpec(memory_space=pltpu.VMEM)
    hbm = pl.BlockSpec(memory_space=pltpu.HBM)
    return pl.pallas_call(
        chain_kernel,
        out_shape=jax.ShapeDtypeStruct((targets, share, 3 * rows), jnp.float32),
        in_specs=[pl.BlockSpec(memory_space=pltpu.SMEM), hbm, vmem, hbm, hbm, vmem, vmem],
        out_specs=vmem,
        scratch_shapes=[
            pltpu.VMEM((pairs, 2 * rows, rows), jnp.float32),
            pltpu.VMEM((2, 2 * rows, rows), jnp.float32),
            pltpu.VMEM((pairs, rows, rows), jnp.bfloat16),
            pltpu.VMEM((pairs, rows, rows), jnp.bfloat16),
            pltpu.VMEM((pairs + 2, padded, 2 * rows), jnp.float32),
            pltpu.VMEM((pairs, padded, rows), jnp.float32),
            pltpu.VMEM((pairs, padded, rows), jnp.float32),
            pltpu.SemaphoreType.DMA((2 * pairs + 2,)),
        ],
        compiler_params=pltpu.CompilerParams(vmem_limit_bytes=(56 * 1024 + 640) * 1024),
        cost_estimate=pl.CostEstimate(
            flops=12 * pairs * 16 * rows * rows,
            bytes_accessed=8 * pairs * rows * rows,
            transcendentals=0,
        ),
        name="chain",
    )(position, coupling_all, shares, low, high, below, above)


def on_device(right_side, inverse_blocks, panels, receive_rows, below_update, above_solution):
    rhs = right_side.shape[0]
    block = inverse_blocks.shape[0]
    rows = panels.shape[0]
    front_count = lax.axis_size("front")
    front_pos = lax.axis_index("front")
    leaf_pos = lax.axis_index("leaf")
    leaf_count = lax.axis_size("leaf")
    is_upper = leaf_pos % 2 == 1
    share = rhs // front_count
    targets = receive_rows[0]

    chunk = rhs // x_chips
    slice_rows = 2 * rows // front_count
    picked = jnp.take(inverse_blocks, targets, axis=1)
    stacked = jnp.concatenate([panels, picked.T], axis=0)
    own_coupling = product(stacked, picked).reshape(front_count, slice_rows, rows)
    own_chunks = jnp.tile(right_side.reshape(x_chips, chunk, block), (front_count // x_chips, 1, 1))
    arrived = exchange(jnp.concatenate([own_coupling, own_chunks], axis=2))
    coupling = jnp.sum(arrived[:, :, :rows], axis=0)
    side_chunk = arrived[:, :, rows:]
    coupling = gather_front(coupling).reshape(2 * rows, rows)
    turned = [turn_along_x(side_chunk, steps) for steps in (1, x_chips - 1)]
    coupling, *turned = lax.optimization_barrier((coupling, *turned))

    swap = [(s, s ^ 1) for s in range(leaf_count)]
    mate = lax.ppermute(coupling, "leaf", swap)
    low = jnp.where(is_upper, mate, coupling)
    high = jnp.where(is_upper, coupling, mate)
    c_low, c_high, g_high = (low[:rows], high[:rows], high[rows:])
    lifted = product(g_high, c_low)
    c_pair = -product(c_high, c_low)
    g_pair = low[rows:] + product(c_low.T, lifted)
    pair_half = jnp.where(is_upper, g_pair, c_pair)
    pair_half, side_chunk = lax.optimization_barrier((pair_half, side_chunk))
    turned.insert(1, turn_along_x(side_chunk, 2))
    coupling_all = gather_leaf(pair_half).reshape(leaf_count // 2, 2 * rows, rows)

    local_forward, vectors = run_forward(
        front_pos % x_chips, [side_chunk, *turned], inverse_blocks, stacked, front_count
    )
    position = jnp.stack([leaf_pos // 2, leaf_pos % 2])
    moved = jnp.where(is_upper, -c_low, lifted)
    shares = exchange(run_share(position, exchange(vectors), c_high, moved, leaf_count), "leaf")

    below_rows = lax.dynamic_slice_in_dim(below_update, front_pos * share, share, 0)
    above_rows = lax.dynamic_slice_in_dim(above_solution, front_pos * share, share, 0)
    result = exchange(
        run_chain(
            position, coupling_all, shares, low, high,
            below_rows, above_rows, front_count,
        )
    )
    spread = run_spread(result, local_forward, stacked, inverse_blocks)
    solution = jnp.sum(exchange(spread), axis=0)
    update_share = rows // front_count
    updates = result[:, :, 2 * rows :].reshape(rhs, rows)
    sent_updates = lax.dynamic_slice_in_dim(updates, front_pos * update_share, update_share, 1)
    return (solution, sent_updates)


def solution(mesh):
    in_specs = (
        P(None, ("leaf", "front")),
        P(("leaf", "front"), None),
        P("leaf", "front"),
        P("leaf", None),
        P(),
        P(),
    )
    out_specs = (P(None, ("leaf", "front")), P(None, ("leaf", "front")))
    return jax.shard_map(
        on_device, mesh=mesh, in_specs=in_specs, out_specs=out_specs, check_vma=False
    )
```

```python
import jax
import jax.numpy as jnp
from jax import lax
from jax.experimental import pallas as pl
from jax.experimental.pallas import tpu as pltpu
from jax.sharding import PartitionSpec as P

exact = lax.Precision.HIGHEST
x_chips = 4
padded = 8
forward_weight = 1000


def product(left, right):
    return jnp.dot(left, right, precision=exact, preferred_element_type=jnp.float32)


def product_nt(left, right):
    return lax.dot_general(
        left, right, (((1,), (1,)), ((), ())), precision=exact, preferred_element_type=jnp.float32
    )


def exchange(blocks, axis="front", groups=None):
    return lax.all_to_all(blocks, axis, 0, 0, tiled=True, axis_index_groups=groups)


def copies(block, count):
    return jnp.broadcast_to(block[None], (count, *block.shape))


def gather_front(block):
    return exchange(copies(block, lax.axis_size("front")))


def gather_leaf(block):
    return lax.all_gather(block, "leaf", axis=0)


def turn_along_x(block, steps):
    count = lax.axis_size("front")
    pairs = [(f, f - f % x_chips + (f + steps) % x_chips) for f in range(count)]
    return lax.ppermute(block, "front", pairs)


def split(value):
    head = value.astype(jnp.bfloat16)
    return head, (value - head.astype(jnp.float32)).astype(jnp.bfloat16)


def two_parts(value):
    head, tail = split(value)
    return jnp.concatenate([head.astype(jnp.float32), tail.astype(jnp.float32)]).astype(
        jnp.bfloat16
    )


def dot_parts(parts, head, tail, contract):
    dims = (((1,), (contract,)), ((), ()))
    both = lax.dot_general(parts, head, dims, preferred_element_type=jnp.float32)
    both += lax.dot_general(parts, tail, dims, preferred_element_type=jnp.float32)
    return both[:padded] + both[padded:]


def fold(parts, rows, columns):
    small = parts[rows:, columns:] + (parts[rows:, :columns] + parts[:rows, columns:])
    return small + parts[:rows, :columns]


def two_columns(value):
    head, tail = split(value)
    return jnp.concatenate([head, tail], axis=1)


def forward_kernel(pos_ref, inverse_ref, stacked_ref, *refs):
    pieces, (forward_ref, vector_ref, side_ref) = refs[:-3], refs[-3:]
    chunks, blocks, chunk, block = side_ref.shape
    for steps, piece in enumerate(pieces):
        side_ref[lax.rem(pos_ref[0] + chunks - steps, chunks)] = piece[...]
    rhs = chunks * chunk
    group = 4
    nt = (((1,), (1,)), ((), ()))
    total = jnp.zeros((2 * rhs, 2 * block), jnp.float32)
    for first in range(0, blocks, group):
        side = jnp.concatenate(
            [
                jnp.concatenate([side_ref[c, first + j] for j in range(group)], axis=1)
                for c in range(chunks)
            ]
        )
        weights = two_parts(inverse_ref[:, first * block : (first + group) * block])
        total += lax.dot_general(
            two_parts(side), weights, nt, preferred_element_type=jnp.float32
        )
    forward = fold(total, rhs, block)
    forward_ref[...] = forward
    vectors = lax.dot_general(
        two_parts(forward), two_parts(stacked_ref[...]), nt, preferred_element_type=jnp.float32
    )
    vectors = fold(vectors, rhs, stacked_ref.shape[0])
    share = vector_ref.shape[1]
    for piece in range(vector_ref.shape[0]):
        vector_ref[piece] = vectors[piece * share : (piece + 1) * share]


def run_forward(x_pos, pieces, inverse_blocks, stacked, targets):
    side_shape = (len(pieces), *pieces[0].shape)
    rhs = side_shape[0] * side_shape[2]
    block = inverse_blocks.shape[0]
    vmem = pl.BlockSpec(memory_space=pltpu.VMEM)
    return pl.pallas_call(
        forward_kernel,
        out_shape=(
            jax.ShapeDtypeStruct((rhs, block), jnp.float32),
            jax.ShapeDtypeStruct((targets, rhs // targets, stacked.shape[0]), jnp.float32),
        ),
        in_specs=[pl.BlockSpec(memory_space=pltpu.SMEM)] + [vmem] * (2 + len(pieces)),
        out_specs=(vmem, vmem),
        scratch_shapes=[pltpu.VMEM(side_shape, jnp.float32)],
        compiler_params=pltpu.CompilerParams(vmem_limit_bytes=16 * 1024 * 1024),
        cost_estimate=pl.CostEstimate(
            flops=8 * rhs * block * inverse_blocks.shape[1] * forward_weight,
            bytes_accessed=4 * inverse_blocks.size + 16 * pieces[0].size,
            transcendentals=0,
        ),
        name="forward",
    )(x_pos.reshape(1), inverse_blocks, stacked, *pieces)


def spread_kernel(result_ref, forward_ref, stacked_ref, inverse_ref, out_ref, held):
    share = result_ref.shape[1]
    rhs, block = forward_ref.shape
    for piece in range(result_ref.shape[0]):
        held[piece * share : (piece + 1) * share, :] = result_ref[piece, :, : held.shape[1]]
    taken = jnp.dot(
        two_parts(held[...]), two_columns(stacked_ref[...]), preferred_element_type=jnp.float32
    )
    reduced = two_parts(forward_ref[...] - fold(taken, rhs, block))
    group = 2
    for first in range(0, out_ref.shape[0], group):
        weights = two_columns(inverse_ref[:, first * block : (first + group) * block])
        parts = jnp.dot(reduced, weights, preferred_element_type=jnp.float32)
        parts = fold(parts, rhs, group * block)
        for j in range(group):
            out_ref[first + j] = parts[:, j * block : (j + 1) * block]


def run_spread(result, forward, stacked, inverse_blocks):
    rhs, block = forward.shape
    vmem = pl.BlockSpec(memory_space=pltpu.VMEM)
    return pl.pallas_call(
        spread_kernel,
        out_shape=jax.ShapeDtypeStruct((inverse_blocks.shape[1] // block, rhs, block), jnp.float32),
        in_specs=[vmem] * 4,
        out_specs=vmem,
        scratch_shapes=[pltpu.VMEM((rhs, stacked.shape[0]), jnp.float32)],
        compiler_params=pltpu.CompilerParams(vmem_limit_bytes=16 * 1024 * 1024),
        cost_estimate=pl.CostEstimate(
            flops=8 * rhs * block * inverse_blocks.shape[1],
            bytes_accessed=4 * inverse_blocks.size + 4 * rhs * inverse_blocks.shape[1],
            transcendentals=0,
        ),
        name="spread",
    )(result, forward, stacked, inverse_blocks)


def share_kernel(pos_ref, arrived_ref, high_ref, moved_ref, out_ref, held):
    share, width = arrived_ref.shape[1:]
    rows = width // 2
    held[...] = jnp.zeros_like(held)
    held[:share, :] = jnp.sum(arrived_ref[...], axis=0)
    vectors = held[...]
    own_u, own_w = vectors[:, :rows], vectors[:, rows:]
    is_upper = pos_ref[1] == 1
    u_moved = -dot_parts(two_parts(own_u), *split(high_ref[...]), 1)
    turned = two_parts(jnp.where(is_upper, own_w, own_u))
    w_moved = dot_parts(turned, *split(moved_ref[...]), 0)
    kept = jnp.concatenate(
        [
            jnp.where(is_upper, own_u, u_moved),
            jnp.where(is_upper, w_moved, own_w + w_moved),
            vectors,
        ],
        axis=1,
    )[:share]
    for piece in range(out_ref.shape[0]):
        out_ref[piece] = kept


def run_share(position, arrived, c_high, moved, targets):
    share, width = arrived.shape[1:]
    vmem = pl.BlockSpec(memory_space=pltpu.VMEM)
    return pl.pallas_call(
        share_kernel,
        out_shape=jax.ShapeDtypeStruct((targets, share, 2 * width), jnp.float32),
        in_specs=[pl.BlockSpec(memory_space=pltpu.SMEM)] + [vmem] * 3,
        out_specs=vmem,
        scratch_shapes=[pltpu.VMEM((padded, width), jnp.float32)],
        compiler_params=pltpu.CompilerParams(vmem_limit_bytes=16 * 1024 * 1024),
        cost_estimate=pl.CostEstimate(
            flops=128 * width * width, bytes_accessed=8 * width * width, transcendentals=0
        ),
        name="share",
    )(position, arrived, c_high, moved)


def chain_kernel(
    pos_ref, coupling_ref, share_ref, low_ref, high_ref, below_ref, above_ref, out_ref,
    held, own, head, tail, vectors, into, above, sems,
):
    pairs = held.shape[0]
    share, rows = below_ref.shape

    def fetch(y):
        return pltpu.make_async_copy(coupling_ref.at[y], held.at[y], sems.at[y])

    for y in range(pairs):
        fetch(y).start()
    own_low = pltpu.make_async_copy(low_ref, own.at[0], sems.at[pairs])
    own_high = pltpu.make_async_copy(high_ref, own.at[1], sems.at[pairs + 1])
    own_low.start()
    own_high.start()
    vectors[...] = jnp.zeros_like(vectors)
    into[0] = jnp.zeros_like(into[0])
    above[pairs - 1] = jnp.zeros_like(into[0])
    for y in range(pairs):
        both = share_ref[2 * y] + share_ref[2 * y + 1]
        vectors[y, :share, :] = both[:, : 2 * rows]
    chip = pos_ref[0]
    vectors[pairs, :share, :] = share_ref[2 * chip][:, 2 * rows :]
    vectors[pairs + 1, :share, :] = share_ref[2 * chip + 1][:, 2 * rows :]
    into[0, :share, :] = below_ref[...]
    above[pairs - 1, :share, :] = above_ref[...]

    incoming = into[0]
    for y in range(pairs):
        fetch(y).wait()
        block_head, block_tail = split(held[y])
        head[y] = block_head[:rows]
        tail[y] = block_tail[:rows]
        result = vectors[y] - dot_parts(two_parts(incoming), block_head, block_tail, 1)
        incoming = result[:, :rows]
        if y + 1 < pairs:
            into[y + 1] = incoming
        vectors[y] = result
    from_above = above[pairs - 1]
    for y in range(pairs - 1, 0, -1):
        taken = dot_parts(two_parts(from_above), head[y], tail[y], 0)
        from_above = vectors[y, :, rows:] - taken
        above[y - 1] = from_above

    own_low.wait()
    own_high.wait()
    low_head, low_tail = split(own[0, :rows])
    high_head, high_tail = split(own[1])
    incoming = into[chip]
    from_above = above[chip]
    middle = vectors[pairs, :, :rows] - dot_parts(two_parts(incoming), low_head, low_tail, 1)
    upper = vectors[pairs + 1] - dot_parts(two_parts(middle), high_head, high_tail, 1)
    taken = dot_parts(two_parts(from_above), high_head[:rows], high_tail[:rows], 0)
    middle_above = upper[:, rows:] - taken
    is_upper = pos_ref[1] == 1
    kept = jnp.concatenate(
        [
            jnp.where(is_upper, from_above, middle_above),
            jnp.where(is_upper, middle, incoming),
            jnp.where(is_upper, upper[:, :rows], middle),
        ],
        axis=1,
    )[:share]
    for piece in range(out_ref.shape[0]):
        out_ref[piece] = kept


def run_chain(position, coupling_all, shares, low, high, below, above, targets):
    share, rows = below.shape
    pairs = coupling_all.shape[0]
    vmem = pl.BlockSpec(memory_space=pltpu.VMEM)
    hbm = pl.BlockSpec(memory_space=pltpu.HBM)
    return pl.pallas_call(
        chain_kernel,
        out_shape=jax.ShapeDtypeStruct((targets, share, 3 * rows), jnp.float32),
        in_specs=[pl.BlockSpec(memory_space=pltpu.SMEM), hbm, vmem, hbm, hbm, vmem, vmem],
        out_specs=vmem,
        scratch_shapes=[
            pltpu.VMEM((pairs, 2 * rows, rows), jnp.float32),
            pltpu.VMEM((2, 2 * rows, rows), jnp.float32),
            pltpu.VMEM((pairs, rows, rows), jnp.bfloat16),
            pltpu.VMEM((pairs, rows, rows), jnp.bfloat16),
            pltpu.VMEM((pairs + 2, padded, 2 * rows), jnp.float32),
            pltpu.VMEM((pairs, padded, rows), jnp.float32),
            pltpu.VMEM((pairs, padded, rows), jnp.float32),
            pltpu.SemaphoreType.DMA((pairs + 2,)),
        ],
        compiler_params=pltpu.CompilerParams(vmem_limit_bytes=(56 * 1024 + 640) * 1024),
        cost_estimate=pl.CostEstimate(
            flops=12 * pairs * 16 * rows * rows,
            bytes_accessed=8 * pairs * rows * rows,
            transcendentals=0,
        ),
        name="chain",
    )(position, coupling_all, shares, low, high, below, above)


def on_device(right_side, inverse_blocks, panels, receive_rows, below_update, above_solution):
    rhs = right_side.shape[0]
    block = inverse_blocks.shape[0]
    rows = panels.shape[0]
    front_count = lax.axis_size("front")
    front_pos = lax.axis_index("front")
    leaf_pos = lax.axis_index("leaf")
    leaf_count = lax.axis_size("leaf")
    is_upper = leaf_pos % 2 == 1
    share = rhs // front_count
    targets = receive_rows[0]

    chunk = rhs // x_chips
    slice_rows = 2 * rows // front_count
    picked = jnp.take(inverse_blocks, targets, axis=1)
    stacked = jnp.concatenate([panels, picked.T], axis=0)
    own_coupling = product(stacked, picked).reshape(front_count, slice_rows, rows)
    own_chunks = jnp.tile(right_side.reshape(x_chips, chunk, block), (front_count // x_chips, 1, 1))
    arrived = exchange(jnp.concatenate([own_coupling, own_chunks], axis=2))
    coupling = jnp.sum(arrived[:, :, :rows], axis=0)
    side_chunk = arrived[:, :, rows:]
    coupling = gather_front(coupling).reshape(2 * rows, rows)
    turned = [turn_along_x(side_chunk, steps) for steps in (1, x_chips - 1)]
    coupling, side_chunk, *turned = lax.optimization_barrier((coupling, side_chunk, *turned))
    far = turn_along_x(side_chunk, 2)

    swap = [(s, s ^ 1) for s in range(leaf_count)]
    mate = lax.ppermute(coupling, "leaf", swap)
    low = jnp.where(is_upper, mate, coupling)
    high = jnp.where(is_upper, coupling, mate)
    c_low, c_high, g_high = (low[:rows], high[:rows], high[rows:])
    lifted = product(g_high, c_low)
    c_pair = -product(c_high, c_low)
    g_pair = low[rows:] + product(c_low.T, lifted)
    pair_half = jnp.where(is_upper, g_pair, c_pair)
    turned.insert(1, far)
    coupling_all = gather_leaf(pair_half).reshape(leaf_count // 2, 2 * rows, rows)

    local_forward, vectors = run_forward(
        front_pos % x_chips, [side_chunk, *turned], inverse_blocks, stacked, front_count
    )
    position = jnp.stack([leaf_pos // 2, leaf_pos % 2])
    moved = jnp.where(is_upper, -c_low, lifted)
    shares = exchange(run_share(position, exchange(vectors), c_high, moved, leaf_count), "leaf")

    below_rows = lax.dynamic_slice_in_dim(below_update, front_pos * share, share, 0)
    above_rows = lax.dynamic_slice_in_dim(above_solution, front_pos * share, share, 0)
    result = exchange(
        run_chain(
            position, coupling_all, shares, low, high,
            below_rows, above_rows, front_count,
        )
    )
    spread = run_spread(result, local_forward, stacked, inverse_blocks)
    solution = jnp.sum(exchange(spread), axis=0)
    update_share = rows // front_count
    updates = result[:, :, 2 * rows :].reshape(rhs, rows)
    sent_updates = lax.dynamic_slice_in_dim(updates, front_pos * update_share, update_share, 1)
    return (solution, sent_updates)


def solution(mesh):
    in_specs = (
        P(None, ("leaf", "front")),
        P(("leaf", "front"), None),
        P("leaf", "front"),
        P("leaf", None),
        P(),
        P(),
    )
    out_specs = (P(None, ("leaf", "front")), P(None, ("leaf", "front")))
    return jax.shard_map(
        on_device, mesh=mesh, in_specs=in_specs, out_specs=out_specs, check_vma=False
    )
```
